32 devices in a mesh: seq: 4 (over y, x), expert: 8 (over z, core).
Axes of the slice: x: 2, y: 2, z: 4, core: 2. Of those that a mesh axis runs over, the one named last changes fastest.
Arguments:
- tokens: bfloat16 [512, 4096], P('seq'), may hold values from -8 to 8
- norm_gain: float32 [4096], replicated, may hold values from 0.25 to 1.75
- in_weight: bfloat16 [4096, 2, 8192], P('seq', None, 'expert'), may hold values from -0.09375 to 0.09375
- conv_weight: float32 [4, 8192], P(None, 'expert'), may hold values from -0.5 to 0.5
- conv_bias: float32 [8192], P('expert'), may hold values from -0.5 to 0.5
- proj_weight: bfloat16 [8192, 288], P('expert'), may hold values from -0.0625 to 0.0625
- step_weight: bfloat16 [256, 8192], P(None, 'expert'), may hold values from -1 to 1
- step_bias: float32 [8192], P('expert'), may hold values from -5 to -1
- decay_log: float32 [8192, 16], P('expert'), may hold values from -6 to 2.7
- skip_gain: float32 [8192], P('expert'), may hold values from 0.5 to 1.5
- out_weight: bfloat16 [8192, 4096], P('expert', 'seq'), may hold values from -0.0625 to 0.0625
- moe_gain: float32 [4096], replicated, may hold values from 0.25 to 1.75
- router_weight: bfloat16 [4096, 8], replicated, may hold values from -0.09375 to 0.09375
- routes: int32 [512, 2], P(('seq', 'expert')), may hold values from 0 to 7, all different within a row; in each aligned block of 16 rows (0 to 15, 16 to 31, ...) at most 6 rows name the same one
- gate_weight: bfloat16 [8, 4096, 7168], P('expert', None, 'seq'), may hold values from -0.09375 to 0.09375
- up_weight: bfloat16 [8, 4096, 7168], P('expert', None, 'seq'), may hold values from -0.09375 to 0.09375
- down_weight: bfloat16 [8, 7168, 4096], P('expert', 'seq'), may hold values from -0.0625 to 0.0625
Outputs:
- mixed: bfloat16 [512, 4096], P(('seq', 'expert'))
The draws below stay inside these ranges and needn't reach their ends.
Inputs may be any that keep to these rules, and one draw needn't show every extreme that they name: `routes`: each row names two different experts; within each aligned block of 16 rows no expert is named by more than 6 rows, and that number is reached in some blocks.
All inputs are finite; a program needn't handle non-finite values.
Results may differ from the reference program's by a relative error of at most 0.013.
Values may be sent and summed in bfloat16 or wider, within the bound.
No kernel may reach another device: no remote copies, remote signals or barrier semaphores. Data moves between devices by JAX's collectives and lax.ppermute only.
A program may use at most 128 MiB of HBM per device.

```python
import math
import jax
import jax.numpy as jnp
import numpy as np
from jax import lax

D = 4096
DI = 8192
STATE = 16
RANK = 256
CONV = 4
FF = 7168
TOK_SEQ = 128
TOKENS = 512
EXPERTS = 8
BLOCK = 16
MOST = 6
N_SEQ = 4


def draw_tokens(key, part):
    noise_key, shard_key = jax.random.split(jax.random.fold_in(key, 17))
    noise = jax.random.normal(noise_key, (TOKENS, D), jnp.float32)
    lift = 1.5
    shard_rows = jax.random.normal(shard_key, (TOKENS // TOK_SEQ, D), jnp.float32)
    common = jnp.repeat(shard_rows, TOK_SEQ, axis=0)
    return jnp.clip(noise + lift * common, -8.0, 8.0).astype(jnp.bfloat16)


def block_scale(stream_key, dims, shards, least, top_value):
    def one(dim, parts):
        heights = jax.random.uniform(jax.random.fold_in(jax.random.fold_in(stream_key, 6), dim), (parts,), jnp.float32, least / len(shards), top_value / len(shards))
        return jnp.repeat(jnp.exp(heights), dims[dim] // parts).reshape((-1,) + (1,) * (len(dims) - dim - 1))

    factor_of = one(*shards[0])
    for cut in shards[1:]:
        factor_of = factor_of * one(*cut)
    return factor_of


def shared_out(own_key, own, number, rows, count, top, limit, slope):
    order = jax.random.permutation(own_key, count)
    heavy_load, usual = load_shares(count, rows * top, limit, slope, True), load_shares(count, rows * top, limit, slope, False)
    places = jnp.arange(count)

    def named(tallies, rotation):
        used = int((tallies > 0).sum())
        fixed = max(1, used // 4)
        moved = fixed + (places - fixed + rotation * (used - fixed)) % max(1, count - fixed)
        return jnp.zeros((count,), jnp.int32).at[order[jnp.where(places < fixed, places, moved)]].set(jnp.asarray(tallies, jnp.int32))

    tallies = jnp.where(number % 4 == 0, named(heavy_load, number // 4), named(usual, number - number // 4 - 1))
    mixed = jax.random.permutation(jax.random.fold_in(own, 3), count)
    source_of, sink = mixed[0:count // 2 * 2:2], mixed[1:count // 2 * 2:2]
    room = jnp.minimum(tallies[source_of] - 1, limit - tallies[sink]) // 2
    room = jnp.where((source_of == order[0]) | (sink == order[0]) | (tallies[sink] == 0), 0, jnp.maximum(room, 0))
    moved = jax.random.randint(jax.random.fold_in(own, 4), (count // 2,), 0, 1 << 20) % (room + 1)
    tallies = tallies.at[source_of].add(-moved).at[sink].add(moved)
    members = jnp.searchsorted(jnp.cumsum(tallies), jnp.arange(rows * top), side="right").astype(jnp.int32)
    listing = members.reshape(top, rows).T
    listing = listing[jax.random.permutation(jax.random.fold_in(own, 1), rows)]
    rotation = jax.random.randint(jax.random.fold_in(own, 2), (rows, 1), 0, top)
    return jnp.take_along_axis(listing, (jnp.arange(top)[None, :] + rotation) % top, axis=1)


def load_shares(count, total, most, slope, full):
    loads = [(1 << 20) // math.isqrt(standing ** slope) + 1 for standing in range(1, count + 1)]
    largest = most if full else min(most, max(-(-total // count), total * loads[0] // sum(loads)))
    least = 1 if total - largest >= count - 1 else 0
    given, rest = [largest] + [least] * (count - 1), total - largest - least * (count - 1)
    while rest > 0:
        candidates = [i for i in range(1, count) if given[i] < largest] or [i for i in range(1, count) if given[i] < most]
        pool, remaining = sum([loads[i] for i in candidates]), rest
        for i in candidates:
            addition = min(most - given[i], max(1, remaining * loads[i] // pool), rest)
            given[i] = given[i] + addition
            rest = rest - addition
    return np.array(given)


def centred(rng, dims, width, limit, shards=(), held_as=jnp.bfloat16):
    factor_of = block_scale(rng, dims, shards, -0.22, 0.18) if shards else 1.0
    values = jax.random.normal(rng, dims, jnp.float32) * width * factor_of
    return jnp.minimum(jnp.maximum(values, -limit), limit).astype(held_as)


def setup_inputs(seed: int = 0) -> dict:
    key_of = jax.random.split(jax.random.key(seed), 18)
    tokens = draw_tokens(jax.random.fold_in(key_of[17], 71), 0)
    norm_gain = jnp.clip(1.0 + 0.15 * jax.random.normal(key_of[1], (D,), jnp.float32), 0.25, 1.75)
    in_weight = centred(key_of[2], (D, 2, DI), D ** -0.5, 0.09375, ((0, 4), (2, 8)))
    conv_weight = jnp.clip(jax.random.uniform(key_of[3], (CONV, DI), jnp.float32, -0.5, 0.5) * block_scale(key_of[3], (CONV, DI), ((1, 8),), -0.4, 0.0), -0.5, 0.5)
    conv_bias = jnp.clip(jax.random.uniform(key_of[4], (DI,), jnp.float32, -0.5, 0.5) * block_scale(key_of[4], (DI,), ((0, 8),), -0.4, 0.0), -0.5, 0.5)
    proj_weight = centred(key_of[5], (DI, RANK + 2 * STATE), DI ** -0.5, 0.0625, ((0, 8),))
    step_weight = centred(key_of[6], (RANK, DI), (3.0 / RANK ** 0.5), 1.0, ((1, 8),))
    step_bias = jnp.clip(-5.0 + 4.0 * jax.random.uniform(key_of[7], (DI,), jnp.float32) ** block_scale(key_of[7], (DI,), ((0, 8),), -0.2, 0.2), -5.0, -1.0)
    decay_log = jnp.clip(-6.0 + 8.7 * jax.random.uniform(key_of[8], (DI, STATE), jnp.float32) ** block_scale(key_of[8], (DI, STATE), ((0, 8),), -0.2, 0.2), -6.0, 2.7)
    skip_gain = jnp.clip(0.5 + 1.0 * jax.random.uniform(key_of[9], (DI,), jnp.float32) ** block_scale(key_of[9], (DI,), ((0, 8),), -0.2, 0.2), 0.5, 1.5)
    out_weight = centred(key_of[10], (DI, D), DI ** -0.5, 0.0625, ((0, 8), (1, 4)))
    moe_gain = jnp.clip(1.0 + 0.15 * jax.random.normal(key_of[11], (D,), jnp.float32), 0.25, 1.75)
    router_weight = centred(key_of[12], (D, EXPERTS), D ** -0.5, 0.09375)
    routes_keys = jax.random.split(jax.random.fold_in(key_of[13], 1), TOKENS // BLOCK)
    routes_turns = jax.random.permutation(jax.random.fold_in(key_of[13], 3), TOKENS // BLOCK)
    routes = jax.vmap(lambda own, number: shared_out(jax.random.fold_in(key_of[13], 2), own, number, BLOCK, EXPERTS, 2, MOST, 2))(routes_keys, routes_turns).reshape((TOKENS, 2))
    gate_weight = centred(key_of[14], (EXPERTS, D, FF), D ** -0.5, 0.09375, ((0, 8), (2, 4)))
    up_weight = centred(key_of[15], (EXPERTS, D, FF), D ** -0.5, 0.09375, ((0, 8), (2, 4)))
    down_weight = centred(key_of[16], (EXPERTS, FF, D), FF ** -0.5, 0.0625, ((0, 8), (1, 4)))
    return {"tokens": tokens, "norm_gain": norm_gain, "in_weight": in_weight, "conv_weight": conv_weight, "conv_bias": conv_bias, "proj_weight": proj_weight, "step_weight": step_weight, "step_bias": step_bias, "decay_log": decay_log, "skip_gain": skip_gain, "out_weight": out_weight, "moe_gain": moe_gain, "router_weight": router_weight, "routes": routes, "gate_weight": gate_weight, "up_weight": up_weight, "down_weight": down_weight}


EPSILON = 1e-06

def rms_norm(values_in, gain_row):
    as_float = values_in.astype(jnp.float32)
    inverse = lax.rsqrt(lax.optimization_barrier(jnp.mean(as_float * as_float, axis=-1, keepdims=True)) + EPSILON)
    return (as_float * inverse * gain_row).astype(jnp.bfloat16)

def scan_pairs(former, latter):
    return (former[0] * latter[0], latter[0] * former[1] + latter[1])

def route_tables(routes, logits, experts, block_rows, most_slots):
    expert_ids = lax.broadcasted_iota(jnp.int32, (1, 1, experts), 2)
    matches = routes[:, :, None] == expert_ids
    picked = lax.optimization_barrier(jnp.sum(jnp.where(matches, logits[:, None, :], 0.0), axis=2))
    first_share = jax.nn.sigmoid(picked[:, 0] - picked[:, 1])
    shares = jnp.stack([first_share, 1.0 - first_share], axis=1)
    weight_table = lax.optimization_barrier(jnp.sum(jnp.where(matches, shares[:, :, None], 0.0), axis=1))
    counts = lax.optimization_barrier(jnp.sum(matches.astype(jnp.int32), axis=1)).astype(jnp.int32)
    blocked = counts.reshape(-1, block_rows, experts)
    before = (jnp.cumsum(blocked, axis=1) - blocked).astype(jnp.int32)
    slot_ids = lax.broadcasted_iota(jnp.int32, (1, 1, 1, most_slots), 3)
    chosen = (blocked[..., None] > 0) & (before[..., None] == slot_ids)
    slot_table = jnp.where(chosen, 1.0, 0.0).astype(jnp.float32)
    return (slot_table, weight_table.reshape(-1, block_rows, experts))

def mixer_scan(step_size, drive_in, input_map, output_map, decay_rate):
    length = step_size.shape[0]
    blocks = length // TOK_SEQ

    def advance(carried, block_in):
        step_block, drive_block, input_block, output_block = block_in
        decay_step = jnp.exp(step_block[:, :, None] * decay_rate[None])
        inject = (step_block * drive_block)[:, :, None] * input_block[:, None, :]
        cumulated, local_state = lax.associative_scan(scan_pairs, (decay_step, inject), axis=0)
        states = local_state + cumulated * carried[None]
        return (states[-1], jnp.einsum('tcn,tn->tc', states, output_block))
    initial = jnp.zeros((DI, STATE), jnp.float32)
    inputs = (step_size.reshape(blocks, TOK_SEQ, DI), drive_in.reshape(blocks, TOK_SEQ, DI), input_map.reshape(blocks, TOK_SEQ, STATE), output_map.reshape(blocks, TOK_SEQ, STATE))
    final_state, outputs = lax.scan(advance, initial, inputs)
    return outputs.reshape(length, DI)

def reference(tokens, norm_gain, in_weight, conv_weight, conv_bias, proj_weight, step_weight, step_bias, decay_log, skip_gain, out_weight, moe_gain, router_weight, routes, gate_weight, up_weight, down_weight):
    length = tokens.shape[0]
    normed = rms_norm(tokens, norm_gain)
    projected = jnp.dot(normed, in_weight.reshape(D, 2 * DI), preferred_element_type=jnp.float32).astype(jnp.bfloat16)
    mixer_in = projected[:, :DI].astype(jnp.float32)
    gate_in = projected[:, DI:].astype(jnp.float32)
    padded = jnp.pad(mixer_in, ((CONV - 1, 0), (0, 0)))
    convolved = conv_bias + jnp.zeros((length, DI), jnp.float32)
    for tap_index in range(CONV):
        convolved = convolved + conv_weight[tap_index] * padded[tap_index:tap_index + length]
    activated = jax.nn.silu(convolved).astype(jnp.bfloat16)
    features = jnp.dot(activated, proj_weight, preferred_element_type=jnp.float32)
    low_rank = features[:, :RANK].astype(jnp.bfloat16)
    input_map = features[:, RANK:RANK + STATE]
    output_map = features[:, RANK + STATE:]
    step_size = jax.nn.softplus(jnp.dot(low_rank, step_weight, preferred_element_type=jnp.float32) + step_bias)
    decay_rate = -jnp.exp(decay_log)
    drive_in = activated.astype(jnp.float32)
    scanned = mixer_scan(step_size, drive_in, input_map, output_map, decay_rate)
    gated_out = ((scanned + skip_gain * drive_in) * jax.nn.silu(gate_in)).astype(jnp.bfloat16)
    mamba_out = jnp.dot(gated_out, out_weight, preferred_element_type=jnp.float32)
    hidden_state = (tokens.astype(jnp.float32) + mamba_out).astype(jnp.bfloat16)
    moe_in = rms_norm(hidden_state, moe_gain)
    logits = jnp.dot(moe_in, router_weight, preferred_element_type=jnp.float32)
    slot_table, weight_table = route_tables(routes, logits, EXPERTS, BLOCK, MOST)
    slotted = jnp.einsum('btem,btd->ebmd', slot_table, moe_in.reshape(-1, BLOCK, D).astype(jnp.float32)).astype(jnp.bfloat16)
    shard_width = FF // N_SEQ

    def one_expert(operands):
        rows_in, gate_mat, up_mat, down_mat = operands
        flat_rows = rows_in.reshape(-1, D)
        gate_act = jnp.dot(flat_rows, gate_mat, preferred_element_type=jnp.float32)
        up_act = jnp.dot(flat_rows, up_mat, preferred_element_type=jnp.float32)
        hidden = (jax.nn.silu(gate_act) * up_act).astype(jnp.bfloat16)
        running = jnp.zeros((flat_rows.shape[0], D), jnp.float32)
        for shard_index in range(N_SEQ):
            lower_edge = shard_index * shard_width
            partial_value = jnp.dot(hidden[:, lower_edge:lower_edge + shard_width], down_mat[lower_edge:lower_edge + shard_width], preferred_element_type=jnp.float32).astype(jnp.bfloat16)
            partial_value = lax.optimization_barrier(partial_value)
            running = running + partial_value.astype(jnp.float32)
        return running.astype(jnp.bfloat16).reshape(rows_in.shape)
    expert_out = lax.map(one_expert, (slotted, gate_weight, up_weight, down_weight))
    mixed_weights = slot_table * weight_table[..., None]
    moe_out = jnp.einsum('btem,ebmd->btd', mixed_weights, expert_out.astype(jnp.float32)).reshape(length, D)
    return (hidden_state.astype(jnp.float32) + moe_out).astype(jnp.bfloat16)
```

```python
import functools

import jax
import jax.numpy as jnp
from jax import lax
from jax.experimental import pallas as pl
from jax.experimental.pallas import tpu as pltpu
from jax.sharding import PartitionSpec as P

EPSILON = 1e-06
HALO = 16
MIB = 1 << 20
BF16 = jnp.bfloat16
F32 = jnp.float32

VMEM = pl.BlockSpec(memory_space=pltpu.VMEM)
SMEM = pl.BlockSpec(memory_space=pltpu.SMEM)


def partner(block, axis, mask):
    size = lax.axis_size(axis)
    return lax.ppermute(block, axis, [(i, i ^ mask) for i in range(size)])


def later_partner(block, axis, mask):
    size = lax.axis_size(axis)
    return lax.ppermute(block, axis, [(i, i ^ mask) for i in range(size) if i < i ^ mask])


def after(values, *done):
    flat, tree = jax.tree.flatten(values)
    held = lax.optimization_barrier((*flat, *done))
    return jax.tree.unflatten(tree, held[: len(flat)])


def shape(dims, dtype):
    return jax.ShapeDtypeStruct(tuple(dims), dtype)


def kernel_call(body, outs, in_specs, scratch=(), flops=0, moved=0, limit=32):
    return pl.pallas_call(
        body,
        out_shape=outs,
        in_specs=in_specs,
        out_specs=jax.tree.map(lambda _: VMEM, outs),
        scratch_shapes=list(scratch),
        compiler_params=pltpu.CompilerParams(vmem_limit_bytes=limit * MIB),
        cost_estimate=pl.CostEstimate(flops=flops, bytes_accessed=moved, transcendentals=0),
    )


def dot(left, right):
    return jnp.dot(left, right, preferred_element_type=F32)


def silu(v):
    return v / (1.0 + jnp.exp(-v))


def norm_body(seq, place, tokens, gain, own, *sends):
    values = tokens[...].astype(F32)
    inverse = lax.rsqrt(jnp.mean(values * values, axis=-1, keepdims=True) + EPSILON)
    own_width = own.shape[1]
    half = own_width // 2
    me, core = place[0], place[1]

    def columns(start, width):
        start = pl.multiple_of(start, 128)
        part = tokens[:, pl.ds(start, width)].astype(F32)
        return (part * inverse * gain[:, pl.ds(start, width)]).astype(BF16)

    own[...] = columns(me * own_width, own_width)
    for mask in range(1, seq):
        sends[mask - 1][...] = columns((me ^ mask) * own_width + core * half, half)


def project(x_own, x_mine, x_other, weight, core):
    half = weight.shape[0] // 2
    yield dot(x_own[...], weight[...])
    first = weight[pl.ds(pl.multiple_of(core * half, half), half), :]
    second = weight[pl.ds(pl.multiple_of((1 - core) * half, half), half), :]
    for mine, other in zip(x_mine, x_other):
        yield dot(mine[...], first) + dot(other[...], second)


def mixer_project_body(seq, place, x_own, *refs):
    x_mine, x_other = refs[: seq - 1], refs[seq - 1 : 2 * seq - 2]
    weight = refs[2 * seq - 2]
    outs = refs[2 * seq - 1 : 3 * seq - 1]
    tails = refs[3 * seq - 1]
    me, core = place[0], place[1]
    length = x_own.shape[0]
    for index, product in enumerate(project(x_own, x_mine, x_other, weight, core)):
        outs[index][HALO:, :] = product.astype(outs[index].dtype)
        tails[index] = product[length - HALO :, :]
    for mask in range(seq):
        shard = me ^ mask
        source = me ^ jnp.maximum(shard - 1, 0)
        before = jnp.where(shard > 0, tails[source], 0.0)
        outs[mask][:HALO, :] = before.astype(outs[mask].dtype)


def gate_project_body(seq, place, x_own, *refs):
    x_mine, x_other = refs[: seq - 1], refs[seq - 1 : 2 * seq - 2]
    weight = refs[2 * seq - 2]
    outs = refs[2 * seq - 1 :]
    for index, product in enumerate(project(x_own, x_mine, x_other, weight, place[1])):
        outs[index][...] = product.astype(outs[index].dtype)


def conv_body(seq, *refs):
    terms = refs[:seq]
    taps, bias, proj, activated, features = refs[seq:]
    total = terms[0][...]
    for term in terms[1:]:
        total = total + term[...].astype(F32)
    padded = total.astype(BF16).astype(F32)
    length = activated.shape[0]
    count = taps.shape[0]
    convolved = bias[...]
    for tap in range(count):
        start = HALO - count + 1 + tap
        convolved = convolved + taps[tap : tap + 1, :] * padded[start : start + length]
    rounded = silu(convolved).astype(BF16)
    activated[...] = rounded
    features[...] = dot(rounded, proj[...])


def scan_body(maps, low_rank, activated, step_weight, step_bias, rate, y, cumulated, final, steps, drive):
    length, groups, lanes = y.shape
    states = rate.shape[0]
    raw = dot(low_rank[...], step_weight[...]) + step_bias[...]
    step_size = jnp.maximum(raw, 0.0) + jnp.log1p(jnp.exp(-jnp.abs(raw)))
    driven = step_size * activated[...].astype(F32)
    for group in range(groups):
        part = slice(group * lanes, (group + 1) * lanes)
        steps[:, group, :] = step_size[:, part]
        drive[:, group, :] = driven[:, part]
    rates = [rate[n] for n in range(states)]

    def advance(t, carry):
        state, running = carry
        step, push = steps[t], drive[t]
        running = running + step
        fresh = []
        out = jnp.zeros_like(step)
        for n in range(states):
            value = jnp.exp(step * rates[n]) * state[n] + push * maps[t, n]
            out = out + value * maps[t, states + n]
            fresh.append(value)
        y[t] = out
        cumulated[t] = running
        return tuple(fresh), running

    zero = jnp.zeros((groups, lanes), F32)
    state, running = lax.fori_loop(0, length, advance, ((zero,) * states, zero), unroll=4)
    for n in range(states):
        final[n] = state[n]
    final[states] = running


def gated_body(seq, own_rows, place, maps, *refs):
    arrived = refs[: seq - 1]
    y, cumulated, rate, activated, skip_gain = refs[seq - 1 : seq + 4]
    gates = refs[seq + 4 : 2 * seq + 4]
    gated, scanned, result = refs[2 * seq + 4 :]
    length, groups, lanes = y.shape
    states = rate.shape[0]
    me, expert = place[0], place[2]
    zero = jnp.zeros((groups, lanes), F32)
    incoming = [zero] * states
    for mask in range(1, seq):
        shard = me ^ mask
        between = zero
        for other in range(1, seq):
            middle = me ^ other
            inside = (shard < middle) & (middle < me)
            between = between + jnp.where(inside, arrived[other - 1][states], 0.0)
        for n in range(states):
            term = jnp.exp(rate[n] * between) * arrived[mask - 1][n]
            incoming[n] = incoming[n] + jnp.where(shard < me, term, 0.0)
    rates = [rate[n] for n in range(states)]

    def correct(t, carry):
        steps = cumulated[t]
        out = y[t]
        for n in range(states):
            out = out + (jnp.exp(steps * rates[n]) * incoming[n]) * maps[t, states + n]
        scanned[t] = out
        return carry

    lax.fori_loop(0, length, correct, 0, unroll=4)
    for group in range(groups):
        part = slice(group * lanes, (group + 1) * lanes)
        gate = gates[0][:, part]
        for term in gates[1:]:
            gate = gate + term[:, part].astype(F32)
        gate = gate.astype(BF16).astype(F32)
        drive = activated[:, part].astype(F32)
        result[:, part] = (scanned[:, group, :] + skip_gain[:, part] * drive) * silu(gate)
    blocks = length // own_rows
    moved = [
        result[pl.ds(pl.multiple_of((expert ^ k) * own_rows, own_rows), own_rows), :]
        for k in range(blocks)
    ]
    gated[...] = jnp.concatenate(moved, axis=0).astype(BF16)


def out_project_body(seq, own_rows, *refs):
    blocks = refs[:seq]
    weight, keep, send = refs[seq:]
    for shard in range(seq):
        product = dot(blocks[shard][...], weight[...])
        for owner in range(product.shape[0] // own_rows):
            rows = product[owner * own_rows : (owner + 1) * own_rows]
            place = (owner // 2, pl.ds(shard * own_rows, own_rows))
            if owner % 2 == 0:
                keep[place[0], place[1], :] = rows
            else:
                send[place[0], place[1], :] = rows.astype(BF16)


def core_sum_body(keep, arrived, own, *sends):
    own[...] = keep[0] + arrived[0].astype(F32)
    for w in range(1, keep.shape[0]):
        sends[w - 1][...] = (keep[w] + arrived[w].astype(F32)).astype(BF16)


def hidden_body(chips, own, *refs):
    terms = refs[: chips - 1]
    residual, choose, hidden = refs[chips - 1 : chips + 2]
    outs = refs[chips + 2 :]
    total = own[...]
    for term in terms:
        total = total + term[...].astype(F32)
    rounded = (residual[...].astype(F32) + total).astype(BF16)
    hidden[...] = rounded
    slots = dot(choose[...], rounded).astype(BF16)
    rows = slots.shape[0] // chips
    for w in range(chips):
        outs[w][...] = slots[w * rows : (w + 1) * rows]


def expert_body(seq, place, *refs):
    pieces = refs[:seq]
    gain, gate, up, hidden, rows = refs[seq:]
    width = pieces[0].shape[1]

    @pl.when(pl.program_id(0) == 0)
    def _():
        square = jnp.zeros((pieces[0].shape[0], 1), F32)
        for piece in pieces:
            values = piece[...].astype(F32)
            square = square + jnp.sum(values * values, axis=-1, keepdims=True)
        inverse = lax.rsqrt(square / (seq * width) + EPSILON)
        for mask in range(seq):
            start = pl.multiple_of((place[0] ^ mask) * width, 128)
            scaled = pieces[mask][...].astype(F32) * inverse * gain[:, pl.ds(start, width)]
            rows[:, pl.ds(start, width)] = scaled.astype(BF16)

    gate_act = dot(rows[...], gate[...])
    up_act = dot(rows[...], up[...])
    hidden[...] = (silu(gate_act) * up_act).astype(BF16)


def down_body(place, hidden, down, out):
    out[...] = dot(hidden[...], down[...]).astype(BF16)


def expert_sum_body(seq, *refs):
    terms, outs = refs[:seq], refs[seq:]
    total = terms[0][...].astype(F32)
    for term in terms[1:]:
        total = total + term[...].astype(F32)
    rounded = total.astype(BF16)
    rows = rounded.shape[0] // len(outs)
    for w, out in enumerate(outs):
        out[...] = rounded[w * rows : (w + 1) * rows]


def combine_body(chips, seq, *refs):
    direct = refs[:chips]
    crossed, hidden, first, second, shares = refs[chips : chips + 5]
    outs = refs[chips + 5 :]
    half = crossed.shape[1]
    table = jnp.concatenate(
        [block for w in range(chips) for block in (direct[w][:half, :], crossed[w])], axis=0
    )
    picked = shares[:, 0:1] * dot(first[...], table) + shares[:, 1:2] * dot(second[...], table)
    mixed = (hidden[...].astype(F32) + picked).astype(BF16)
    rows = mixed.shape[0] // seq
    for d, out in enumerate(outs):
        out[...] = mixed[d * rows : (d + 1) * rows]


def place_body(place, *refs):
    pieces, out = refs[:-1], refs[-1]
    width = pieces[0].shape[1]
    for mask, piece in enumerate(pieces):
        out[:, pl.ds(pl.multiple_of((place[0] ^ mask) * width, 128), width)] = piece[...]


def tile_of(total, most):
    for width in range(most, 0, -128):
        if total % width == 0:
            return width
    return total


def local(
    tokens,
    norm_gain,
    in_weight,
    conv_weight,
    conv_bias,
    proj_weight,
    step_weight,
    step_bias,
    decay_log,
    skip_gain,
    out_weight,
    moe_gain,
    router_weight,
    routes,
    gate_weight,
    up_weight,
    down_weight,
):
    seq, groups = lax.axis_size("seq"), lax.axis_size("expert")
    chips = groups // 2
    me, expert = lax.axis_index("seq"), lax.axis_index("expert")
    core = expert % 2
    place = jnp.stack([me, core, expert]).astype(jnp.int32)
    masks = range(1, seq)
    length, model_width = tokens.shape
    width = model_width // seq
    half = width // 2
    channels = in_weight.shape[2]
    rank_width = step_weight.shape[0]
    state_width = decay_log.shape[1]
    lanes = 128
    tiles = channels // lanes
    own_rows = routes.shape[0]
    experts = router_weight.shape[1]
    most_slots = max(2, 3 * own_rows // experts)
    window = seq * own_rows

    x_own, *x_send = kernel_call(
        functools.partial(norm_body, seq),
        [shape((length, width), BF16)] + [shape((length, half), BF16)] * (seq - 1),
        [SMEM, VMEM, VMEM],
        flops=8 * length * model_width,
        moved=4 * length * model_width,
    )(place, tokens, norm_gain[None])
    x_mine = [partner(block, "seq", mask) for mask, block in zip(masks, x_send)]
    x_other = [partner(block, "expert", 1) for block in x_mine]
    mixer_weight, side_weight = in_weight[:, 0, :], in_weight[:, 1, :]
    in_specs = [SMEM] + [VMEM] * (2 * seq)
    cost = dict(flops=2 * seq * length * width * channels, moved=2 * width * channels)
    mixer_own, *mixer_send = kernel_call(
        functools.partial(mixer_project_body, seq),
        [shape((HALO + length, channels), F32)] + [shape((HALO + length, channels), BF16)] * (seq - 1),
        in_specs,
        [pltpu.VMEM((seq, HALO, channels), F32)],
        **cost,
    )(place, x_own, *x_mine, *x_other, mixer_weight)
    mixer_terms = [partner(block, "seq", mask) for mask, block in zip(masks, mixer_send)]
    side_own, *side_send = kernel_call(
        functools.partial(gate_project_body, seq),
        [shape((length, channels), F32)] + [shape((length, channels), BF16)] * (seq - 1),
        in_specs,
        **cost,
    )(place, x_own, *x_mine, *x_other, side_weight)
    side_send = after(side_send, *mixer_terms)
    side_terms = [partner(block, "seq", mask) for mask, block in zip(masks, side_send)]

    activated, features = kernel_call(
        functools.partial(conv_body, seq),
        [shape((length, channels), BF16), shape((length, proj_weight.shape[1]), F32)],
        [VMEM] * (seq + 3),
        flops=2 * length * channels * proj_weight.shape[1] + 16 * length * channels,
        moved=2 * channels * proj_weight.shape[1] + 10 * length * channels,
    )(mixer_own, *mixer_terms, conv_weight, conv_bias[None], proj_weight)
    features = features + partner(features, "expert", 1)
    sent = features.astype(BF16)
    for w in range(1, chips):
        features = features + partner(sent, "expert", 2 * w).astype(F32)
    low_rank, maps = features[:, :rank_width].astype(BF16), features[:, rank_width:]

    rate = -jnp.exp(jnp.transpose(decay_log)).reshape(state_width, tiles, lanes)
    tiled = shape((length, tiles, lanes), F32)
    y, cumulated, final = kernel_call(
        scan_body,
        [tiled, tiled, shape((state_width + 1, tiles, lanes), F32)],
        [SMEM] + [VMEM] * 5,
        [pltpu.VMEM(tiled.shape, F32)] * 2,
        flops=8 * length * channels * state_width,
        moved=12 * length * channels,
    )(maps, low_rank, activated, step_weight, step_bias[None], rate)
    arrived = [later_partner(final, "seq", mask) for mask in masks]
    gated = kernel_call(
        functools.partial(gated_body, seq, own_rows),
        shape((length, channels), BF16),
        [SMEM, SMEM] + [VMEM] * (2 * seq + 4),
        [pltpu.VMEM(tiled.shape, F32), pltpu.VMEM((length, channels), F32)],
        flops=8 * length * channels * state_width,
        moved=16 * length * channels,
    )(place, maps, *arrived, y, cumulated, rate, activated, skip_gain[None], side_own, *side_terms)

    others = after((routes, tokens), *side_terms)
    near_routes = jnp.stack(
        [others[0]] + [partner(others[0], "seq", mask) for mask in masks]
    )
    own_tokens = lax.dynamic_slice_in_dim(others[1], expert * own_rows, own_rows, 0)
    residual = jnp.concatenate(
        [lax.dynamic_slice_in_dim(own_tokens, me * width, width, 1)]
        + [
            partner(lax.dynamic_slice_in_dim(own_tokens, (me ^ mask) * width, width, 1), "seq", mask)
            for mask in masks
        ],
        axis=0,
    )
    ids = expert ^ jnp.arange(groups, dtype=jnp.int32)
    named = near_routes[None] == ids[:, None, None, None]
    either = named[..., 0] | named[..., 1]
    earlier = jnp.arange(own_rows)[:, None] > jnp.arange(own_rows)[None, :]
    before = jnp.sum((either[:, :, None, :] & earlier).astype(jnp.int32), axis=-1)
    shards = me ^ jnp.arange(seq, dtype=jnp.int32)
    slot = jnp.arange(most_slots, dtype=jnp.int32)
    fits = (
        (jnp.arange(seq)[None, :, None, None, None] == shards[None, None, None, :, None])
        & (before[:, None, None] == slot[None, None, :, None, None])
    )
    slots = groups * seq * most_slots
    choose = (fits & either[:, None, None]).reshape(slots, window).astype(BF16)
    first = (fits & named[:, None, None, :, :, 0]).reshape(slots, window).astype(BF16).T
    second = (fits & named[:, None, None, :, :, 1]).reshape(slots, window).astype(BF16).T

    blocks = [gated] + [partner(gated, "seq", mask) for mask in masks]
    keep, send = kernel_call(
        functools.partial(out_project_body, seq, own_rows),
        [shape((chips, window, width), F32), shape((chips, window, width), BF16)],
        [VMEM] * (seq + 1),
        flops=2 * seq * length * channels * width,
        moved=2 * channels * width + 8 * seq * length * width,
    )(*blocks, out_weight)
    crossing = partner(send, "expert", 1)
    own_sum, *chip_sends = kernel_call(
        core_sum_body,
        [shape((window, width), F32)] + [shape((window, width), BF16)] * (chips - 1),
        [VMEM] * 2,
        flops=chips * window * width,
        moved=10 * chips * window * width,
    )(keep, crossing)
    chip_terms = [partner(block, "expert", 2 * w) for w, block in zip(range(1, chips), chip_sends)]
    per_chip = slots // chips
    per_group = slots // groups
    hidden_state, *outgoing = kernel_call(
        functools.partial(hidden_body, chips),
        [shape((window, width), BF16)] + [shape((per_chip, width), BF16)] * chips,
        [VMEM] * (chips + 2),
        flops=2 * slots * window * width,
        moved=10 * window * width,
    )(own_sum, *chip_terms, residual, choose)

    came = [outgoing[0]] + [
        partner(block, "expert", 2 * w) for w, block in zip(range(1, chips), outgoing[1:])
    ]
    crossed = partner(jnp.stack([block[per_group:] for block in came]), "expert", 1)
    rows = jnp.concatenate(
        [piece for w in range(chips) for piece in (came[w][:per_group], crossed[w])], axis=0
    )
    pieces = [rows] + [partner(rows, "seq", mask) for mask in masks]

    hidden_units = gate_weight.shape[2]
    tile = tile_of(hidden_units, 256)
    hidden = pl.pallas_call(
        functools.partial(expert_body, seq),
        out_shape=shape((slots, hidden_units), BF16),
        grid=(hidden_units // tile,),
        in_specs=[SMEM]
        + [pl.BlockSpec((slots, width), lambda i: (0, 0))] * seq
        + [pl.BlockSpec((1, model_width), lambda i: (0, 0))]
        + [pl.BlockSpec((None, model_width, tile), lambda i: (0, 0, i))] * 2,
        out_specs=pl.BlockSpec((slots, tile), lambda i: (0, i)),
        scratch_shapes=[pltpu.VMEM((slots, model_width), BF16)],
        compiler_params=pltpu.CompilerParams(vmem_limit_bytes=40 * MIB),
        cost_estimate=pl.CostEstimate(
            flops=4 * slots * model_width * hidden_units,
            bytes_accessed=4 * model_width * hidden_units,
            transcendentals=0,
        ),
    )(place, *pieces, moe_gain[None], gate_weight, up_weight)
    expert_out = pl.pallas_call(
        down_body,
        out_shape=shape((seq, slots, width), BF16),
        grid_spec=pltpu.PrefetchScalarGridSpec(
            num_scalar_prefetch=1,
            grid=(seq,),
            in_specs=[
                pl.BlockSpec((slots, hidden_units), lambda i, place: (0, 0)),
                pl.BlockSpec((None, hidden_units, width), lambda i, place: (0, 0, place[0] ^ i)),
            ],
            out_specs=pl.BlockSpec((None, slots, width), lambda i, place: (i, 0, 0)),
        ),
        compiler_params=pltpu.CompilerParams(vmem_limit_bytes=32 * MIB),
        cost_estimate=pl.CostEstimate(
            flops=2 * slots * model_width * hidden_units,
            bytes_accessed=2 * model_width * hidden_units,
            transcendentals=0,
        ),
    )(place, hidden, down_weight)
    terms = [expert_out[0]] + [partner(expert_out[mask], "seq", mask) for mask in masks]
    answers = kernel_call(
        functools.partial(expert_sum_body, seq),
        [shape((per_chip, width), BF16)] * chips,
        [VMEM] * seq,
        flops=seq * slots * width,
        moved=10 * slots * width,
    )(*terms)
    answers = [answers[0]] + [
        partner(block, "expert", 2 * w) for w, block in zip(range(1, chips), answers[1:])
    ]
    crossed_back = partner(jnp.stack([block[per_group:] for block in answers]), "expert", 1)

    values = hidden_state.astype(F32)
    square = jnp.sum(values * values, axis=-1)
    square = seq_sum_by_shard(square.reshape(seq, own_rows), masks, me)
    inverse = lax.rsqrt(square / model_width + EPSILON).reshape(window, 1)
    own_gain = lax.dynamic_slice_in_dim(moe_gain, me * width, width, 0)
    moe_in = (values * inverse * own_gain).astype(BF16)
    own_router = lax.dynamic_slice_in_dim(router_weight, me * width, width, 0)
    logits = dot(moe_in, own_router).reshape(seq, own_rows, experts)
    logits = seq_sum_by_shard(logits, masks, me)
    matches = near_routes[..., None] == jnp.arange(experts, dtype=jnp.int32)
    picked = jnp.sum(jnp.where(matches, logits[:, :, None, :], 0.0), axis=-1)
    first_share = jax.nn.sigmoid(picked[..., 0] - picked[..., 1])
    shares = jnp.stack([first_share, 1.0 - first_share], axis=-1).reshape(window, 2)

    mixed_own, *mixed_send = kernel_call(
        functools.partial(combine_body, chips, seq),
        [shape((own_rows, width), BF16)] * seq,
        [VMEM] * (chips + 5),
        flops=4 * slots * window * width,
        moved=8 * slots * width,
    )(*answers, crossed_back, hidden_state, first, second, shares)
    mixed = [mixed_own] + [partner(block, "seq", mask) for mask, block in zip(masks, mixed_send)]
    return kernel_call(
        place_body,
        shape((own_rows, model_width), BF16),
        [SMEM] + [VMEM] * seq,
        flops=0,
        moved=4 * own_rows * model_width,
    )(place, *mixed)


def seq_sum_by_shard(blocks, masks, me):
    total = blocks
    for mask in masks:
        other = partner(blocks, "seq", mask)
        total = total + jnp.stack([other[d ^ mask] for d in range(blocks.shape[0])])
    return total


def solution(mesh):
    in_specs = (
        P("seq", None),
        P(),
        P("seq", None, "expert"),
        P(None, "expert"),
        P("expert"),
        P("expert", None),
        P(None, "expert"),
        P("expert"),
        P("expert", None),
        P("expert"),
        P("expert", "seq"),
        P(),
        P(),
        P(("seq", "expert"), None),
        P("expert", None, "seq"),
        P("expert", None, "seq"),
        P("expert", "seq", None),
    )
    out_specs = P(("seq", "expert"), None)
    return jax.shard_map(local, mesh=mesh, in_specs=in_specs, out_specs=out_specs, check_vma=False)
```

```python
import functools

import jax
import jax.numpy as jnp
from jax import lax
from jax.experimental import pallas as pl
from jax.experimental.pallas import tpu as pltpu
from jax.sharding import PartitionSpec as P

EPSILON = 1e-06
HALO = 16
ROUTE_ROWS = 2
LOG2_E = 1.4426950408889634
MIB = 1 << 20
BF16 = jnp.bfloat16
F32 = jnp.float32

VMEM = pl.BlockSpec(memory_space=pltpu.VMEM)
SMEM = pl.BlockSpec(memory_space=pltpu.SMEM)


def partner(block, axis, mask):
    size = lax.axis_size(axis)
    return lax.ppermute(block, axis, [(i, i ^ mask) for i in range(size)])


def later_partner(block, axis, mask):
    size = lax.axis_size(axis)
    return lax.ppermute(block, axis, [(i, i ^ mask) for i in range(size) if i < i ^ mask])


def after(values, *done):
    flat, tree = jax.tree.flatten(values)
    held = lax.optimization_barrier((*flat, *done))
    return jax.tree.unflatten(tree, held[: len(flat)])


def shape(dims, dtype):
    return jax.ShapeDtypeStruct(tuple(dims), dtype)


def kernel_call(body, outs, in_specs, scratch=(), flops=0, moved=0, limit=8, deps=()):
    deps = list(deps)
    count = len(in_specs)

    def with_deps(*refs):
        body(*refs[:count], *refs[count + len(deps) :])

    call = pl.pallas_call(
        with_deps,
        out_shape=outs,
        in_specs=list(in_specs) + [pl.BlockSpec(memory_space=pl.ANY)] * len(deps),
        out_specs=jax.tree.map(lambda _: VMEM, outs),
        scratch_shapes=list(scratch),
        compiler_params=pltpu.CompilerParams(vmem_limit_bytes=limit * MIB),
        cost_estimate=pl.CostEstimate(flops=flops, bytes_accessed=moved, transcendentals=0),
    )
    return lambda *operands: call(*operands, *deps)


def dot(left, right):
    return jnp.dot(left, right, preferred_element_type=F32)


def silu(v):
    return v / (1.0 + jnp.exp(-v))


def norm_body(seq, place, tokens, gain, own, *sends):
    values = tokens[...].astype(F32)
    inverse = lax.rsqrt(jnp.mean(values * values, axis=-1, keepdims=True) + EPSILON)
    own_width = own.shape[1]
    half = own_width // 2
    me, core = place[0], place[1]

    def columns(start, width):
        start = pl.multiple_of(start, 128)
        part = tokens[:, pl.ds(start, width)].astype(F32)
        return (part * inverse * gain[:, pl.ds(start, width)]).astype(BF16)

    own[...] = columns(me * own_width, own_width)
    for mask in range(1, seq):
        sends[mask - 1][...] = columns((me ^ mask) * own_width + core * half, half)


def project(x_own, x_mine, x_other, weight, core, branch):
    half = weight.shape[0] // 2
    channels = weight.shape[1] // 2
    part = slice(branch * channels, (branch + 1) * channels)
    yield dot(x_own[...], weight[:, part])
    first = weight[pl.ds(pl.multiple_of(core * half, half), half), part]
    second = weight[pl.ds(pl.multiple_of((1 - core) * half, half), half), part]
    for mine, other in zip(x_mine, x_other):
        yield dot(mine[...], first) + dot(other[...], second)


def mixer_project_body(seq, place, x_own, *refs):
    x_mine, x_other = refs[: seq - 1], refs[seq - 1 : 2 * seq - 2]
    weight, routes = refs[2 * seq - 2 : 2 * seq]
    outs = refs[2 * seq : 3 * seq]
    tails = refs[3 * seq]
    me, core = place[0], place[1]
    length = x_own.shape[0]
    for index, product in enumerate(project(x_own, x_mine, x_other, weight, core, 0)):
        outs[index][HALO:, :] = product.astype(outs[index].dtype)
        tails[index] = product[length - HALO :, :]
    for mask in range(seq):
        shard = me ^ mask
        source = me ^ jnp.maximum(shard - 1, 0)
        before = jnp.where(shard > 0, tails[source], 0.0)
        row = lax.broadcasted_iota(jnp.int32, before.shape, 0)
        before = jnp.where(row < ROUTE_ROWS, routes[mask], before)
        outs[mask][:HALO, :] = before.astype(outs[mask].dtype)


def gate_project_body(seq, place, x_own, *refs):
    x_mine, x_other = refs[: seq - 1], refs[seq - 1 : 2 * seq - 2]
    weight, own_tokens = refs[2 * seq - 2 : 2 * seq]
    outs = refs[2 * seq :]
    length, width = x_own.shape
    for index, product in enumerate(project(x_own, x_mine, x_other, weight, place[1], 1)):
        outs[index][:length, :] = product.astype(outs[index].dtype)
        if index:
            start = pl.multiple_of((place[0] ^ index) * width, 128)
            rows = own_tokens[:, pl.ds(start, width)]
            spare = outs[index].shape[1] - width
            if spare:
                rows = jnp.concatenate([rows, jnp.zeros((rows.shape[0], spare), rows.dtype)], axis=1)
            outs[index][length:, :] = rows


def conv_body(seq, *refs):
    terms = refs[:seq]
    taps, bias, proj, activated, features = refs[seq:]
    total = terms[0][...]
    for term in terms[1:]:
        total = total + term[...].astype(F32)
    padded = total.astype(BF16).astype(F32)
    length = activated.shape[0]
    count = taps.shape[0]
    convolved = bias[...]
    for tap in range(count):
        start = HALO - count + 1 + tap
        convolved = convolved + taps[tap : tap + 1, :] * padded[start : start + length]
    rounded = silu(convolved).astype(BF16)
    activated[...] = rounded
    features[...] = lax.dot_general(
        rounded, proj[...], (((1,), (1,)), ((), ())), preferred_element_type=F32
    )


def scan_body(maps, low_rank, activated, step_weight, step_bias, rate, y, cumulated, final, steps, drive):
    length, groups, lanes = y.shape
    states = rate.shape[0]
    raw = dot(low_rank[...], step_weight[...]) + step_bias[...]
    step_size = jnp.maximum(raw, 0.0) + jnp.log1p(jnp.exp(-jnp.abs(raw)))
    driven = step_size * activated[...].astype(F32)
    for group in range(groups):
        part = slice(group * lanes, (group + 1) * lanes)
        steps[:, group, :] = step_size[:, part]
        drive[:, group, :] = driven[:, part]
    rates = [rate[n] for n in range(states)]

    def advance(t, carry):
        state, running = carry
        step, push = steps[t], drive[t]
        running = running + step
        fresh = []
        out = jnp.zeros_like(step)
        for n in range(states):
            value = jnp.exp2(step * rates[n]) * state[n] + push * maps[t, n]
            out = out + value * maps[t, states + n]
            fresh.append(value)
        y[t] = out
        cumulated[t] = running
        return tuple(fresh), running

    zero = jnp.zeros((groups, lanes), F32)
    state, running = lax.fori_loop(0, length, advance, ((zero,) * states, zero), unroll=4)
    for n in range(states):
        final[n] = state[n]
    final[states] = running


def gated_body(seq, own_rows, place, maps, *refs):
    arrived = refs[: seq - 1]
    y, cumulated, rate, activated, skip_gain = refs[seq - 1 : seq + 4]
    gates = refs[seq + 4 : 2 * seq + 4]
    gated, scanned, result = refs[2 * seq + 4 :]
    length, groups, lanes = y.shape
    states = rate.shape[0]
    me, expert = place[0], place[2]
    zero = jnp.zeros((groups, lanes), F32)
    incoming = [zero] * states
    for mask in range(1, seq):
        shard = me ^ mask
        between = zero
        for other in range(1, seq):
            middle = me ^ other
            inside = (shard < middle) & (middle < me)
            between = between + jnp.where(inside, arrived[other - 1][states], 0.0)
        for n in range(states):
            term = jnp.exp2(rate[n] * between) * arrived[mask - 1][n]
            incoming[n] = incoming[n] + jnp.where(shard < me, term, 0.0)
    rates = [rate[n] for n in range(states)]

    def correct(t, carry):
        steps = cumulated[t]
        out = y[t]
        for n in range(states):
            out = out + (jnp.exp2(steps * rates[n]) * incoming[n]) * maps[t, states + n]
        scanned[t] = out
        return carry

    lax.fori_loop(0, length, correct, 0, unroll=4)
    for group in range(groups):
        part = slice(group * lanes, (group + 1) * lanes)
        gate = gates[0][:, part]
        for term in gates[1:]:
            gate = gate + term[:length, part].astype(F32)
        gate = gate.astype(BF16).astype(F32)
        drive = activated[:, part].astype(F32)
        result[:, part] = (scanned[:, group, :] + skip_gain[:, part] * drive) * silu(gate)
    blocks = length // own_rows
    moved = [
        result[pl.ds(pl.multiple_of((expert ^ k) * own_rows, own_rows), own_rows), :]
        for k in range(blocks)
    ]
    gated[...] = jnp.concatenate(moved, axis=0).astype(BF16)


def out_project_body(seq, own_rows, *refs):
    blocks = refs[:seq]
    weight, keep, send = refs[seq:]
    for shard in range(seq):
        product = dot(blocks[shard][...], weight[...])
        for owner in range(product.shape[0] // own_rows):
            rows = product[owner * own_rows : (owner + 1) * own_rows]
            place = (owner // 2, pl.ds(shard * own_rows, own_rows))
            if owner % 2 == 0:
                keep[place[0], place[1], :] = rows
            else:
                send[place[0], place[1], :] = rows.astype(BF16)


def core_sum_body(keep, arrived, own, *sends):
    own[...] = keep[0] + arrived[0].astype(F32)
    for w in range(1, keep.shape[0]):
        sends[w - 1][...] = (keep[w] + arrived[w].astype(F32)).astype(BF16)


def tables_body(seq, own_rows, most_slots, place, routes, *refs):
    terms, outs = refs[: seq - 1], refs[seq - 1 :]
    choose, first, second, named = outs
    slots, window = choose.shape
    near = routes[:8, :window]
    for term in terms:
        near = near + term[:16, :window].astype(F32)[:8]
    row = lax.broadcasted_iota(jnp.int32, (slots, window), 0)
    column = lax.broadcasted_iota(jnp.int32, (slots, window), 1)
    wanted = (place[2] ^ (row // (seq * most_slots))).astype(F32)
    shard = (row // most_slots) % seq
    hits = [jnp.where(near[i : i + 1, :] == wanted, 1.0, 0.0) for i in range(2)]
    source = lax.broadcasted_iota(jnp.int32, (window, window), 0)
    target = lax.broadcasted_iota(jnp.int32, (window, window), 1)
    earlier = (source // own_rows == target // own_rows) & (source < target)
    before = dot((hits[0] + hits[1]).astype(BF16), jnp.where(earlier, 1.0, 0.0).astype(BF16))
    here = (before == (row % most_slots).astype(F32)) & (shard == (place[0] ^ (column // own_rows)))
    fits = jnp.where(here, 1.0, 0.0)
    choose[...] = (fits * (hits[0] + hits[1])).astype(BF16)
    first[...] = (fits * hits[0]).astype(BF16)
    second[...] = (fits * hits[1]).astype(BF16)
    same = jnp.where(source == target, 1.0, 0.0).astype(BF16)
    named[...] = lax.dot_general(
        same, near.astype(BF16), (((1,), (1,)), ((), ())), preferred_element_type=F32
    )


def hidden_body(chips, seq, place, own, *refs):
    terms, refs = refs[: chips - 1], refs[chips - 1 :]
    own_tokens, refs = refs[0], refs[1:]
    payloads, refs = refs[: seq - 1], refs[seq - 1 :]
    choose, hidden = refs[:2]
    outs = refs[2:]
    total = own[...]
    for term in terms:
        total = total + term[...].astype(F32)
    width = own.shape[1]
    rows = own_tokens.shape[0]
    start = pl.multiple_of(place[0] * width, 128)
    residual = [own_tokens[:, pl.ds(start, width)].astype(F32)]
    for payload in payloads:
        residual.append(payload[payload.shape[0] - rows :, :width].astype(F32))
    rounded = (jnp.concatenate(residual, axis=0) + total).astype(BF16)
    hidden[...] = rounded
    slots = dot(choose[...], rounded).astype(BF16)
    rows = slots.shape[0] // chips
    for w in range(chips):
        outs[w][...] = slots[w * rows : (w + 1) * rows]


def start_copies(jobs, place, sources, outs, sems):
    copies = []
    for index, (source, mask, axis) in enumerate(jobs):
        size = outs[index].shape[axis]
        start = pl.multiple_of((place[0] ^ mask) * size, 128 if axis else 16)
        where = (0, slice(None), pl.ds(start, size)) if axis else (0, pl.ds(start, size))
        copies.append(pltpu.make_async_copy(sources[source].at[where], outs[index], sems.at[index]))
    for copy in copies:
        copy.start()
    return copies


def in_hbm(sources):
    return [pltpu.with_memory_space_constraint(source, pltpu.HBM) for source in sources]


def fetched_shapes(jobs, sources, width):
    blocks = []
    for source, _, axis in jobs:
        rows, columns = sources[source].shape[1:]
        blocks.append(pltpu.VMEM((rows, width) if axis else (width, columns), BF16))
    return blocks


def fetch_body(jobs, count, place, *refs):
    sources, outs, sems = refs[:count], refs[count:-1], refs[-1]
    for copy in start_copies(jobs, place, sources, outs, sems):
        copy.wait()


def fetch(place, jobs, width, sources, deps):
    return kernel_call(
        functools.partial(fetch_body, jobs, len(sources)),
        fetched_shapes(jobs, sources, width),
        [SMEM] + [pl.BlockSpec(memory_space=pltpu.HBM)] * len(sources),
        [pltpu.SemaphoreType.DMA((len(jobs),))],
        moved=2 * len(jobs) * width * sources[0].shape[2],
        deps=deps,
    )(place, *in_hbm(sources))


def expert_body(mask, first, last, model_width, jobs, count, place, piece, gain, gate, up, *refs):
    before, refs = ([], refs) if first else (refs[:3], refs[3:])
    sources, refs = refs[:count], refs[count:]
    outs, refs = (refs[:1], refs[1:]) if last else (refs[:3], refs[3:])
    copies = start_copies(jobs, place, sources, refs[:-1], refs[-1]) if jobs else []
    width = piece.shape[1]
    values = piece[...].astype(F32)
    square = jnp.sum(values * values, axis=-1, keepdims=True)
    if not first:
        square = square + before[2][:, 0:1]
    start = pl.multiple_of((place[0] ^ mask) * width, 128)
    rows = (values * gain[:, pl.ds(start, width)]).astype(BF16)
    inverse = lax.rsqrt(square / model_width + EPSILON)
    if not last:
        outs[2][...] = jnp.broadcast_to(square, outs[2].shape)
    hidden_units = gate.shape[1]
    tile = tile_of(hidden_units, 512)
    for step in range(hidden_units // tile):
        part = slice(step * tile, (step + 1) * tile)
        gate_act = dot(rows, gate[:, part])
        up_act = dot(rows, up[:, part])
        if not first:
            gate_act = gate_act + before[0][:, part]
            up_act = up_act + before[1][:, part]
        if last:
            outs[0][:, part] = (silu(gate_act * inverse) * (up_act * inverse)).astype(BF16)
        else:
            outs[0][:, part] = gate_act
            outs[1][:, part] = up_act
    for copy in copies:
        copy.wait()


def expert_chunk(mask, first, last, place, piece, gain, gate, up, before, jobs, sources):
    slots, width = piece.shape
    model_width, hidden_units = gain.shape[1], gate.shape[1]
    total = shape((slots, hidden_units), F32)
    outs = [total, total, shape((slots, 128), F32)]
    if last:
        outs = [shape((slots, hidden_units), BF16)]
    sources = sources if jobs else []
    far = pl.BlockSpec(memory_space=pltpu.HBM)
    results = kernel_call(
        functools.partial(expert_body, mask, first, last, model_width, jobs, len(sources)),
        outs + fetched_shapes(jobs, sources, width),
        [SMEM] + [VMEM] * (4 + len(before)) + [far] * len(sources),
        [pltpu.SemaphoreType.DMA((len(jobs),))] if jobs else [],
        flops=4 * slots * width * hidden_units,
        moved=4 * width * hidden_units,
        limit=12,
    )(place, piece, gain, gate, up, *before, *in_hbm(sources))
    return results[: len(outs)], results[len(outs) :]


def down_body(hidden, down, out):
    width = out.shape[1]
    tile = tile_of(width, 512)
    for step in range(width // tile):
        part = slice(step * tile, (step + 1) * tile)
        out[:, part] = dot(hidden[...], down[:, part]).astype(BF16)


def down_chunk(hidden, down):
    slots, hidden_units = hidden.shape
    width = down.shape[1]
    return kernel_call(
        down_body,
        shape((slots, width), BF16),
        [VMEM] * 2,
        flops=2 * slots * width * hidden_units,
        moved=2 * width * hidden_units,
        limit=16,
    )(hidden, down)


def expert_sum_body(seq, *refs):
    terms, outs = refs[:seq], refs[seq:]
    total = terms[0][...].astype(F32)
    for term in terms[1:]:
        total = total + term[...].astype(F32)
    rounded = total.astype(BF16)
    rows = rounded.shape[0] // len(outs)
    for w, out in enumerate(outs):
        out[...] = rounded[w * rows : (w + 1) * rows]


def scores_body(experts, hidden, gain, router, scores):
    values = hidden[...].astype(F32)
    part = dot((values * gain[...]).astype(BF16), router[...])
    square = jnp.sum(values * values, axis=-1, keepdims=True)
    lane = lax.broadcasted_iota(jnp.int32, part.shape, 1)
    scores[...] = jnp.where(lane < experts, part, square)


def halves_body(*refs):
    blocks, out = refs[:-1], refs[-1]
    for w, block in enumerate(blocks):
        out[w] = block[out.shape[1] :, :]


def second_halves(blocks, deps=()):
    rows, width = blocks[0].shape
    return kernel_call(
        halves_body,
        shape((len(blocks), rows // 2, width), BF16),
        [VMEM] * len(blocks),
        moved=2 * len(blocks) * rows * width,
        deps=deps,
    )(*blocks)


def rows_body(chips, *refs):
    direct, crossed, out = refs[:chips], refs[chips], refs[chips + 1]
    half = crossed.shape[1]
    out[...] = jnp.concatenate(
        [block for w in range(chips) for block in (direct[w][:half, :], crossed[w])], axis=0
    )


def combine_body(chips, seq, experts, model_width, *refs):
    direct = refs[:chips]
    crossed, hidden, first, second, routes = refs[chips : chips + 5]
    scores = refs[chips + 5 : chips + 5 + seq]
    outs = refs[chips + 5 + seq :]
    rows = outs[0].shape[0]
    total = scores[0][...]
    for mask in range(1, seq):
        other = scores[mask][...]
        total = total + jnp.concatenate(
            [other[(d ^ mask) * rows : ((d ^ mask) + 1) * rows] for d in range(seq)], axis=0
        )
    logits = total * lax.rsqrt(total[:, experts : experts + 1] / model_width + EPSILON)
    lane = lax.broadcasted_iota(jnp.int32, logits.shape, 1).astype(F32)
    picked = [
        jnp.sum(jnp.where(lane == routes[:, i : i + 1], logits, 0.0), axis=-1, keepdims=True)
        for i in range(2)
    ]
    first_share = 1.0 / (1.0 + jnp.exp(picked[1] - picked[0]))
    half = crossed.shape[1]
    table = jnp.concatenate(
        [block for w in range(chips) for block in (direct[w][:half, :], crossed[w])], axis=0
    )

    def rows_of(choice):
        return lax.dot_general(
            choice[...], table, (((0,), (0,)), ((), ())), preferred_element_type=F32
        )

    sent = first_share * rows_of(first) + (1.0 - first_share) * rows_of(second)
    mixed = (hidden[...].astype(F32) + sent).astype(BF16)
    for d, out in enumerate(outs):
        out[...] = mixed[d * rows : (d + 1) * rows]


def place_body(place, *refs):
    pieces, out = refs[:-1], refs[-1]
    width = pieces[0].shape[1]
    for mask, piece in enumerate(pieces):
        out[:, pl.ds(pl.multiple_of((place[0] ^ mask) * width, 128), width)] = piece[...]


def tile_of(total, most):
    for width in range(most, 0, -128):
        if total % width == 0:
            return width
    return total


def local(
    tokens,
    norm_gain,
    in_weight,
    conv_weight,
    conv_bias,
    proj_weight,
    step_weight,
    step_bias,
    decay_log,
    skip_gain,
    out_weight,
    moe_gain,
    router_weight,
    routes,
    gate_weight,
    up_weight,
    down_weight,
):
    seq, groups = lax.axis_size("seq"), lax.axis_size("expert")
    chips = groups // 2
    me, expert = lax.axis_index("seq"), lax.axis_index("expert")
    core = expert % 2
    place = jnp.stack([me, core, expert]).astype(jnp.int32)
    masks = range(1, seq)
    length, model_width = tokens.shape
    width = model_width // seq
    half = width // 2
    channels = in_weight.shape[2]
    rank_width = step_weight.shape[0]
    state_width = decay_log.shape[1]
    lanes = 128
    tiles = channels // lanes
    own_rows = routes.shape[0]
    experts = router_weight.shape[1]
    most_slots = max(2, 3 * own_rows // experts)
    window = seq * own_rows

    x_own, *x_send = kernel_call(
        functools.partial(norm_body, seq),
        [shape((length, width), BF16)] + [shape((length, half), BF16)] * (seq - 1),
        [SMEM, VMEM, VMEM],
        flops=8 * length * model_width,
        moved=4 * length * model_width,
        limit=24,
    )(place, tokens, norm_gain[None])
    x_mine = [partner(block, "seq", mask) for mask, block in zip(masks, x_send)]
    weight = after(in_weight, x_own).reshape(width, 2 * channels)
    x_mine = after(x_mine, weight)
    x_other = [partner(block, "expert", 1) for block in x_mine]
    lane_routes = jnp.transpose(routes).astype(F32)
    spread_routes = jnp.stack(
        [
            jnp.pad(lane_routes, ((0, HALO - ROUTE_ROWS), (d * own_rows, channels - (d + 1) * own_rows)))
            for d in range(seq)
        ]
    )
    in_specs = [SMEM] + [VMEM] * (2 * seq)
    cost = dict(flops=2 * seq * length * width * channels, moved=2 * width * channels, limit=24)
    mixer_own, *mixer_send = kernel_call(
        functools.partial(mixer_project_body, seq),
        [shape((HALO + length, channels), F32)] + [shape((HALO + length, channels), BF16)] * (seq - 1),
        in_specs + [VMEM],
        [pltpu.VMEM((seq, HALO, channels), F32)],
        **cost,
    )(place, x_own, *x_mine, *x_other, weight, spread_routes)
    mixer_terms = [partner(block, "seq", mask) for mask, block in zip(masks, mixer_send)]
    assert width <= channels and window <= channels
    own_tokens = lax.dynamic_slice_in_dim(tokens, expert * own_rows, own_rows, 0)
    side_own, *side_send = kernel_call(
        functools.partial(gate_project_body, seq),
        [shape((length, channels), F32)] + [shape((length + own_rows, channels), BF16)] * (seq - 1),
        in_specs + [VMEM],
        **cost,
    )(place, x_own, *x_mine, *x_other, weight, own_tokens)

    early = seq // 2
    mixer_own = after(mixer_own, side_own)
    activated, features = kernel_call(
        functools.partial(conv_body, seq),
        [shape((length, channels), BF16), shape((length, proj_weight.shape[1]), F32)],
        [VMEM] * (seq + 3),
        flops=2 * length * channels * proj_weight.shape[1] + 16 * length * channels,
        moved=2 * channels * proj_weight.shape[1] + 10 * length * channels,
        limit=16,
    )(mixer_own, *mixer_terms, conv_weight, conv_bias[None], jnp.transpose(proj_weight))
    features = features + partner(features, "expert", 1)
    sent = features.astype(BF16)
    features_came = [partner(sent, "expert", 2 * w) for w in range(1, chips)]
    side_send = after(side_send[:early], mixer_terms[early - 1]) + after(side_send[early:], features_came[0])
    side_terms = [partner(block, "seq", mask) for mask, block in zip(masks, side_send)]
    for term in features_came:
        features = features + term.astype(F32)
    low_rank, maps = features[:, :rank_width].astype(BF16), features[:, rank_width:]

    rate = -LOG2_E * jnp.exp(jnp.transpose(decay_log)).reshape(state_width, tiles, lanes)
    tiled = shape((length, tiles, lanes), F32)
    y, cumulated, final = kernel_call(
        scan_body,
        [tiled, tiled, shape((state_width + 1, tiles, lanes), F32)],
        [SMEM] + [VMEM] * 5,
        [pltpu.VMEM(tiled.shape, F32)] * 2,
        flops=8 * length * channels * state_width,
        moved=12 * length * channels,
        limit=24,
    )(maps, low_rank, activated, step_weight, step_bias[None], rate)
    arrived = [later_partner(final, "seq", mask) for mask in masks]
    gated = kernel_call(
        functools.partial(gated_body, seq, own_rows),
        shape((length, channels), BF16),
        [SMEM, SMEM] + [VMEM] * (2 * seq + 4),
        [pltpu.VMEM(tiled.shape, F32), pltpu.VMEM((length, channels), F32)],
        flops=8 * length * channels * state_width,
        moved=16 * length * channels,
        limit=24,
    )(place, maps, *arrived, y, cumulated, rate, activated, skip_gain[None], side_own, *side_terms)

    blocks = [gated] + [partner(gated, "seq", mask) for mask in masks]

    slots = groups * seq * most_slots
    per_chip = slots // chips
    per_group = slots // groups
    choose, first, second, named = kernel_call(
        functools.partial(tables_body, seq, own_rows, most_slots),
        [shape((slots, window), BF16)] * 3 + [shape((window, 8), F32)],
        [SMEM, VMEM] + [VMEM] * (seq - 1),
        flops=2 * slots * window * window,
        moved=8 * slots * window,
    )(place, spread_routes[0], *mixer_terms)

    keep, send = kernel_call(
        functools.partial(out_project_body, seq, own_rows),
        [shape((chips, window, width), F32), shape((chips, window, width), BF16)],
        [VMEM] * (seq + 1),
        flops=2 * seq * length * channels * width,
        moved=2 * channels * width + 8 * seq * length * width,
        limit=16,
    )(*blocks, out_weight)
    crossing = partner(send, "expert", 1)
    own_sum, *chip_sends = kernel_call(
        core_sum_body,
        [shape((window, width), F32)] + [shape((window, width), BF16)] * (chips - 1),
        [VMEM] * 2,
        flops=chips * window * width,
        moved=10 * chips * window * width,
    )(keep, crossing)
    chip_terms = [partner(block, "expert", 2 * w) for w, block in zip(range(1, chips), chip_sends)]

    hidden_state, *outgoing = kernel_call(
        functools.partial(hidden_body, chips, seq),
        [shape((window, width), BF16)] + [shape((per_chip, width), BF16)] * chips,
        [SMEM] + [VMEM] * (chips + seq + 1),
        flops=2 * slots * window * width,
        moved=10 * window * width,
    )(place, own_sum, *chip_terms, own_tokens, *side_terms, choose)

    came = [outgoing[0]] + [
        partner(block, "expert", 2 * w) for w, block in zip(range(1, chips), outgoing[1:])
    ]
    sources = [gate_weight, up_weight, down_weight]
    both = lambda mask: [(0, mask, 0), (1, mask, 0)]
    current = list(fetch(place, both(0) + both(1), width, sources[:2], [hidden_state]))
    crossed = partner(second_halves(came, current), "expert", 1)
    rows = kernel_call(
        functools.partial(rows_body, chips),
        shape((slots, width), BF16),
        [VMEM] * (chips + 1),
        moved=4 * slots * width,
    )(*came, crossed)
    pieces = [rows] + [partner(rows, "seq", mask) for mask in masks]

    before, waiting = [], current
    for mask in range(seq):
        jobs = both(mask + 2) if mask + 2 < seq else []
        if mask == max(0, seq - 4):
            jobs = jobs + (both(mask + 3) if mask + 3 < seq else [])
        elif mask == seq - 3:
            jobs = [(2, other, 1) for other in range(seq)]
        elif mask > seq - 3:
            jobs = []
        before, came_in = expert_chunk(
            mask, mask == 0, mask == seq - 1, place, pieces[mask], moe_gain[None], *waiting[:2], before, jobs, sources
        )
        waiting = waiting[2:] + list(came_in)
    downs = waiting
    hidden = before[0]
    sums = []
    for mask in reversed(range(seq)):
        sums = [down_chunk(hidden, downs[mask])] + sums
    terms = [sums[0]] + [partner(sums[mask], "seq", mask) for mask in masks]
    router = jnp.pad(
        lax.dynamic_slice_in_dim(router_weight, me * width, width, 0), ((0, 0), (0, lanes - experts))
    )
    scores = kernel_call(
        functools.partial(scores_body, experts),
        shape((window, lanes), F32),
        [VMEM] * 3,
        flops=2 * window * width * lanes,
        moved=4 * window * width,
        deps=[sums[0]],
    )(hidden_state, lax.dynamic_slice_in_dim(moe_gain, me * width, width, 0)[None], router)
    scores = [scores] + [partner(scores, "seq", mask) for mask in masks]

    answers = kernel_call(
        functools.partial(expert_sum_body, seq),
        [shape((per_chip, width), BF16)] * chips,
        [VMEM] * seq,
        flops=seq * slots * width,
        moved=10 * slots * width,
        deps=scores[1:],
    )(*terms)
    answers = [answers[0]] + [
        partner(block, "expert", 2 * w) for w, block in zip(range(1, chips), answers[1:])
    ]
    crossed_back = partner(second_halves(answers), "expert", 1)

    mixed_own, *mixed_send = kernel_call(
        functools.partial(combine_body, chips, seq, experts, model_width),
        [shape((own_rows, width), BF16)] * seq,
        [VMEM] * (chips + 5 + seq),
        flops=4 * slots * window * width,
        moved=8 * slots * width,
    )(*answers, crossed_back, hidden_state, first, second, named, *scores)
    mixed = [mixed_own] + [partner(block, "seq", mask) for mask, block in zip(masks, mixed_send)]
    return kernel_call(
        place_body,
        shape((own_rows, model_width), BF16),
        [SMEM] + [VMEM] * seq,
        flops=0,
        moved=4 * own_rows * model_width,
    )(place, *mixed)


def solution(mesh):
    in_specs = (
        P("seq", None),
        P(),
        P("seq", None, "expert"),
        P(None, "expert"),
        P("expert"),
        P("expert", None),
        P(None, "expert"),
        P("expert"),
        P("expert", None),
        P("expert"),
        P("expert", "seq"),
        P(),
        P(),
        P(("seq", "expert"), None),
        P("expert", None, "seq"),
        P("expert", None, "seq"),
        P("expert", "seq", None),
    )
    out_specs = P(("seq", "expert"), None)
    return jax.shard_map(local, mesh=mesh, in_specs=in_specs, out_specs=out_specs, check_vma=False)
```

```python
import functools

import jax
import jax.numpy as jnp
from jax import lax
from jax.experimental import pallas as pl
from jax.experimental.pallas import tpu as pltpu
from jax.sharding import PartitionSpec as P

EPSILON = 1e-06
HALO = 16
ROUTE_ROWS = 2
LOG2_E = 1.4426950408889634
MIB = 1 << 20
BF16 = jnp.bfloat16
F32 = jnp.float32

VMEM = pl.BlockSpec(memory_space=pltpu.VMEM)
SMEM = pl.BlockSpec(memory_space=pltpu.SMEM)


def partner(block, axis, mask):
    size = lax.axis_size(axis)
    return lax.ppermute(block, axis, [(i, i ^ mask) for i in range(size)])


def later_partner(block, axis, mask):
    size = lax.axis_size(axis)
    return lax.ppermute(block, axis, [(i, i ^ mask) for i in range(size) if i < i ^ mask])


def after(values, *done):
    flat, tree = jax.tree.flatten(values)
    held = lax.optimization_barrier((*flat, *done))
    return jax.tree.unflatten(tree, held[: len(flat)])


def shape(dims, dtype):
    return jax.ShapeDtypeStruct(tuple(dims), dtype)


def kernel_call(body, outs, in_specs, scratch=(), flops=0, moved=0, limit=8, deps=()):
    deps = list(deps)
    count = len(in_specs)

    def with_deps(*refs):
        body(*refs[:count], *refs[count + len(deps) :])

    call = pl.pallas_call(
        with_deps,
        out_shape=outs,
        in_specs=list(in_specs) + [pl.BlockSpec(memory_space=pl.ANY)] * len(deps),
        out_specs=jax.tree.map(lambda _: VMEM, outs),
        scratch_shapes=list(scratch),
        compiler_params=pltpu.CompilerParams(vmem_limit_bytes=limit * MIB),
        cost_estimate=pl.CostEstimate(flops=flops, bytes_accessed=moved, transcendentals=0),
    )
    return lambda *operands: call(*operands, *deps)


def dot(left, right):
    return jnp.dot(left, right, preferred_element_type=F32)


def silu(v):
    return v / (1.0 + jnp.exp(-v))


def norm_body(seq, place, tokens, gain, own, *sends):
    values = tokens[...].astype(F32)
    inverse = lax.rsqrt(jnp.mean(values * values, axis=-1, keepdims=True) + EPSILON)
    own_width = own.shape[1]
    half = own_width // 2
    me, core = place[0], place[1]

    def columns(start, width):
        part = pl.ds(pl.multiple_of(start, 128), width)
        return (tokens[:, part].astype(F32) * inverse * gain[:, part]).astype(BF16)

    own[...] = columns(me * own_width, own_width)
    for mask in range(1, seq):
        sends[mask - 1][...] = columns((me ^ mask) * own_width + core * half, half)


def pass_body(*refs):
    for block, out in zip(refs[: len(refs) // 2], refs[len(refs) // 2 :]):
        out[...] = block[...]


def project(core, own, mine, other, source, branch, weight, sems):
    depth, channels = weight.shape
    parts = sems.shape[0]
    copies = []
    for i in range(parts):
        rows = pl.ds(i * (depth // parts), depth // parts)
        part = source.at[rows, pl.ds(branch * channels, channels)]
        copies.append((rows, pltpu.make_async_copy(part, weight.at[rows], sems.at[i])))
    for _, copy in copies:
        copy.start()
    first = 0.0
    for rows, copy in copies:
        copy.wait()
        first = first + dot(own[:, rows], weight[rows, :])
    yield first
    half = depth // 2
    near = weight[pl.ds(pl.multiple_of(core * half, half), half), :]
    far = weight[pl.ds(pl.multiple_of((1 - core) * half, half), half), :]
    for left, right in zip(mine, other):
        yield dot(left[...], near) + dot(right[...], far)


def mixer_project_body(seq, place, *refs):
    own, mine, other = refs[0], refs[1:seq], refs[seq : 2 * seq - 1]
    refs = refs[2 * seq - 1 :]
    (weight, routes), outs, (tails, held, sems) = refs[:2], refs[2 : seq + 2], refs[seq + 2 :]
    me = place[0]
    length = own.shape[0]
    for index, product in enumerate(project(place[1], own, mine, other, weight, 0, held, sems)):
        outs[index][HALO:, :] = product.astype(outs[index].dtype)
        tails[index] = product[length - HALO :, :]
    for mask in range(seq):
        shard = me ^ mask
        source = me ^ jnp.maximum(shard - 1, 0)
        before = jnp.where(shard > 0, tails[source], 0.0)
        row = lax.broadcasted_iota(jnp.int32, before.shape, 0)
        before = jnp.where(row < ROUTE_ROWS, routes[mask], before)
        outs[mask][:HALO, :] = before.astype(outs[mask].dtype)


def gate_project_body(seq, place, *refs):
    own, mine, other = refs[0], refs[1:seq], refs[seq : 2 * seq - 1]
    refs = refs[2 * seq - 1 :]
    (weight, own_tokens), outs, (held, sems) = refs[:2], refs[2 : seq + 2], refs[seq + 2 :]
    length, width = own.shape
    for index, product in enumerate(project(place[1], own, mine, other, weight, 1, held, sems)):
        outs[index][:length, :] = product.astype(outs[index].dtype)
        if index:
            start = pl.multiple_of((place[0] ^ index) * width, 128)
            rows = own_tokens[:, pl.ds(start, width)]
            spare = outs[index].shape[1] - width
            if spare:
                rows = jnp.concatenate([rows, jnp.zeros((rows.shape[0], spare), rows.dtype)], axis=1)
            outs[index][length:, :] = rows


def conv_body(seq, *refs):
    terms = refs[:seq]
    taps, bias, proj, activated, features = refs[seq:]
    total = terms[0][...]
    for term in terms[1:]:
        total = total + term[...].astype(F32)
    padded = total.astype(BF16).astype(F32)
    length = activated.shape[0]
    count = taps.shape[0]
    convolved = bias[...]
    for tap in range(count):
        start = HALO - count + 1 + tap
        convolved = convolved + taps[tap : tap + 1, :] * padded[start : start + length]
    rounded = silu(convolved).astype(BF16)
    activated[...] = rounded
    features[...] = lax.dot_general(
        rounded, proj[...], (((1,), (1,)), ((), ())), preferred_element_type=F32
    )


def scan_body(maps, low_rank, activated, step_weight, step_bias, rate, y, cumulated, final, steps, drive):
    length, groups, lanes = y.shape
    states = rate.shape[0]
    raw = dot(low_rank[...], step_weight[...]) + step_bias[...]
    step_size = jnp.maximum(raw, 0.0) + jnp.log1p(jnp.exp(-jnp.abs(raw)))
    driven = step_size * activated[...].astype(F32)
    for group in range(groups):
        part = slice(group * lanes, (group + 1) * lanes)
        steps[:, group, :] = step_size[:, part]
        drive[:, group, :] = driven[:, part]
    rates = [rate[n] for n in range(states)]

    def advance(t, carry):
        state, running = carry
        step, push = steps[t], drive[t]
        running = running + step
        fresh = []
        out = jnp.zeros_like(step)
        for n in range(states):
            value = jnp.exp2(step * rates[n]) * state[n] + push * maps[t, n]
            out = out + value * maps[t, states + n]
            fresh.append(value)
        y[t] = out
        cumulated[t] = running
        return tuple(fresh), running

    zero = jnp.zeros((groups, lanes), F32)
    state, running = lax.fori_loop(0, length, advance, ((zero,) * states, zero), unroll=4)
    for n in range(states):
        final[n] = state[n].astype(BF16)
    upper = running.astype(BF16)
    final[states] = upper
    final[states + 1] = (running - upper.astype(F32)).astype(BF16)


def gated_body(seq, own_rows, place, maps, *refs):
    arrived = refs[: seq - 1]
    y, cumulated, rate, activated, skip_gain = refs[seq - 1 : seq + 4]
    gates = refs[seq + 4 : 2 * seq + 4]
    gated, scanned, result = refs[2 * seq + 4 :]
    length, groups, lanes = y.shape
    states = rate.shape[0]
    me, expert = place[0], place[2]
    zero = jnp.zeros((groups, lanes), F32)
    incoming = [zero] * states
    sums = [block[states].astype(F32) + block[states + 1].astype(F32) for block in arrived]
    for mask in range(1, seq):
        shard = me ^ mask
        between = zero
        for other in range(1, seq):
            middle = me ^ other
            inside = (shard < middle) & (middle < me)
            between = between + jnp.where(inside, sums[other - 1], 0.0)
        for n in range(states):
            term = jnp.exp2(rate[n] * between) * arrived[mask - 1][n].astype(F32)
            incoming[n] = incoming[n] + jnp.where(shard < me, term, 0.0)
    rates = [rate[n] for n in range(states)]

    def correct(t, carry):
        steps = cumulated[t]
        out = y[t]
        for n in range(states):
            out = out + (jnp.exp2(steps * rates[n]) * incoming[n]) * maps[t, states + n]
        scanned[t] = out
        return carry

    lax.fori_loop(0, length, correct, 0, unroll=4)
    for group in range(groups):
        part = slice(group * lanes, (group + 1) * lanes)
        gate = gates[0][:, part]
        for term in gates[1:]:
            gate = gate + term[:length, part].astype(F32)
        gate = gate.astype(BF16).astype(F32)
        drive = activated[:, part].astype(F32)
        result[:, part] = (scanned[:, group, :] + skip_gain[:, part] * drive) * silu(gate)
    blocks = length // own_rows
    moved = [
        result[pl.ds(pl.multiple_of((expert ^ k) * own_rows, own_rows), own_rows), :]
        for k in range(blocks)
    ]
    gated[...] = jnp.concatenate(moved, axis=0).astype(BF16)


def out_project_body(seq, own_rows, *refs):
    blocks = refs[:seq]
    weight, keep, send = refs[seq:]
    for shard in range(seq):
        product = dot(blocks[shard][...], weight[...])
        for owner in range(product.shape[0] // own_rows):
            rows = product[owner * own_rows : (owner + 1) * own_rows]
            place = (owner // 2, pl.ds(shard * own_rows, own_rows))
            if owner % 2 == 0:
                keep[place[0], place[1], :] = rows
            else:
                send[place[0], place[1], :] = rows.astype(BF16)


def core_sum_body(keep, arrived, own, *sends):
    own[...] = keep[0] + arrived[0].astype(F32)
    for w in range(1, keep.shape[0]):
        sends[w - 1][...] = (keep[w] + arrived[w].astype(F32)).astype(BF16)


def tables_body(seq, own_rows, most_slots, place, routes, *refs):
    terms, outs = refs[: seq - 1], refs[seq - 1 :]
    choose, first, second, named = outs
    slots, window = choose.shape
    near = routes[:8, :window]
    for term in terms:
        near = near + term[:16, :window].astype(F32)[:8]
    row = lax.broadcasted_iota(jnp.int32, (slots, window), 0)
    column = lax.broadcasted_iota(jnp.int32, (slots, window), 1)
    wanted = (place[2] ^ (row // (seq * most_slots))).astype(F32)
    shard = (row // most_slots) % seq
    hits = [jnp.where(near[i : i + 1, :] == wanted, 1.0, 0.0) for i in range(2)]
    source = lax.broadcasted_iota(jnp.int32, (window, window), 0)
    target = lax.broadcasted_iota(jnp.int32, (window, window), 1)
    earlier = (source // own_rows == target // own_rows) & (source < target)
    before = dot((hits[0] + hits[1]).astype(BF16), jnp.where(earlier, 1.0, 0.0).astype(BF16))
    numbered = jnp.where(before == (row % most_slots).astype(F32), 1.0, 0.0)
    here = jnp.where(shard == (place[0] ^ (column // own_rows)), numbered, 0.0)
    choose[...] = (here * (hits[0] + hits[1])).astype(BF16)
    first[...] = (numbered * hits[0])[:, :own_rows]
    second[...] = (numbered * hits[1])[:, :own_rows]
    same = jnp.where(source == target, 1.0, 0.0).astype(BF16)
    columns = lax.dot_general(
        same, near.astype(BF16), (((1,), (1,)), ((), ())), preferred_element_type=F32
    )
    named[...] = columns[:own_rows]


def reordered(table, outer, inner, count):
    rows = table.shape[0]
    row = lax.broadcasted_iota(jnp.int32, (rows, rows), 0)
    column = lax.broadcasted_iota(jnp.int32, (rows, rows), 1)
    big, small, number = row // (inner * count), (row // count) % inner, row % count
    choice = jnp.where(column == small * (outer * count) + big * count + number, 1.0, 0.0).astype(BF16)
    return dot(choice, table).astype(BF16)


def hidden_body(chips, seq, place, own, *refs):
    terms, refs = refs[: chips - 1], refs[chips - 1 :]
    own_tokens, refs = refs[0], refs[1:]
    payloads, refs = refs[: seq - 1], refs[seq - 1 :]
    choose, hidden = refs[0], refs[1 : 1 + seq]
    outs = refs[1 + seq :]
    total = own[...]
    for term in terms:
        total = total + term[...].astype(F32)
    width = own.shape[1]
    rows = own_tokens.shape[0]
    start = pl.multiple_of(place[0] * width, 128)
    residual = [own_tokens[:, pl.ds(start, width)].astype(F32)]
    for payload in payloads:
        residual.append(payload[payload.shape[0] - rows :, :width].astype(F32))
    rounded = (jnp.concatenate(residual, axis=0) + total).astype(BF16)
    for d, out in enumerate(hidden):
        out[...] = rounded[d * rows : (d + 1) * rows]
    slots = dot(choose[...], rounded).astype(BF16)
    rows = slots.shape[0] // chips
    for w in range(chips):
        outs[w][...] = slots[w * rows : (w + 1) * rows]


def start_copies(jobs, place, sources, outs, sems):
    copies = []
    for index, (source, mask, axis) in enumerate(jobs):
        size = outs[index].shape[axis]
        if axis:
            where = (0, slice(None), pl.ds(mask * size, size))
        else:
            where = (0, pl.ds(pl.multiple_of((place[0] ^ mask) * size, 16), size))
        copies.append(pltpu.make_async_copy(sources[source].at[where], outs[index], sems.at[index]))
    for copy in copies:
        copy.start()
    return copies


def in_hbm(sources):
    return [pltpu.with_memory_space_constraint(source, pltpu.HBM) for source in sources]


def fetched_shapes(jobs, sources, width):
    blocks = []
    for source, _, axis in jobs:
        rows, columns = sources[source].shape[1:]
        blocks.append(pltpu.VMEM((rows, width) if axis else (width, columns), BF16))
    return blocks


def fetch_body(jobs, count, place, *refs):
    sources, outs, sems = refs[:count], refs[count:-1], refs[-1]
    for copy in start_copies(jobs, place, sources, outs, sems):
        copy.wait()


def fetch(place, jobs, width, sources, deps):
    return kernel_call(
        functools.partial(fetch_body, jobs, len(sources)),
        fetched_shapes(jobs, sources, width),
        [SMEM] + [pl.BlockSpec(memory_space=pltpu.HBM)] * len(sources),
        [pltpu.SemaphoreType.DMA((len(jobs),))],
        moved=2 * len(jobs) * width * sources[0].shape[2],
        deps=deps,
    )(place, *in_hbm(sources))


def expert_body(mask, first, last, model_width, jobs, count, place, piece, gain, gate, up, *refs):
    before, refs = ([], refs) if first else (refs[:3], refs[3:])
    sources, refs = refs[:count], refs[count:]
    outs, refs = (refs[:1], refs[1:]) if last else (refs[:3], refs[3:])
    copies = start_copies(jobs, place, sources, refs[:-1], refs[-1]) if jobs else []
    width = piece.shape[1]
    values = piece[...].astype(F32)
    square = jnp.sum(values * values, axis=-1, keepdims=True)
    if not first:
        square = square + before[2][:, 0:1]
    start = pl.multiple_of((place[0] ^ mask) * width, 128)
    rows = (values * gain[:, pl.ds(start, width)]).astype(BF16)
    inverse = lax.rsqrt(square / model_width + EPSILON)
    if not last:
        outs[2][...] = jnp.broadcast_to(square, outs[2].shape)
    hidden_units = gate.shape[1]
    tile = tile_of(hidden_units, 512)
    for step in range(hidden_units // tile):
        part = slice(step * tile, (step + 1) * tile)
        gate_act = dot(rows, gate[:, part])
        up_act = dot(rows, up[:, part])
        if not first:
            gate_act = gate_act + before[0][:, part]
            up_act = up_act + before[1][:, part]
        if last:
            outs[0][:, part] = (silu(gate_act * inverse) * (up_act * inverse)).astype(BF16)
        else:
            outs[0][:, part] = gate_act
            outs[1][:, part] = up_act
    for copy in copies:
        copy.wait()


def expert_chunk(mask, first, last, place, piece, gain, gate, up, before, jobs, sources):
    slots, width = piece.shape
    model_width, hidden_units = gain.shape[1], gate.shape[1]
    total = shape((slots, hidden_units), F32)
    outs = [total, total, shape((slots, 128), F32)]
    if last:
        outs = [shape((slots, hidden_units), BF16)]
    sources = sources if jobs else []
    far = pl.BlockSpec(memory_space=pltpu.HBM)
    results = kernel_call(
        functools.partial(expert_body, mask, first, last, model_width, jobs, len(sources)),
        outs + fetched_shapes(jobs, sources, width),
        [SMEM] + [VMEM] * (4 + len(before)) + [far] * len(sources),
        [pltpu.SemaphoreType.DMA((len(jobs),))] if jobs else [],
        flops=4 * slots * width * hidden_units,
        moved=4 * width * hidden_units,
        limit=12,
    )(place, piece, gain, gate, up, *before, *in_hbm(sources))
    return results[: len(outs)], results[len(outs) :]


def down_body(seq, place, hidden, *refs):
    downs, outs, product = refs[:seq], refs[seq:-1], refs[-1]
    width = downs[0].shape[1]
    tile = tile_of(width, 512)
    for block, down in enumerate(downs):
        for step in range(width // tile):
            part = slice(step * tile, (step + 1) * tile)
            to = slice(block * width + step * tile, block * width + (step + 1) * tile)
            product[:, to] = dot(hidden[...], down[:, part]).astype(BF16)
    for mask, out in enumerate(outs):
        rows = out.shape[0]
        out[...] = product[pl.ds(pl.multiple_of((place[0] ^ mask) * rows, 16), rows), :]


def expert_sum_body(seq, groups, most_slots, *refs):
    terms, outs = refs[:seq], refs[seq:]
    total = terms[0][...].astype(F32)
    for term in terms[1:]:
        total = total + term[...].astype(F32)
    rounded = total.astype(BF16)
    width = outs[0].shape[1]
    pieces = jnp.concatenate([rounded[:, q * width : (q + 1) * width] for q in range(seq)], axis=0)
    pieces = reordered(pieces, groups, seq, most_slots)
    rows = pieces.shape[0] // len(outs)
    for w, out in enumerate(outs):
        out[...] = pieces[w * rows : (w + 1) * rows]


def shares_body(seq, place, gain, router, named, *refs):
    pieces, rows, shares = refs[:seq], refs[seq], refs[seq + 1]
    width = pieces[0].shape[1]
    for mask, piece in enumerate(pieces):
        start = pl.multiple_of((place[0] ^ mask) * width, 128)
        rows[:, pl.ds(start, width)] = piece[...].astype(F32)
    values = rows[...]
    inverse = lax.rsqrt(jnp.mean(values * values, axis=-1, keepdims=True) + EPSILON)
    moe_in = (values * inverse * gain[...]).astype(BF16)
    logits = lax.dot_general(
        moe_in, router[...], (((1,), (1,)), ((), ())), preferred_element_type=F32
    )
    lane = lax.broadcasted_iota(jnp.int32, logits.shape, 1).astype(F32)
    picked = [
        jnp.sum(jnp.where(lane == named[:, i : i + 1], logits, 0.0), axis=-1, keepdims=True)
        for i in range(2)
    ]
    first_share = 1.0 / (1.0 + jnp.exp(picked[1] - picked[0]))
    shares[...] = jnp.broadcast_to(first_share, shares.shape)


def halves_body(*refs):
    blocks, out = refs[:-1], refs[-1]
    for w, block in enumerate(blocks):
        out[w] = block[out.shape[1] :, :]


def second_halves(blocks, deps=()):
    rows, width = blocks[0].shape
    return kernel_call(
        halves_body,
        shape((len(blocks), rows // 2, width), BF16),
        [VMEM] * len(blocks),
        moved=2 * len(blocks) * rows * width,
        deps=deps,
    )(*blocks)


def rows_body(chips, seq, groups, most_slots, *refs):
    direct, crossed, out = refs[:chips], refs[chips], refs[chips + 1]
    half = crossed.shape[1]
    table = jnp.concatenate(
        [block for w in range(chips) for block in (direct[w][:half, :], crossed[w])], axis=0
    )
    out[...] = reordered(table, seq, groups, most_slots)


def combine_body(chips, seq, most_slots, *refs):
    direct = refs[:chips]
    crossed, first, second, rows, shares, out = refs[chips:]
    half = crossed.shape[1]
    table = jnp.concatenate(
        [block for w in range(chips) for block in (direct[w][:half, :], crossed[w])], axis=0
    )
    width = table.shape[1]
    row = lax.broadcasted_iota(jnp.int32, first.shape, 0)
    piece = (row // most_slots) % seq
    first_share = shares[:, 0:1]
    for q in range(seq):

        def rows_of(choice):
            chosen = jnp.where(piece == q, choice[...], 0.0).astype(BF16)
            return lax.dot_general(
                chosen, table, (((0,), (0,)), ((), ())), preferred_element_type=F32
            )

        part = slice(q * width, (q + 1) * width)
        sent = first_share * rows_of(first) + (1.0 - first_share) * rows_of(second)
        out[:, part] = (rows[:, part] + sent).astype(BF16)


def tile_of(total, most):
    for width in range(most, 0, -128):
        if total % width == 0:
            return width
    return total


def local(
    tokens,
    norm_gain,
    in_weight,
    conv_weight,
    conv_bias,
    proj_weight,
    step_weight,
    step_bias,
    decay_log,
    skip_gain,
    out_weight,
    moe_gain,
    router_weight,
    routes,
    gate_weight,
    up_weight,
    down_weight,
):
    seq, groups = lax.axis_size("seq"), lax.axis_size("expert")
    chips = groups // 2
    me, expert = lax.axis_index("seq"), lax.axis_index("expert")
    core = expert % 2
    place = jnp.stack([me, core, expert]).astype(jnp.int32)
    masks = range(1, seq)
    length, model_width = tokens.shape
    width = model_width // seq
    channels = in_weight.shape[2]
    rank_width = step_weight.shape[0]
    state_width = decay_log.shape[1]
    lanes = 128
    tiles = channels // lanes
    own_rows = routes.shape[0]
    experts = router_weight.shape[1]
    most_slots = max(2, 3 * own_rows // experts)
    window = seq * own_rows

    x_own, *x_send = kernel_call(
        functools.partial(norm_body, seq),
        [shape((length, width), BF16)] + [shape((length, width // 2), BF16)] * (seq - 1),
        [SMEM, VMEM, VMEM],
        flops=8 * length * model_width,
        moved=4 * length * model_width,
        limit=24,
    )(place, tokens, norm_gain[None])
    x_mine = [partner(block, "seq", mask) for mask, block in zip(masks, x_send)]
    weight = in_hbm([in_weight.reshape(width, 2 * channels)])[0]
    x_passed = kernel_call(
        pass_body,
        [shape((length, width // 2), BF16)] * (seq - 1),
        [VMEM] * (seq - 1),
        deps=[weight],
    )(*x_mine)
    x_other = [partner(block, "expert", 1) for block in x_passed]
    x = [x_own, *x_mine, *x_other]
    lane_routes = jnp.transpose(routes).astype(F32)
    spread_routes = jnp.stack(
        [
            jnp.pad(lane_routes, ((0, HALO - ROUTE_ROWS), (d * own_rows, channels - (d + 1) * own_rows)))
            for d in range(seq)
        ]
    )
    in_specs = [SMEM] + [VMEM] * (2 * seq - 1) + [pl.BlockSpec(memory_space=pltpu.HBM), VMEM]
    scratch = [pltpu.VMEM((width, channels), BF16), pltpu.SemaphoreType.DMA((4,))]
    cost = dict(flops=2 * seq * length * width * channels, moved=2 * width * channels, limit=24)
    mixer_own, *mixer_send = kernel_call(
        functools.partial(mixer_project_body, seq),
        [shape((HALO + length, channels), F32)] + [shape((HALO + length, channels), BF16)] * (seq - 1),
        in_specs,
        [pltpu.VMEM((seq, HALO, channels), F32)] + scratch,
        **cost,
    )(place, *x, weight, spread_routes)
    mixer_terms = [partner(block, "seq", mask) for mask, block in zip(masks, mixer_send)]
    assert width <= channels and window <= channels
    own_tokens = lax.dynamic_slice_in_dim(tokens, expert * own_rows, own_rows, 0)
    side_own, *side_send = kernel_call(
        functools.partial(gate_project_body, seq),
        [shape((length, channels), F32)] + [shape((length + own_rows, channels), BF16)] * (seq - 1),
        in_specs,
        scratch,
        deps=[mixer_terms[seq // 2 - 1]],
        **cost,
    )(place, *x, weight, own_tokens)

    side_terms = [partner(block, "seq", mask) for mask, block in zip(masks, side_send)]
    activated, features = kernel_call(
        functools.partial(conv_body, seq),
        [shape((length, channels), BF16), shape((length, proj_weight.shape[1]), F32)],
        [VMEM] * (seq + 3),
        limit=16,
        deps=[side_own],
    )(mixer_own, *mixer_terms, conv_weight, conv_bias[None], jnp.transpose(proj_weight))
    features = features + partner(features, "expert", 1)
    sent = features.astype(BF16)
    features_came = [partner(sent, "expert", 2 * w) for w in range(1, chips)]
    for term in features_came:
        features = features + term.astype(F32)
    low_rank, maps = features[:, :rank_width].astype(BF16), features[:, rank_width:]

    rate = -LOG2_E * jnp.exp(jnp.transpose(decay_log)).reshape(state_width, tiles, lanes)
    tiled = shape((length, tiles, lanes), F32)
    y, cumulated, final = kernel_call(
        scan_body,
        [tiled, tiled, shape((state_width + 2, tiles, lanes), BF16)],
        [SMEM] + [VMEM] * 5,
        [pltpu.VMEM(tiled.shape, F32)] * 2,
        limit=24,
    )(maps, low_rank, activated, step_weight, step_bias[None], rate)
    arrived = [later_partner(final, "seq", mask) for mask in masks]
    gated = kernel_call(
        functools.partial(gated_body, seq, own_rows),
        shape((length, channels), BF16),
        [SMEM, SMEM] + [VMEM] * (2 * seq + 4),
        [pltpu.VMEM(tiled.shape, F32), pltpu.VMEM((length, channels), F32)],
        limit=24,
    )(place, maps, *arrived, y, cumulated, rate, activated, skip_gain[None], side_own, *side_terms)

    blocks = [gated] + [partner(gated, "seq", mask) for mask in masks]

    slots = groups * seq * most_slots
    per_chip = slots // chips
    per_group = slots // groups
    choose, first, second, named = kernel_call(
        functools.partial(tables_body, seq, own_rows, most_slots),
        [shape((slots, window), BF16)] + [shape((slots, own_rows), F32)] * 2 + [shape((own_rows, 8), F32)],
        [SMEM, VMEM] + [VMEM] * (seq - 1),
        flops=2 * slots * window * window,
        moved=8 * slots * window,
    )(place, spread_routes[0], *mixer_terms)

    keep, send = kernel_call(
        functools.partial(out_project_body, seq, own_rows),
        [shape((chips, window, width), F32), shape((chips, window, width), BF16)],
        [VMEM] * (seq + 1),
        flops=2 * seq * length * channels * width,
        moved=2 * channels * width + 8 * seq * length * width,
        limit=16,
    )(*blocks, out_weight)
    crossing = partner(send, "expert", 1)
    own_sum, *chip_sends = kernel_call(
        core_sum_body,
        [shape((window, width), F32)] + [shape((window, width), BF16)] * (chips - 1),
        [VMEM] * 2,
        flops=chips * window * width,
        moved=10 * chips * window * width,
    )(keep, crossing)
    chip_terms = [partner(block, "expert", 2 * w) for w, block in zip(range(1, chips), chip_sends)]

    sources = [gate_weight, up_weight, down_weight]
    both = lambda mask: [(0, mask, 0), (1, mask, 0)]
    current = list(fetch(place, both(0) + both(1), width, sources[:2], [own_sum]))
    near_hidden = kernel_call(
        functools.partial(hidden_body, chips, seq),
        [shape((own_rows, width), BF16)] * seq + [shape((per_chip, width), BF16)] * chips,
        [SMEM] + [VMEM] * (chips + seq + 1),
        flops=2 * slots * window * width,
        moved=10 * window * width,
        deps=current,
    )(place, own_sum, *chip_terms, own_tokens, *side_terms, choose)
    near_hidden, outgoing = near_hidden[:seq], near_hidden[seq:]

    came = [outgoing[0]] + [
        partner(block, "expert", 2 * w) for w, block in zip(range(1, chips), outgoing[1:])
    ]
    whole = [near_hidden[0]] + [partner(near_hidden[mask], "seq", mask) for mask in masks]
    crossed = partner(second_halves(came, whole[1:]), "expert", 1)
    rows = kernel_call(
        functools.partial(rows_body, chips, seq, groups, most_slots),
        shape((slots, width), BF16),
        [VMEM] * (chips + 1),
        moved=4 * slots * width,
    )(*came, crossed)
    pieces = [rows] + [partner(rows, "seq", mask) for mask in masks]

    before, waiting, downs = [], current, []
    for mask in range(seq):
        jobs = both(mask + 2) if mask + 2 < seq else []
        if mask == seq - 4:
            jobs = both(mask + 2) + both(mask + 3)
        elif mask == seq - 3:
            jobs = [(2, block, 1) for block in range(seq)]
        before, came_in = expert_chunk(
            mask, mask == 0, mask == seq - 1, place, pieces[mask], moe_gain[None], *waiting[:2], before, jobs, sources
        )
        waiting = waiting[2:]
        if mask == seq - 3:
            downs = list(came_in)
        else:
            waiting = waiting + list(came_in)
    hidden = before[0]
    back = groups * most_slots
    sums = kernel_call(
        functools.partial(down_body, seq),
        [shape((back, model_width), BF16)] * seq,
        [SMEM] + [VMEM] * (seq + 1),
        [pltpu.VMEM((slots, model_width), BF16)],
        flops=2 * slots * model_width * gate_weight.shape[2],
        moved=2 * model_width * gate_weight.shape[2],
        limit=16,
    )(place, hidden, *downs)
    terms = [sums[0]] + [partner(sums[mask], "seq", mask) for mask in masks]

    own_hidden, shares = kernel_call(
        functools.partial(shares_body, seq),
        [shape((own_rows, model_width), F32), shape((own_rows, lanes), F32)],
        [SMEM] + [VMEM] * (seq + 3),
        flops=2 * own_rows * model_width * lanes,
        moved=16 * own_rows * model_width,
        deps=[sums[0]],
    )(place, moe_gain[None], jnp.transpose(router_weight), named, *whole)
    answers = kernel_call(
        functools.partial(expert_sum_body, seq, groups, most_slots),
        [shape((per_chip, width), BF16)] * chips,
        [VMEM] * seq,
        flops=seq * slots * width,
        moved=10 * slots * width,
        deps=[shares],
    )(*terms)
    answers = [answers[0]] + [
        partner(block, "expert", 2 * w) for w, block in zip(range(1, chips), answers[1:])
    ]
    crossed_back = partner(second_halves(answers), "expert", 1)
    return kernel_call(
        functools.partial(combine_body, chips, seq, most_slots),
        shape((own_rows, model_width), BF16),
        [VMEM] * (chips + 5),
        flops=4 * slots * own_rows * model_width,
        moved=8 * slots * width,
    )(*answers, crossed_back, first, second, own_hidden, shares)


def solution(mesh):
    in_specs = (
        P("seq", None),
        P(),
        P("seq", None, "expert"),
        P(None, "expert"),
        P("expert"),
        P("expert", None),
        P(None, "expert"),
        P("expert"),
        P("expert", None),
        P("expert"),
        P("expert", "seq"),
        P(),
        P(),
        P(("seq", "expert"), None),
        P("expert", None, "seq"),
        P("expert", None, "seq"),
        P("expert", "seq", None),
    )
    out_specs = P(("seq", "expert"), None)
    return jax.shard_map(local, mesh=mesh, in_specs=in_specs, out_specs=out_specs, check_vma=False)
```

```python
import functools

import jax
import jax.numpy as jnp
from jax import lax
from jax.experimental import pallas as pl
from jax.experimental.pallas import tpu as pltpu
from jax.sharding import PartitionSpec as P

EPSILON = 1e-06
HALO = 16
ROUTE_ROWS = 2
LOG2_E = 1.4426950408889634
MIB = 1 << 20
BF16 = jnp.bfloat16
F32 = jnp.float32

VMEM = pl.BlockSpec(memory_space=pltpu.VMEM)
SMEM = pl.BlockSpec(memory_space=pltpu.SMEM)


def partner(block, axis, mask):
    size = lax.axis_size(axis)
    return lax.ppermute(block, axis, [(i, i ^ mask) for i in range(size)])


def later_partner(block, axis, mask):
    size = lax.axis_size(axis)
    return lax.ppermute(block, axis, [(i, i ^ mask) for i in range(size) if i < i ^ mask])


def after(values, *done):
    flat, tree = jax.tree.flatten(values)
    held = lax.optimization_barrier((*flat, *done))
    return jax.tree.unflatten(tree, held[: len(flat)])


def shape(dims, dtype):
    return jax.ShapeDtypeStruct(tuple(dims), dtype)


def kernel_call(body, outs, in_specs, scratch=(), flops=0, moved=0, limit=8, deps=()):
    deps = list(deps)
    count = len(in_specs)

    def with_deps(*refs):
        body(*refs[:count], *refs[count + len(deps) :])

    call = pl.pallas_call(
        with_deps,
        out_shape=outs,
        in_specs=list(in_specs) + [pl.BlockSpec(memory_space=pl.ANY)] * len(deps),
        out_specs=jax.tree.map(lambda _: VMEM, outs),
        scratch_shapes=list(scratch),
        compiler_params=pltpu.CompilerParams(vmem_limit_bytes=limit * MIB),
        cost_estimate=pl.CostEstimate(flops=flops, bytes_accessed=moved, transcendentals=0),
    )
    return lambda *operands: call(*operands, *deps)


def dot(left, right):
    return jnp.dot(left, right, preferred_element_type=F32)


def silu(v):
    return v / (1.0 + jnp.exp(-v))


def norm_body(seq, place, tokens, gain, own, *sends):
    values = tokens[...].astype(F32)
    inverse = lax.rsqrt(jnp.mean(values * values, axis=-1, keepdims=True) + EPSILON)
    own_width = own.shape[1]
    half = own_width // 2
    me, core = place[0], place[1]

    def columns(start, width):
        part = pl.ds(pl.multiple_of(start, 128), width)
        return (tokens[:, part].astype(F32) * inverse * gain[:, part]).astype(BF16)

    own[...] = columns(me * own_width, own_width)
    for mask in range(1, seq):
        sends[mask - 1][...] = columns((me ^ mask) * own_width + core * half, half)


def pass_body(*refs):
    for block, out in zip(refs[: len(refs) // 2], refs[len(refs) // 2 :]):
        out[...] = block[...]


def project(core, own, mine, other, source, branch, weight, sems):
    depth, channels = weight.shape
    parts = sems.shape[0]
    copies = []
    for i in range(parts):
        rows = pl.ds(i * (depth // parts), depth // parts)
        part = source.at[rows, pl.ds(branch * channels, channels)]
        copies.append((rows, pltpu.make_async_copy(part, weight.at[rows], sems.at[i])))
    for _, copy in copies:
        copy.start()
    first = 0.0
    for rows, copy in copies:
        copy.wait()
        first = first + dot(own[:, rows], weight[rows, :])
    yield first
    half = depth // 2
    near = weight[pl.ds(pl.multiple_of(core * half, half), half), :]
    far = weight[pl.ds(pl.multiple_of((1 - core) * half, half), half), :]
    for left, right in zip(mine, other):
        yield dot(left[...], near) + dot(right[...], far)


def mixer_project_body(seq, place, *refs):
    own, mine, other = refs[0], refs[1:seq], refs[seq : 2 * seq - 1]
    refs = refs[2 * seq - 1 :]
    (weight, routes), outs, (tails, held, sems) = refs[:2], refs[2 : seq + 2], refs[seq + 2 :]
    me = place[0]
    length = own.shape[0]
    for index, product in enumerate(project(place[1], own, mine, other, weight, 0, held, sems)):
        outs[index][HALO:, :] = product.astype(outs[index].dtype)
        tails[index] = product[length - HALO :, :]
    for mask in range(seq):
        shard = me ^ mask
        source = me ^ jnp.maximum(shard - 1, 0)
        before = jnp.where(shard > 0, tails[source], 0.0)
        row = lax.broadcasted_iota(jnp.int32, before.shape, 0)
        before = jnp.where(row < ROUTE_ROWS, routes[mask], before)
        outs[mask][:HALO, :] = before.astype(outs[mask].dtype)


def gate_project_body(seq, place, *refs):
    own, mine, other = refs[0], refs[1:seq], refs[seq : 2 * seq - 1]
    refs = refs[2 * seq - 1 :]
    (weight, own_tokens), outs, (held, sems) = refs[:2], refs[2 : seq + 2], refs[seq + 2 :]
    length, width = own.shape
    for index, product in enumerate(project(place[1], own, mine, other, weight, 1, held, sems)):
        outs[index][:length, :] = product.astype(outs[index].dtype)
        if index:
            start = pl.multiple_of((place[0] ^ index) * width, 128)
            rows = own_tokens[:, pl.ds(start, width)]
            spare = outs[index].shape[1] - width
            if spare:
                rows = jnp.concatenate([rows, jnp.zeros((rows.shape[0], spare), rows.dtype)], axis=1)
            outs[index][length:, :] = rows


def conv_body(seq, *refs):
    terms = refs[:seq]
    taps, bias, proj, activated, features = refs[seq:]
    total = terms[0][...]
    for term in terms[1:]:
        total = total + term[...].astype(F32)
    padded = total.astype(BF16).astype(F32)
    length = activated.shape[0]
    count = taps.shape[0]
    convolved = bias[...]
    for tap in range(count):
        start = HALO - count + 1 + tap
        convolved = convolved + taps[tap : tap + 1, :] * padded[start : start + length]
    rounded = silu(convolved).astype(BF16)
    activated[...] = rounded
    features[...] = lax.dot_general(
        rounded, proj[...], (((1,), (1,)), ((), ())), preferred_element_type=F32
    )


def scan_body(maps, low_rank, activated, step_weight, step_bias, rate, y, cumulated, final, steps, drive):
    length, groups, lanes = y.shape
    states = rate.shape[0]
    raw = dot(low_rank[...], step_weight[...]) + step_bias[...]
    step_size = jnp.maximum(raw, 0.0) + jnp.log1p(jnp.exp(-jnp.abs(raw)))
    driven = step_size * activated[...].astype(F32)
    for group in range(groups):
        part = slice(group * lanes, (group + 1) * lanes)
        steps[:, group, :] = step_size[:, part]
        drive[:, group, :] = driven[:, part]
    rates = [rate[n] for n in range(states)]

    def advance(t, carry):
        state, running = carry
        step, push = steps[t], drive[t]
        running = running + step
        fresh = []
        out = jnp.zeros_like(step)
        for n in range(states):
            value = jnp.exp2(step * rates[n]) * state[n] + push * maps[t, n]
            out = out + value * maps[t, states + n]
            fresh.append(value)
        y[t] = out
        cumulated[t] = running
        return tuple(fresh), running

    zero = jnp.zeros((groups, lanes), F32)
    state, running = lax.fori_loop(0, length, advance, ((zero,) * states, zero), unroll=4)
    for n in range(states):
        final[n] = state[n].astype(BF16)
    upper = running.astype(BF16)
    final[states] = upper
    final[states + 1] = (running - upper.astype(F32)).astype(BF16)


def gated_body(seq, own_rows, place, maps, *refs):
    arrived = refs[: seq - 1]
    y, cumulated, rate, activated, skip_gain = refs[seq - 1 : seq + 4]
    gates = refs[seq + 4 : 2 * seq + 4]
    gated, scanned, result = refs[2 * seq + 4 :]
    length, groups, lanes = y.shape
    states = rate.shape[0]
    me, expert = place[0], place[2]
    zero = jnp.zeros((groups, lanes), F32)
    incoming = [zero] * states
    sums = [block[states].astype(F32) + block[states + 1].astype(F32) for block in arrived]
    for mask in range(1, seq):
        shard = me ^ mask
        between = zero
        for other in range(1, seq):
            middle = me ^ other
            inside = (shard < middle) & (middle < me)
            between = between + jnp.where(inside, sums[other - 1], 0.0)
        for n in range(states):
            term = jnp.exp2(rate[n] * between) * arrived[mask - 1][n].astype(F32)
            incoming[n] = incoming[n] + jnp.where(shard < me, term, 0.0)
    rates = [rate[n] for n in range(states)]

    def correct(t, carry):
        steps = cumulated[t]
        out = y[t]
        for n in range(states):
            out = out + (jnp.exp2(steps * rates[n]) * incoming[n]) * maps[t, states + n]
        scanned[t] = out
        return carry

    lax.fori_loop(0, length, correct, 0, unroll=4)
    for group in range(groups):
        part = slice(group * lanes, (group + 1) * lanes)
        gate = gates[0][:, part]
        for term in gates[1:]:
            gate = gate + term[:length, part].astype(F32)
        gate = gate.astype(BF16).astype(F32)
        drive = activated[:, part].astype(F32)
        result[:, part] = (scanned[:, group, :] + skip_gain[:, part] * drive) * silu(gate)
    blocks = length // own_rows
    moved = [
        result[pl.ds(pl.multiple_of((expert ^ k) * own_rows, own_rows), own_rows), :]
        for k in range(blocks)
    ]
    gated[...] = jnp.concatenate(moved, axis=0).astype(BF16)


def out_project_body(seq, own_rows, *refs):
    blocks = refs[:seq]
    weight, keep, send = refs[seq:]
    for shard in range(seq):
        product = dot(blocks[shard][...], weight[...])
        for owner in range(product.shape[0] // own_rows):
            rows = product[owner * own_rows : (owner + 1) * own_rows]
            place = (owner // 2, pl.ds(shard * own_rows, own_rows))
            if owner % 2 == 0:
                keep[place[0], place[1], :] = rows
            else:
                send[place[0], place[1], :] = rows.astype(BF16)


def core_sum_body(keep, arrived, own, *sends):
    own[...] = keep[0] + arrived[0].astype(F32)
    for w in range(1, keep.shape[0]):
        sends[w - 1][...] = (keep[w] + arrived[w].astype(F32)).astype(BF16)


def tables_body(seq, own_rows, most_slots, place, routes, *refs):
    terms, outs = refs[: seq - 1], refs[seq - 1 :]
    choose, first, second, named = outs
    slots, window = choose.shape
    near = routes[:8, :window]
    for term in terms:
        near = near + term[:16, :window].astype(F32)[:8]
    row = lax.broadcasted_iota(jnp.int32, (slots, window), 0)
    column = lax.broadcasted_iota(jnp.int32, (slots, window), 1)
    wanted = (place[2] ^ (row // (seq * most_slots))).astype(F32)
    shard = (row // most_slots) % seq
    hits = [jnp.where(near[i : i + 1, :] == wanted, 1.0, 0.0) for i in range(2)]
    source = lax.broadcasted_iota(jnp.int32, (window, window), 0)
    target = lax.broadcasted_iota(jnp.int32, (window, window), 1)
    earlier = (source // own_rows == target // own_rows) & (source < target)
    before = dot((hits[0] + hits[1]).astype(BF16), jnp.where(earlier, 1.0, 0.0).astype(BF16))
    numbered = jnp.where(before == (row % most_slots).astype(F32), 1.0, 0.0)
    here = jnp.where(shard == (place[0] ^ (column // own_rows)), numbered, 0.0)
    choose[...] = (here * (hits[0] + hits[1])).astype(BF16)
    first[...] = (numbered * hits[0])[:, :own_rows]
    second[...] = (numbered * hits[1])[:, :own_rows]
    same = jnp.where(source == target, 1.0, 0.0).astype(BF16)
    columns = lax.dot_general(
        same, near.astype(BF16), (((1,), (1,)), ((), ())), preferred_element_type=F32
    )
    named[...] = columns[:own_rows]


def reordered(table, outer, inner, count):
    rows = table.shape[0]
    row = lax.broadcasted_iota(jnp.int32, (rows, rows), 0)
    column = lax.broadcasted_iota(jnp.int32, (rows, rows), 1)
    big, small, number = row // (inner * count), (row // count) % inner, row % count
    choice = jnp.where(column == small * (outer * count) + big * count + number, 1.0, 0.0).astype(BF16)
    return dot(choice, table).astype(BF16)


def hidden_body(chips, seq, place, own, *refs):
    terms, refs = refs[: chips - 1], refs[chips - 1 :]
    own_tokens, refs = refs[0], refs[1:]
    payloads, refs = refs[: seq - 1], refs[seq - 1 :]
    choose, hidden = refs[0], refs[1 : 1 + seq]
    outs = refs[1 + seq :]
    total = own[...]
    for term in terms:
        total = total + term[...].astype(F32)
    width = own.shape[1]
    rows = own_tokens.shape[0]
    start = pl.multiple_of(place[0] * width, 128)
    residual = [own_tokens[:, pl.ds(start, width)].astype(F32)]
    for payload in payloads:
        residual.append(payload[payload.shape[0] - rows :, :width].astype(F32))
    rounded = (jnp.concatenate(residual, axis=0) + total).astype(BF16)
    for d, out in enumerate(hidden):
        out[...] = rounded[d * rows : (d + 1) * rows]
    slots = dot(choose[...], rounded).astype(BF16)
    rows = slots.shape[0] // chips
    for w in range(chips):
        outs[w][...] = slots[w * rows : (w + 1) * rows]


def start_copies(jobs, place, sources, outs, sems):
    copies = []
    for index, (source, mask, axis) in enumerate(jobs):
        size = outs[index].shape[axis]
        if axis:
            where = (0, slice(None), pl.ds(mask * size, size))
        else:
            where = (0, pl.ds(pl.multiple_of((place[0] ^ mask) * size, 16), size))
        copies.append(pltpu.make_async_copy(sources[source].at[where], outs[index], sems.at[index]))
    for copy in copies:
        copy.start()
    return copies


def in_hbm(sources):
    return [pltpu.with_memory_space_constraint(source, pltpu.HBM) for source in sources]


def fetched_shapes(jobs, sources, width):
    blocks = []
    for source, _, axis in jobs:
        rows, columns = sources[source].shape[1:]
        blocks.append(pltpu.VMEM((rows, width) if axis else (width, columns), BF16))
    return blocks


def fetch_body(jobs, count, place, *refs):
    sources, outs, sems = refs[:count], refs[count:-1], refs[-1]
    for copy in start_copies(jobs, place, sources, outs, sems):
        copy.wait()


def fetch(place, jobs, width, sources, deps):
    return kernel_call(
        functools.partial(fetch_body, jobs, len(sources)),
        fetched_shapes(jobs, sources, width),
        [SMEM] + [pl.BlockSpec(memory_space=pltpu.HBM)] * len(sources),
        [pltpu.SemaphoreType.DMA((len(jobs),))],
        moved=2 * len(jobs) * width * sources[0].shape[2],
        deps=deps,
    )(place, *in_hbm(sources))


def expert_body(mask, first, last, model_width, jobs, count, parts, place, *refs):
    pieces, (gain, gate, up), refs = refs[:parts], refs[parts : parts + 3], refs[parts + 3 :]
    before, refs = ([], refs) if first else (refs[:3], refs[3:])
    sources, refs = refs[:count], refs[count:]
    outs, refs = (refs[:1], refs[1:]) if last else (refs[:3], refs[3:])
    copies = start_copies(jobs, place, sources, refs[:-1], refs[-1]) if jobs else []
    width = pieces[0].shape[1]
    values = jnp.concatenate([piece[...].astype(F32) for piece in pieces], axis=0)
    square = jnp.sum(values * values, axis=-1, keepdims=True)
    if not first:
        square = square + before[2][:, 0:1]
    start = pl.multiple_of((place[0] ^ mask) * width, 128)
    rows = (values * gain[:, pl.ds(start, width)]).astype(BF16)
    inverse = lax.rsqrt(square / model_width + EPSILON)
    if not last:
        outs[2][...] = jnp.broadcast_to(square, outs[2].shape)
    hidden_units = gate.shape[1]
    tile = tile_of(hidden_units, 512)
    for step in range(hidden_units // tile):
        part = slice(step * tile, (step + 1) * tile)
        gate_act = dot(rows, gate[:, part])
        up_act = dot(rows, up[:, part])
        if not first:
            gate_act = gate_act + before[0][:, part]
            up_act = up_act + before[1][:, part]
        if last:
            outs[0][:, part] = (silu(gate_act * inverse) * (up_act * inverse)).astype(BF16)
        else:
            outs[0][:, part] = gate_act
            outs[1][:, part] = up_act
    for copy in copies:
        copy.wait()


def expert_chunk(mask, first, last, place, piece, gain, gate, up, before, jobs, sources, deps):
    slots, width = sum(part.shape[0] for part in piece), piece[0].shape[1]
    model_width, hidden_units = gain.shape[1], gate.shape[1]
    total = shape((slots, hidden_units), F32)
    outs = [total, total, shape((slots, 128), F32)]
    if last:
        outs = [shape((slots, hidden_units), BF16)]
    sources = sources if jobs else []
    far = pl.BlockSpec(memory_space=pltpu.HBM)
    results = kernel_call(
        functools.partial(expert_body, mask, first, last, model_width, jobs, len(sources), len(piece)),
        outs + fetched_shapes(jobs, sources, width),
        [SMEM] + [VMEM] * (3 + len(piece) + len(before)) + [far] * len(sources),
        [pltpu.SemaphoreType.DMA((len(jobs),))] if jobs else [],
        flops=4 * slots * width * hidden_units,
        moved=4 * width * hidden_units,
        limit=12,
        deps=deps,
    )(place, *piece, gain, gate, up, *before, *in_hbm(sources))
    return results[: len(outs)], results[len(outs) :]


def down_body(seq, place, hidden, *refs):
    downs, outs, product = refs[:seq], refs[seq:-1], refs[-1]
    width = downs[0].shape[1]
    tile = tile_of(width, 512)
    for block, down in enumerate(downs):
        for step in range(width // tile):
            part = slice(step * tile, (step + 1) * tile)
            to = slice(block * width + step * tile, block * width + (step + 1) * tile)
            product[:, to] = dot(hidden[...], down[:, part]).astype(BF16)
    for mask, out in enumerate(outs):
        rows = out.shape[0]
        out[...] = product[pl.ds(pl.multiple_of((place[0] ^ mask) * rows, 16), rows), :]


def expert_sum_body(seq, groups, most_slots, *refs):
    terms, outs = refs[:seq], refs[seq:]
    total = terms[0][...].astype(F32)
    for term in terms[1:]:
        total = total + term[...].astype(F32)
    rounded = total.astype(BF16)
    width = outs[0].shape[1]
    pieces = jnp.concatenate([rounded[:, q * width : (q + 1) * width] for q in range(seq)], axis=0)
    pieces = reordered(pieces, groups, seq, most_slots)
    rows = pieces.shape[0] // len(outs)
    for w, out in enumerate(outs):
        out[...] = pieces[w * rows : (w + 1) * rows]


def shares_body(seq, place, gain, router, named, *refs):
    pieces, rows, shares = refs[:seq], refs[seq], refs[seq + 1]
    width = pieces[0].shape[1]
    for mask, piece in enumerate(pieces):
        start = pl.multiple_of((place[0] ^ mask) * width, 128)
        rows[:, pl.ds(start, width)] = piece[...].astype(F32)
    values = rows[...]
    inverse = lax.rsqrt(jnp.mean(values * values, axis=-1, keepdims=True) + EPSILON)
    moe_in = (values * inverse * gain[...]).astype(BF16)
    logits = lax.dot_general(
        moe_in, router[...], (((1,), (1,)), ((), ())), preferred_element_type=F32
    )
    lane = lax.broadcasted_iota(jnp.int32, logits.shape, 1).astype(F32)
    picked = [
        jnp.sum(jnp.where(lane == named[:, i : i + 1], logits, 0.0), axis=-1, keepdims=True)
        for i in range(2)
    ]
    first_share = 1.0 / (1.0 + jnp.exp(picked[1] - picked[0]))
    shares[...] = jnp.broadcast_to(first_share, shares.shape)


def halves_body(*refs):
    blocks, out = refs[:-1], refs[-1]
    for w, block in enumerate(blocks):
        out[w] = block[out.shape[1] :, :]


def second_halves(blocks, deps=()):
    rows, width = blocks[0].shape
    return kernel_call(
        halves_body,
        shape((len(blocks), rows // 2, width), BF16),
        [VMEM] * len(blocks),
        moved=2 * len(blocks) * rows * width,
        deps=deps,
    )(*blocks)


def rows_body(chips, seq, groups, most_slots, *refs):
    direct, crossed, out = refs[:chips], refs[chips], refs[chips + 1]
    half = crossed.shape[1]
    table = jnp.concatenate(
        [block for w in range(chips) for block in (direct[w][:half, :], crossed[w])], axis=0
    )
    out[...] = reordered(table, seq, groups, most_slots)


def combine_body(chips, seq, most_slots, *refs):
    direct = refs[:chips]
    crossed, first, second, rows, shares, out = refs[chips:]
    half = crossed.shape[1]
    table = jnp.concatenate(
        [block for w in range(chips) for block in (direct[w][:half, :], crossed[w])], axis=0
    )
    width = table.shape[1]
    row = lax.broadcasted_iota(jnp.int32, first.shape, 0)
    piece = (row // most_slots) % seq
    first_share = shares[:, 0:1]
    for q in range(seq):

        def rows_of(choice):
            chosen = jnp.where(piece == q, choice[...], 0.0).astype(BF16)
            return lax.dot_general(
                chosen, table, (((0,), (0,)), ((), ())), preferred_element_type=F32
            )

        part = slice(q * width, (q + 1) * width)
        sent = first_share * rows_of(first) + (1.0 - first_share) * rows_of(second)
        out[:, part] = (rows[:, part] + sent).astype(BF16)


def tile_of(total, most):
    for width in range(most, 0, -128):
        if total % width == 0:
            return width
    return total


def local(
    tokens,
    norm_gain,
    in_weight,
    conv_weight,
    conv_bias,
    proj_weight,
    step_weight,
    step_bias,
    decay_log,
    skip_gain,
    out_weight,
    moe_gain,
    router_weight,
    routes,
    gate_weight,
    up_weight,
    down_weight,
):
    seq, groups = lax.axis_size("seq"), lax.axis_size("expert")
    chips = groups // 2
    me, expert = lax.axis_index("seq"), lax.axis_index("expert")
    core = expert % 2
    place = jnp.stack([me, core, expert]).astype(jnp.int32)
    masks = range(1, seq)
    length, model_width = tokens.shape
    width = model_width // seq
    channels = in_weight.shape[2]
    rank_width = step_weight.shape[0]
    state_width = decay_log.shape[1]
    lanes = 128
    tiles = channels // lanes
    own_rows = routes.shape[0]
    experts = router_weight.shape[1]
    most_slots = max(2, 3 * own_rows // experts)
    window = seq * own_rows

    x_own, *x_send = kernel_call(
        functools.partial(norm_body, seq),
        [shape((length, width), BF16)] + [shape((length, width // 2), BF16)] * (seq - 1),
        [SMEM, VMEM, VMEM],
        flops=8 * length * model_width,
        moved=4 * length * model_width,
        limit=24,
    )(place, tokens, norm_gain[None])
    x_mine = [partner(block, "seq", mask) for mask, block in zip(masks, x_send)]
    weight = in_hbm([in_weight.reshape(width, 2 * channels)])[0]
    x_passed = kernel_call(
        pass_body,
        [shape((length, width // 2), BF16)] * (seq - 1),
        [VMEM] * (seq - 1),
        deps=[weight],
    )(*x_mine)
    x_other = [partner(block, "expert", 1) for block in x_passed]
    x = [x_own, *x_mine, *x_other]
    lane_routes = jnp.transpose(routes).astype(F32)
    spread_routes = jnp.stack(
        [
            jnp.pad(lane_routes, ((0, HALO - ROUTE_ROWS), (d * own_rows, channels - (d + 1) * own_rows)))
            for d in range(seq)
        ]
    )
    in_specs = [SMEM] + [VMEM] * (2 * seq - 1) + [pl.BlockSpec(memory_space=pltpu.HBM), VMEM]
    scratch = [pltpu.VMEM((width, channels), BF16), pltpu.SemaphoreType.DMA((4,))]
    cost = dict(flops=2 * seq * length * width * channels, moved=2 * width * channels, limit=24)
    mixer_own, *mixer_send = kernel_call(
        functools.partial(mixer_project_body, seq),
        [shape((HALO + length, channels), F32)] + [shape((HALO + length, channels), BF16)] * (seq - 1),
        in_specs,
        [pltpu.VMEM((seq, HALO, channels), F32)] + scratch,
        **cost,
    )(place, *x, weight, spread_routes)
    mixer_terms = [partner(block, "seq", mask) for mask, block in zip(masks, mixer_send)]
    assert width <= channels and window <= channels
    own_tokens = lax.dynamic_slice_in_dim(tokens, expert * own_rows, own_rows, 0)
    side_own, *side_send = kernel_call(
        functools.partial(gate_project_body, seq),
        [shape((length, channels), F32)] + [shape((length + own_rows, channels), BF16)] * (seq - 1),
        in_specs,
        scratch,
        deps=[mixer_terms[seq // 2 - 1]],
        **cost,
    )(place, *x, weight, own_tokens)

    side_terms = [partner(block, "seq", mask) for mask, block in zip(masks, side_send)]
    activated, features = kernel_call(
        functools.partial(conv_body, seq),
        [shape((length, channels), BF16), shape((length, proj_weight.shape[1]), F32)],
        [VMEM] * (seq + 3),
        limit=16,
        deps=[side_own],
    )(mixer_own, *mixer_terms, conv_weight, conv_bias[None], jnp.transpose(proj_weight))
    features = features + partner(features, "expert", 1)
    sent = features.astype(BF16)
    features_came = [partner(sent, "expert", 2 * w) for w in range(1, chips)]
    for term in features_came:
        features = features + term.astype(F32)
    low_rank, maps = features[:, :rank_width].astype(BF16), features[:, rank_width:]

    rate = -LOG2_E * jnp.exp(jnp.transpose(decay_log)).reshape(state_width, tiles, lanes)
    tiled = shape((length, tiles, lanes), F32)
    y, cumulated, final = kernel_call(
        scan_body,
        [tiled, tiled, shape((state_width + 2, tiles, lanes), BF16)],
        [SMEM] + [VMEM] * 5,
        [pltpu.VMEM(tiled.shape, F32)] * 2,
        limit=24,
    )(maps, low_rank, activated, step_weight, step_bias[None], rate)
    arrived = [partner(final, "seq", mask) for mask in masks]
    gated = kernel_call(
        functools.partial(gated_body, seq, own_rows),
        shape((length, channels), BF16),
        [SMEM, SMEM] + [VMEM] * (2 * seq + 4),
        [pltpu.VMEM(tiled.shape, F32), pltpu.VMEM((length, channels), F32)],
        limit=24,
    )(place, maps, *arrived, y, cumulated, rate, activated, skip_gain[None], side_own, *side_terms)

    blocks = [gated] + [partner(gated, "seq", mask) for mask in masks]

    slots = groups * seq * most_slots
    per_chip = slots // chips
    per_group = slots // groups
    choose, first, second, named = kernel_call(
        functools.partial(tables_body, seq, own_rows, most_slots),
        [shape((slots, window), BF16)] + [shape((slots, own_rows), F32)] * 2 + [shape((own_rows, 8), F32)],
        [SMEM, VMEM] + [VMEM] * (seq - 1),
        flops=2 * slots * window * window,
        moved=8 * slots * window,
    )(place, spread_routes[0], *mixer_terms)

    keep, send = kernel_call(
        functools.partial(out_project_body, seq, own_rows),
        [shape((chips, window, width), F32), shape((chips, window, width), BF16)],
        [VMEM] * (seq + 1),
        flops=2 * seq * length * channels * width,
        moved=2 * channels * width + 8 * seq * length * width,
        limit=16,
    )(*blocks, out_weight)
    crossing = partner(send, "expert", 1)
    own_sum, *chip_sends = kernel_call(
        core_sum_body,
        [shape((window, width), F32)] + [shape((window, width), BF16)] * (chips - 1),
        [VMEM] * 2,
        flops=chips * window * width,
        moved=10 * chips * window * width,
    )(keep, crossing)
    chip_terms = [partner(block, "expert", 2 * w) for w, block in zip(range(1, chips), chip_sends)]

    sources = [gate_weight, up_weight, down_weight]
    both = lambda mask: [(0, mask, 0), (1, mask, 0)]
    early = min(seq, 3)
    current = list(fetch(place, sum([both(mask) for mask in range(early)], []), width, sources[:2], [own_sum]))
    near_hidden = kernel_call(
        functools.partial(hidden_body, chips, seq),
        [shape((own_rows, width), BF16)] * seq + [shape((per_chip, width), BF16)] * chips,
        [SMEM] + [VMEM] * (chips + seq + 1),
        flops=2 * slots * window * width,
        moved=10 * window * width,
        deps=current,
    )(place, own_sum, *chip_terms, own_tokens, *side_terms, choose)
    near_hidden, outgoing = near_hidden[:seq], near_hidden[seq:]

    came = [outgoing[0]] + [
        partner(block, "expert", 2 * w) for w, block in zip(range(1, chips), outgoing[1:])
    ]
    whole = [near_hidden[0]] + [partner(near_hidden[mask], "seq", mask) for mask in masks]
    more = list(fetch(place, both(early), width, sources[:2], [outgoing[0]])) if early < seq else []
    crossed = partner(second_halves(came, whole[1:] + more), "expert", 1)
    rows = kernel_call(
        functools.partial(rows_body, chips, seq, groups, most_slots),
        shape((slots, width), BF16),
        [VMEM] * (chips + 1),
        moved=4 * slots * width,
    )(*came, crossed)
    if seq == 4:
        pieces = [rows, partner(rows, "seq", 1), partner(rows, "seq", 2)]
        half = slots // 2
        pieces = [[piece] for piece in pieces] + [
            [partner(pieces[1][:half], "seq", 2), partner(pieces[2][half:], "seq", 1)]
        ]
    else:
        pieces = [[rows]] + [[partner(rows, "seq", mask)] for mask in masks]

    before, waiting, downs = [], current + more, []
    for mask in range(seq):
        jobs = both(mask + 4) if mask + 4 < seq else []
        if mask == max(0, seq - 4):
            jobs = [(2, block, 1) for block in range(seq)]
        before, came_in = expert_chunk(
            mask, mask == 0, mask == seq - 1, place, pieces[mask], moe_gain[None], *waiting[:2], before, jobs, sources, downs
        )
        waiting = waiting[2:]
        if mask == max(0, seq - 4):
            downs = list(came_in)
        else:
            waiting = waiting + list(came_in)
    hidden = before[0]
    back = groups * most_slots
    sums = kernel_call(
        functools.partial(down_body, seq),
        [shape((back, model_width), BF16)] * seq,
        [SMEM] + [VMEM] * (seq + 1),
        [pltpu.VMEM((slots, model_width), BF16)],
        flops=2 * slots * model_width * gate_weight.shape[2],
        moved=2 * model_width * gate_weight.shape[2],
        limit=16,
    )(place, hidden, *downs)
    terms = [sums[0]] + [partner(sums[mask], "seq", mask) for mask in masks]

    own_hidden, shares = kernel_call(
        functools.partial(shares_body, seq),
        [shape((own_rows, model_width), F32), shape((own_rows, lanes), F32)],
        [SMEM] + [VMEM] * (seq + 3),
        flops=2 * own_rows * model_width * lanes,
        moved=16 * own_rows * model_width,
        deps=[sums[0]],
    )(place, moe_gain[None], jnp.transpose(router_weight), named, *whole)
    answers = kernel_call(
        functools.partial(expert_sum_body, seq, groups, most_slots),
        [shape((per_chip, width), BF16)] * chips,
        [VMEM] * seq,
        flops=seq * slots * width,
        moved=10 * slots * width,
        deps=[shares],
    )(*terms)
    answers = [answers[0]] + [
        partner(block, "expert", 2 * w) for w, block in zip(range(1, chips), answers[1:])
    ]
    crossed_back = partner(second_halves(answers), "expert", 1)
    return kernel_call(
        functools.partial(combine_body, chips, seq, most_slots),
        shape((own_rows, model_width), BF16),
        [VMEM] * (chips + 5),
        flops=4 * slots * own_rows * model_width,
        moved=8 * slots * width,
    )(*answers, crossed_back, first, second, own_hidden, shares)


def solution(mesh):
    in_specs = (
        P("seq", None),
        P(),
        P("seq", None, "expert"),
        P(None, "expert"),
        P("expert"),
        P("expert", None),
        P(None, "expert"),
        P("expert"),
        P("expert", None),
        P("expert"),
        P("expert", "seq"),
        P(),
        P(),
        P(("seq", "expert"), None),
        P("expert", None, "seq"),
        P("expert", None, "seq"),
        P("expert", "seq", None),
    )
    out_specs = P(("seq", "expert"), None)
    return jax.shard_map(local, mesh=mesh, in_specs=in_specs, out_specs=out_specs, check_vma=False)
```

```python
import functools

import jax
import jax.numpy as jnp
from jax import lax
from jax.experimental import pallas as pl
from jax.experimental.pallas import tpu as pltpu
from jax.sharding import PartitionSpec as P

EPSILON = 1e-06
HALO = 16
ROUTE_ROWS = 2
LOG2_E = 1.4426950408889634
MIB = 1 << 20
BF16 = jnp.bfloat16
F32 = jnp.float32

VMEM = pl.BlockSpec(memory_space=pltpu.VMEM)
SMEM = pl.BlockSpec(memory_space=pltpu.SMEM)


def partner(block, axis, mask):
    size = lax.axis_size(axis)
    return lax.ppermute(block, axis, [(i, i ^ mask) for i in range(size)])


def later_partner(block, axis, mask):
    size = lax.axis_size(axis)
    return lax.ppermute(block, axis, [(i, i ^ mask) for i in range(size) if i < i ^ mask])


def after(values, *done):
    flat, tree = jax.tree.flatten(values)
    held = lax.optimization_barrier((*flat, *done))
    return jax.tree.unflatten(tree, held[: len(flat)])


def shape(dims, dtype):
    return jax.ShapeDtypeStruct(tuple(dims), dtype)


def kernel_call(body, outs, in_specs, scratch=(), flops=0, moved=0, limit=8, deps=()):
    deps = list(deps)
    count = len(in_specs)

    def with_deps(*refs):
        body(*refs[:count], *refs[count + len(deps) :])

    call = pl.pallas_call(
        with_deps,
        out_shape=outs,
        in_specs=list(in_specs) + [pl.BlockSpec(memory_space=pl.ANY)] * len(deps),
        out_specs=jax.tree.map(lambda _: VMEM, outs),
        scratch_shapes=list(scratch),
        compiler_params=pltpu.CompilerParams(vmem_limit_bytes=limit * MIB),
        cost_estimate=pl.CostEstimate(flops=flops, bytes_accessed=moved, transcendentals=0),
    )
    return lambda *operands: call(*operands, *deps)


def dot(left, right):
    return jnp.dot(left, right, preferred_element_type=F32)


def silu(v):
    return v / (1.0 + jnp.exp(-v))


def norm_body(seq, place, tokens, gain, own, *sends):
    values = tokens[...].astype(F32)
    inverse = lax.rsqrt(jnp.mean(values * values, axis=-1, keepdims=True) + EPSILON)
    own_width = own.shape[1]
    half = own_width // 2
    me, core = place[0], place[1]

    def columns(start, width):
        part = pl.ds(pl.multiple_of(start, 128), width)
        return (tokens[:, part].astype(F32) * inverse * gain[:, part]).astype(BF16)

    own[...] = columns(me * own_width, own_width)
    for mask in range(1, seq):
        sends[mask - 1][...] = columns((me ^ mask) * own_width + core * half, half)


def pass_body(*refs):
    for block, out in zip(refs[: len(refs) // 2], refs[len(refs) // 2 :]):
        out[...] = block[...]


def project(core, own, mine, other, source, branch, weight, sems):
    depth, channels = weight.shape
    parts = sems.shape[0]
    copies = []
    for i in range(parts):
        rows = pl.ds(i * (depth // parts), depth // parts)
        part = source.at[rows, pl.ds(branch * channels, channels)]
        copies.append((rows, pltpu.make_async_copy(part, weight.at[rows], sems.at[i])))
    for _, copy in copies:
        copy.start()
    first = 0.0
    for rows, copy in copies:
        copy.wait()
        first = first + dot(own[:, rows], weight[rows, :])
    yield first
    half = depth // 2
    near = weight[pl.ds(pl.multiple_of(core * half, half), half), :]
    far = weight[pl.ds(pl.multiple_of((1 - core) * half, half), half), :]
    for left, right in zip(mine, other):
        yield dot(left[...], near) + dot(right[...], far)


def mixer_project_body(seq, cuts, place, *refs):
    own, mine, other = refs[0], refs[1:seq], refs[seq : 2 * seq - 1]
    refs = refs[2 * seq - 1 :]
    (weight, routes), outs, (tails, held, sems) = refs[:2], refs[2:-3], refs[-3:]
    me = place[0]
    length = own.shape[0]

    def store(mask, rows, values):
        for (number, index), out in zip(cuts, outs):
            if number == mask:
                columns = out.shape[1]
                out[rows, :] = values[:, index * columns : (index + 1) * columns].astype(out.dtype)

    for mask, product in enumerate(project(place[1], own, mine, other, weight, 0, held, sems)):
        store(mask, slice(HALO, HALO + length), product)
        tails[mask] = product[length - HALO :, :]
    for mask in range(seq):
        shard = me ^ mask
        source = me ^ jnp.maximum(shard - 1, 0)
        before = jnp.where(shard > 0, tails[source], 0.0)
        row = lax.broadcasted_iota(jnp.int32, before.shape, 0)
        store(mask, slice(0, HALO), jnp.where(row < ROUTE_ROWS, routes[mask], before))


def gate_project_body(seq, place, *refs):
    own, mine, other = refs[0], refs[1:seq], refs[seq : 2 * seq - 1]
    refs = refs[2 * seq - 1 :]
    (weight, own_tokens), outs, (held, sems) = refs[:2], refs[2 : seq + 2], refs[seq + 2 :]
    length, width = own.shape
    for index, product in enumerate(project(place[1], own, mine, other, weight, 1, held, sems)):
        outs[index][:length, :] = product.astype(outs[index].dtype)
        if index:
            start = pl.multiple_of((place[0] ^ index) * width, 128)
            rows = own_tokens[:, pl.ds(start, width)]
            spare = outs[index].shape[1] - width
            if spare:
                rows = jnp.concatenate([rows, jnp.zeros((rows.shape[0], spare), rows.dtype)], axis=1)
            outs[index][length:, :] = rows


def conv_body(places, *refs):
    own, terms = refs[0], refs[1 : 1 + len(places)]
    taps, bias, proj, activated, features = refs[1 + len(places) :]
    columns = [own[:, i * terms[0].shape[1] : (i + 1) * terms[0].shape[1]] for i in range(max(places) + 1)]
    for index, term in zip(places, terms):
        columns[index] = columns[index] + term[...].astype(F32)
    total = jnp.concatenate(columns, axis=1)
    padded = total.astype(BF16).astype(F32)
    length = activated.shape[0]
    count = taps.shape[0]
    convolved = bias[...]
    for tap in range(count):
        start = HALO - count + 1 + tap
        convolved = convolved + taps[tap : tap + 1, :] * padded[start : start + length]
    rounded = silu(convolved).astype(BF16)
    activated[...] = rounded
    rank = features.shape[1]
    states = (proj.shape[0] - rank) // 2

    def both_last(one, other):
        return lax.dot_general(one, other, (((1,), (1,)), ((), ())), preferred_element_type=F32)

    features[:length, :] = both_last(rounded, proj[:rank, :])
    maps = both_last(proj[rank:, :], rounded)
    below = jnp.zeros((features.shape[0] - length, rank), F32)
    features[length:, :] = below
    for i in range(2):
        features[length:, i * length : (i + 1) * length] = maps[i * states : (i + 1) * states]


def scan_body(maps, low_rank, activated, step_weight, step_bias, rate, y, cumulated, final, steps, drive):
    length, groups, lanes = y.shape
    states = rate.shape[0]
    raw = dot(low_rank[...], step_weight[...]) + step_bias[...]
    step_size = jnp.maximum(raw, 0.0) + jnp.log1p(jnp.exp(-jnp.abs(raw)))
    driven = step_size * activated[...].astype(F32)
    for group in range(groups):
        part = slice(group * lanes, (group + 1) * lanes)
        steps[:, group, :] = step_size[:, part]
        drive[:, group, :] = driven[:, part]
    rates = [rate[n] for n in range(states)]

    def advance(t, carry):
        state, running = carry
        step, push = steps[t], drive[t]
        running = running + step
        fresh = []
        out = jnp.zeros_like(step)
        for n in range(states):
            value = jnp.exp2(step * rates[n]) * state[n] + push * maps[n, t]
            out = out + value * maps[n, length + t]
            fresh.append(value)
        y[t] = out
        cumulated[t] = running
        return tuple(fresh), running

    zero = jnp.zeros((groups, lanes), F32)
    state, running = lax.fori_loop(0, length, advance, ((zero,) * states, zero), unroll=4)
    for n in range(states):
        final[n] = state[n].astype(BF16)
    upper = running.astype(BF16)
    final[states] = upper
    final[states + 1] = (running - upper.astype(F32)).astype(BF16)


def gated_body(seq, own_rows, place, maps, *refs):
    arrived = refs[: seq - 1]
    y, cumulated, rate, activated, skip_gain = refs[seq - 1 : seq + 4]
    gates = refs[seq + 4 : 2 * seq + 4]
    gated, scanned, result = refs[2 * seq + 4 :]
    length, groups, lanes = y.shape
    states = rate.shape[0]
    me, expert = place[0], place[2]
    zero = jnp.zeros((groups, lanes), F32)
    incoming = [zero] * states
    sums = [block[states].astype(F32) + block[states + 1].astype(F32) for block in arrived]
    for mask in range(1, seq):
        shard = me ^ mask
        between = zero
        for other in range(1, seq):
            middle = me ^ other
            inside = (shard < middle) & (middle < me)
            between = between + jnp.where(inside, sums[other - 1], 0.0)
        for n in range(states):
            term = jnp.exp2(rate[n] * between) * arrived[mask - 1][n].astype(F32)
            incoming[n] = incoming[n] + jnp.where(shard < me, term, 0.0)
    rates = [rate[n] for n in range(states)]

    def correct(t, carry):
        steps = cumulated[t]
        out = y[t]
        for n in range(states):
            out = out + (jnp.exp2(steps * rates[n]) * incoming[n]) * maps[n, length + t]
        scanned[t] = out
        return carry

    lax.fori_loop(0, length, correct, 0, unroll=4)
    for group in range(groups):
        part = slice(group * lanes, (group + 1) * lanes)
        gate = gates[0][:, part]
        for term in gates[1:]:
            gate = gate + term[:length, part].astype(F32)
        gate = gate.astype(BF16).astype(F32)
        drive = activated[:, part].astype(F32)
        result[:, part] = (scanned[:, group, :] + skip_gain[:, part] * drive) * silu(gate)
    blocks = length // own_rows
    moved = [
        result[pl.ds(pl.multiple_of((expert ^ k) * own_rows, own_rows), own_rows), :]
        for k in range(blocks)
    ]
    gated[...] = jnp.concatenate(moved, axis=0).astype(BF16)


def out_project_body(seq, own_rows, *refs):
    blocks = refs[:seq]
    weight, keep, send = refs[seq:]
    for shard in range(seq):
        product = dot(blocks[shard][...], weight[...])
        for owner in range(product.shape[0] // own_rows):
            rows = product[owner * own_rows : (owner + 1) * own_rows]
            place = (owner // 2, pl.ds(shard * own_rows, own_rows))
            if owner % 2 == 0:
                keep[place[0], place[1], :] = rows
            else:
                send[place[0], place[1], :] = rows.astype(BF16)


def core_sum_body(keep, arrived, own, *sends):
    own[...] = keep[0] + arrived[0].astype(F32)
    for w in range(1, keep.shape[0]):
        sends[w - 1][...] = (keep[w] + arrived[w].astype(F32)).astype(BF16)


def tables_body(seq, own_rows, most_slots, place, routes, *refs):
    terms, (choose, first, second, named) = refs[:-4], refs[-4:]
    slots, window = choose.shape
    near = routes[:8, :window]
    for term in terms:
        near = near + term[:16, :window].astype(F32)[:8]
    row = lax.broadcasted_iota(jnp.int32, (slots, window), 0)
    column = lax.broadcasted_iota(jnp.int32, (slots, window), 1)
    wanted = (place[2] ^ (row // (seq * most_slots))).astype(F32)
    shard = (row // most_slots) % seq
    hits = [jnp.where(near[i : i + 1, :] == wanted, 1.0, 0.0) for i in range(2)]
    source = lax.broadcasted_iota(jnp.int32, (window, window), 0)
    target = lax.broadcasted_iota(jnp.int32, (window, window), 1)
    earlier = (source // own_rows == target // own_rows) & (source < target)
    before = dot((hits[0] + hits[1]).astype(BF16), jnp.where(earlier, 1.0, 0.0).astype(BF16))
    numbered = jnp.where(before == (row % most_slots).astype(F32), 1.0, 0.0)
    here = jnp.where(shard == (place[0] ^ (column // own_rows)), numbered, 0.0)
    choose[...] = (here * (hits[0] + hits[1])).astype(BF16)
    first[...] = (numbered * hits[0])[:, :own_rows]
    second[...] = (numbered * hits[1])[:, :own_rows]
    same = jnp.where(source == target, 1.0, 0.0).astype(BF16)
    columns = lax.dot_general(
        same, near.astype(BF16), (((1,), (1,)), ((), ())), preferred_element_type=F32
    )
    named[...] = columns[:own_rows]


def reordered(table, outer, inner, count):
    rows = table.shape[0]
    row = lax.broadcasted_iota(jnp.int32, (rows, rows), 0)
    column = lax.broadcasted_iota(jnp.int32, (rows, rows), 1)
    big, small, number = row // (inner * count), (row // count) % inner, row % count
    choice = jnp.where(column == small * (outer * count) + big * count + number, 1.0, 0.0).astype(BF16)
    return dot(choice, table).astype(BF16)


def hidden_body(chips, seq, place, own, *refs):
    terms, refs = refs[: chips - 1], refs[chips - 1 :]
    own_tokens, refs = refs[0], refs[1:]
    payloads, refs = refs[: seq - 1], refs[seq - 1 :]
    choose, hidden = refs[0], refs[1 : 1 + seq]
    outs = refs[1 + seq :]
    total = own[...]
    for term in terms:
        total = total + term[...].astype(F32)
    width = own.shape[1]
    rows = own_tokens.shape[0]
    start = pl.multiple_of(place[0] * width, 128)
    residual = [own_tokens[:, pl.ds(start, width)].astype(F32)]
    for payload in payloads:
        residual.append(payload[payload.shape[0] - rows :, :width].astype(F32))
    rounded = (jnp.concatenate(residual, axis=0) + total).astype(BF16)
    for d, out in enumerate(hidden):
        out[...] = rounded[d * rows : (d + 1) * rows]
    slots = dot(choose[...], rounded).astype(BF16)
    rows = slots.shape[0] // chips
    for w in range(chips):
        outs[w][...] = slots[w * rows : (w + 1) * rows]


def start_copies(jobs, place, sources, outs, sems):
    copies = []
    for index, (source, mask, axis) in enumerate(jobs):
        size = outs[index].shape[axis]
        if axis:
            where = (0, slice(None), pl.ds(mask * size, size))
        else:
            where = (0, pl.ds(pl.multiple_of((place[0] ^ mask) * size, 16), size))
        copies.append(pltpu.make_async_copy(sources[source].at[where], outs[index], sems.at[index]))
    for copy in copies:
        copy.start()
    return copies


def in_hbm(sources):
    return [pltpu.with_memory_space_constraint(source, pltpu.HBM) for source in sources]


def fetched_shapes(jobs, sources, width):
    blocks = []
    for source, _, axis in jobs:
        rows, columns = sources[source].shape[1:]
        blocks.append(pltpu.VMEM((rows, width) if axis else (width, columns), BF16))
    return blocks


def fetch_body(jobs, count, place, *refs):
    sources, outs, sems = refs[:count], refs[count:-1], refs[-1]
    for copy in start_copies(jobs, place, sources, outs, sems):
        copy.wait()


def fetch(place, jobs, width, sources, deps):
    return kernel_call(
        functools.partial(fetch_body, jobs, len(sources)),
        fetched_shapes(jobs, sources, width),
        [SMEM] + [pl.BlockSpec(memory_space=pltpu.HBM)] * len(sources),
        [pltpu.SemaphoreType.DMA((len(jobs),))],
        moved=2 * len(jobs) * width * sources[0].shape[2],
        deps=deps,
    )(place, *in_hbm(sources))


def expert_body(mask, first, last, model_width, jobs, count, parts, place, *refs):
    pieces, (gain, gate, up), refs = refs[:parts], refs[parts : parts + 3], refs[parts + 3 :]
    before, refs = ([], refs) if first else (refs[:3], refs[3:])
    sources, refs = refs[:count], refs[count:]
    outs, refs = (refs[:1], refs[1:]) if last else (refs[:3], refs[3:])
    copies = start_copies(jobs, place, sources, refs[:-1], refs[-1]) if jobs else []
    width = pieces[0].shape[1]
    values = jnp.concatenate([piece[...].astype(F32) for piece in pieces], axis=0)
    square = jnp.sum(values * values, axis=-1, keepdims=True)
    if not first:
        square = square + before[2][:, 0:1]
    start = pl.multiple_of((place[0] ^ mask) * width, 128)
    rows = (values * gain[:, pl.ds(start, width)]).astype(BF16)
    inverse = lax.rsqrt(square / model_width + EPSILON)
    if not last:
        outs[2][...] = jnp.broadcast_to(square, outs[2].shape)
    hidden_units = gate.shape[1]
    tile = tile_of(hidden_units, 512)
    for step in range(hidden_units // tile):
        part = slice(step * tile, (step + 1) * tile)
        gate_act = dot(rows, gate[:, part])
        up_act = dot(rows, up[:, part])
        if not first:
            gate_act = gate_act + before[0][:, part]
            up_act = up_act + before[1][:, part]
        if last:
            outs[0][:, part] = (silu(gate_act * inverse) * (up_act * inverse)).astype(BF16)
        else:
            outs[0][:, part] = gate_act
            outs[1][:, part] = up_act
    for copy in copies:
        copy.wait()


def expert_chunk(mask, first, last, place, piece, gain, gate, up, before, jobs, sources, deps):
    slots, width = sum(part.shape[0] for part in piece), piece[0].shape[1]
    model_width, hidden_units = gain.shape[1], gate.shape[1]
    total = shape((slots, hidden_units), F32)
    outs = [total, total, shape((slots, 128), F32)]
    if last:
        outs = [shape((slots, hidden_units), BF16)]
    sources = sources if jobs else []
    far = pl.BlockSpec(memory_space=pltpu.HBM)
    results = kernel_call(
        functools.partial(expert_body, mask, first, last, model_width, jobs, len(sources), len(piece)),
        outs + fetched_shapes(jobs, sources, width),
        [SMEM] + [VMEM] * (3 + len(piece) + len(before)) + [far] * len(sources),
        [pltpu.SemaphoreType.DMA((len(jobs),))] if jobs else [],
        flops=4 * slots * width * hidden_units,
        moved=4 * width * hidden_units,
        limit=12,
        deps=deps,
    )(place, *piece, gain, gate, up, *before, *in_hbm(sources))
    return results[: len(outs)], results[len(outs) :]


def down_body(seq, cuts, place, hidden, *refs):
    downs, outs, product = refs[:seq], refs[seq:-1], refs[-1]
    width = downs[0].shape[1]
    tile = tile_of(width, 512)
    for block, down in enumerate(downs):
        for step in range(width // tile):
            part = slice(step * tile, (step + 1) * tile)
            to = slice(block * width + step * tile, block * width + (step + 1) * tile)
            product[:, to] = dot(hidden[...], down[:, part]).astype(BF16)
    for (mask, index), out in zip(cuts, outs):
        rows, columns = out.shape
        start = pl.multiple_of((place[0] ^ mask) * rows, 16)
        out[...] = product[pl.ds(start, rows), index * columns : (index + 1) * columns]


def pair_sum_body(*refs):
    count = len(refs) // 3
    for one, other, out in zip(refs[:count], refs[count : 2 * count], refs[2 * count :]):
        out[...] = (one[...].astype(F32) + other[...].astype(F32)).astype(BF16)


def expert_sum_body(seq, groups, most_slots, places, *refs):
    own, terms, outs = refs[0], refs[1 : 1 + len(places)], refs[1 + len(places) :]
    width = outs[0].shape[1]
    pieces = []
    for q in range(seq):
        total = own[:, q * width : (q + 1) * width].astype(F32)
        for index, term in zip(places, terms):
            start = q * width - index * term.shape[1]
            if 0 <= start < term.shape[1]:
                total = total + term[:, start : start + width].astype(F32)
        pieces.append(total.astype(BF16))
    pieces = reordered(jnp.concatenate(pieces, axis=0), groups, seq, most_slots)
    rows = pieces.shape[0] // len(outs)
    for w, out in enumerate(outs):
        out[...] = pieces[w * rows : (w + 1) * rows]


def shares_body(seq, place, gain, router, named, *refs):
    pieces, rows, shares = refs[:seq], refs[seq], refs[seq + 1]
    width = pieces[0].shape[1]
    for mask, piece in enumerate(pieces):
        start = pl.multiple_of((place[0] ^ mask) * width, 128)
        rows[:, pl.ds(start, width)] = piece[...].astype(F32)
    values = rows[...]
    inverse = lax.rsqrt(jnp.mean(values * values, axis=-1, keepdims=True) + EPSILON)
    moe_in = (values * inverse * gain[...]).astype(BF16)
    logits = lax.dot_general(
        moe_in, router[...], (((1,), (1,)), ((), ())), preferred_element_type=F32
    )
    lane = lax.broadcasted_iota(jnp.int32, logits.shape, 1).astype(F32)
    picked = [
        jnp.sum(jnp.where(lane == named[:, i : i + 1], logits, 0.0), axis=-1, keepdims=True)
        for i in range(2)
    ]
    first_share = 1.0 / (1.0 + jnp.exp(picked[1] - picked[0]))
    shares[...] = jnp.broadcast_to(first_share, shares.shape)


def halves_body(*refs):
    blocks, out = refs[:-1], refs[-1]
    for w, block in enumerate(blocks):
        out[w] = block[out.shape[1] :, :]


def second_halves(blocks, deps=()):
    rows, width = blocks[0].shape
    return kernel_call(
        halves_body,
        shape((len(blocks), rows // 2, width), BF16),
        [VMEM] * len(blocks),
        moved=2 * len(blocks) * rows * width,
        deps=deps,
    )(*blocks)


def rows_body(chips, seq, groups, most_slots, *refs):
    direct, crossed, out = refs[:chips], refs[chips], refs[chips + 1]
    half = crossed.shape[1]
    table = jnp.concatenate(
        [block for w in range(chips) for block in (direct[w][:half, :], crossed[w])], axis=0
    )
    out[...] = reordered(table, seq, groups, most_slots)


def combine_body(chips, seq, most_slots, *refs):
    direct = refs[:chips]
    crossed, first, second, rows, shares, out = refs[chips:]
    half = crossed.shape[1]
    table = jnp.concatenate(
        [block for w in range(chips) for block in (direct[w][:half, :], crossed[w])], axis=0
    )
    width = table.shape[1]
    row = lax.broadcasted_iota(jnp.int32, first.shape, 0)
    piece = (row // most_slots) % seq
    first_share = shares[:, 0:1]
    for q in range(seq):

        def rows_of(choice):
            chosen = jnp.where(piece == q, choice[...], 0.0).astype(BF16)
            return lax.dot_general(
                chosen, table, (((0,), (0,)), ((), ())), preferred_element_type=F32
            )

        part = slice(q * width, (q + 1) * width)
        sent = first_share * rows_of(first) + (1.0 - first_share) * rows_of(second)
        out[:, part] = (rows[:, part] + sent).astype(BF16)


halved = [(0, 0), (1, 0), (1, 1), (2, 0), (2, 1), (3, 0), (3, 1)]


def scattered(sends, masks, deps=()):
    if len(masks) != 3:
        terms = [partner(block, "seq", mask) for mask, block in zip(masks, sends)]
        return terms, [0] * len(terms)
    left, right, lower, upper, far_left, far_right = sends
    over = [partner(far_left, "seq", 1), partner(far_right, "seq", 2)]
    terms = [partner(left, "seq", 1), partner(upper, "seq", 2)]
    rows, columns = left.shape
    lower, right = kernel_call(
        pair_sum_body,
        [shape(left.shape, BF16)] * 2,
        [VMEM] * 4,
        flops=4 * rows * columns,
        moved=12 * rows * columns,
        deps=deps,
    )(lower, right, *over)
    return terms + [partner(right, "seq", 1), partner(lower, "seq", 2)], [0, 1, 1, 0]


def tile_of(total, most):
    for width in range(most, 0, -128):
        if total % width == 0:
            return width
    return total


def local(
    tokens,
    norm_gain,
    in_weight,
    conv_weight,
    conv_bias,
    proj_weight,
    step_weight,
    step_bias,
    decay_log,
    skip_gain,
    out_weight,
    moe_gain,
    router_weight,
    routes,
    gate_weight,
    up_weight,
    down_weight,
):
    seq, groups = lax.axis_size("seq"), lax.axis_size("expert")
    chips = groups // 2
    me, expert = lax.axis_index("seq"), lax.axis_index("expert")
    core = expert % 2
    place = jnp.stack([me, core, expert]).astype(jnp.int32)
    masks = range(1, seq)
    length, model_width = tokens.shape
    width = model_width // seq
    channels = in_weight.shape[2]
    rank_width = step_weight.shape[0]
    state_width = decay_log.shape[1]
    lanes = 128
    tiles = channels // lanes
    own_rows = routes.shape[0]
    experts = router_weight.shape[1]
    most_slots = max(2, 3 * own_rows // experts)
    window = seq * own_rows

    x_own, *x_send = kernel_call(
        functools.partial(norm_body, seq),
        [shape((length, width), BF16)] + [shape((length, width // 2), BF16)] * (seq - 1),
        [SMEM, VMEM, VMEM],
        flops=8 * length * model_width,
        moved=4 * length * model_width,
        limit=24,
    )(place, tokens, norm_gain[None])
    x_mine = [partner(block, "seq", mask) for mask, block in zip(masks, x_send)]
    weight = in_hbm([in_weight.reshape(width, 2 * channels)])[0]
    x_passed = kernel_call(
        pass_body,
        [shape((length, width // 2), BF16)] * (seq - 1),
        [VMEM] * (seq - 1),
        deps=[weight],
    )(*x_mine)
    x_other = [partner(block, "expert", 1) for block in x_passed]
    x = [x_own, *x_mine, *x_other]
    lane_routes = jnp.transpose(routes).astype(F32)
    spread_routes = jnp.stack(
        [
            jnp.pad(lane_routes, ((0, HALO - ROUTE_ROWS), (d * own_rows, channels - (d + 1) * own_rows)))
            for d in range(seq)
        ]
    )
    in_specs = [SMEM] + [VMEM] * (2 * seq - 1) + [pl.BlockSpec(memory_space=pltpu.HBM), VMEM]
    scratch = [pltpu.VMEM((width, channels), BF16), pltpu.SemaphoreType.DMA((4,))]
    cost = dict(flops=2 * seq * length * width * channels, moved=2 * width * channels, limit=24)
    cuts = halved if seq == 4 else [(mask, 0) for mask in range(seq)]
    mixer_own, *mixer_send = kernel_call(
        functools.partial(mixer_project_body, seq, cuts),
        [shape((HALO + length, channels), F32)]
        + [shape((HALO + length, channels // (2 if seq == 4 else 1)), BF16)] * (len(cuts) - 1),
        in_specs,
        [pltpu.VMEM((seq, HALO, channels), F32)] + scratch,
        **cost,
    )(place, *x, weight, spread_routes)
    assert width <= channels and window <= channels and 2 * length <= rank_width
    own_tokens = lax.dynamic_slice_in_dim(tokens, expert * own_rows, own_rows, 0)
    side_own, *side_send = kernel_call(
        functools.partial(gate_project_body, seq),
        [shape((length, channels), F32)] + [shape((length + own_rows, channels), BF16)] * (seq - 1),
        in_specs,
        scratch,
        **cost,
    )(place, *x, weight, own_tokens)

    mixer_terms, places = scattered(mixer_send, masks, [side_own])

    side_terms = [partner(block, "seq", mask) for mask, block in zip(masks, side_send)]
    activated, features = kernel_call(
        functools.partial(conv_body, places),
        [shape((length, channels), BF16), shape((length + state_width, rank_width), F32)],
        [VMEM] * (len(mixer_terms) + 4),
        limit=16,
    )(mixer_own, *mixer_terms, conv_weight, conv_bias[None], jnp.transpose(proj_weight))
    features = features + partner(features, "expert", 1)
    sent = features.astype(BF16)
    features_came = [partner(sent, "expert", 2 * w) for w in range(1, chips)]
    for term in features_came:
        features = features + term.astype(F32)
    low_rank, maps = features[:length].astype(BF16), features[length:]

    rate = -LOG2_E * jnp.exp(jnp.transpose(decay_log)).reshape(state_width, tiles, lanes)
    tiled = shape((length, tiles, lanes), F32)
    y, cumulated, final = kernel_call(
        scan_body,
        [tiled, tiled, shape((state_width + 2, tiles, lanes), BF16)],
        [SMEM] + [VMEM] * 5,
        [pltpu.VMEM(tiled.shape, F32)] * 2,
        limit=24,
    )(maps, low_rank, activated, step_weight, step_bias[None], rate)
    arrived = [partner(final, "seq", mask) for mask in masks]
    gated = kernel_call(
        functools.partial(gated_body, seq, own_rows),
        shape((length, channels), BF16),
        [SMEM, SMEM] + [VMEM] * (2 * seq + 4),
        [pltpu.VMEM(tiled.shape, F32), pltpu.VMEM((length, channels), F32)],
        limit=24,
    )(place, maps, *arrived, y, cumulated, rate, activated, skip_gain[None], side_own, *side_terms)

    blocks = [gated] + [partner(gated, "seq", mask) for mask in masks]

    slots = groups * seq * most_slots
    per_chip = slots // chips
    per_group = slots // groups
    route_terms = [term for term, index in zip(mixer_terms, places) if index == 0]
    choose, first, second, named = kernel_call(
        functools.partial(tables_body, seq, own_rows, most_slots),
        [shape((slots, window), BF16)] + [shape((slots, own_rows), F32)] * 2 + [shape((own_rows, 8), F32)],
        [SMEM, VMEM] + [VMEM] * len(route_terms),
        flops=2 * slots * window * window,
        moved=8 * slots * window,
    )(place, spread_routes[0], *route_terms)

    keep, send = kernel_call(
        functools.partial(out_project_body, seq, own_rows),
        [shape((chips, window, width), F32), shape((chips, window, width), BF16)],
        [VMEM] * (seq + 1),
        flops=2 * seq * length * channels * width,
        moved=2 * channels * width + 8 * seq * length * width,
        limit=16,
    )(*blocks, out_weight)
    crossing = partner(send, "expert", 1)
    own_sum, *chip_sends = kernel_call(
        core_sum_body,
        [shape((window, width), F32)] + [shape((window, width), BF16)] * (chips - 1),
        [VMEM] * 2,
        flops=chips * window * width,
        moved=10 * chips * window * width,
    )(keep, crossing)
    chip_terms = [partner(block, "expert", 2 * w) for w, block in zip(range(1, chips), chip_sends)]

    sources = [gate_weight, up_weight, down_weight]
    both = lambda mask: [(0, mask, 0), (1, mask, 0)]
    early = min(seq, 3)
    current = list(fetch(place, sum([both(mask) for mask in range(early)], []), width, sources[:2], [own_sum]))
    near_hidden = kernel_call(
        functools.partial(hidden_body, chips, seq),
        [shape((own_rows, width), BF16)] * seq + [shape((per_chip, width), BF16)] * chips,
        [SMEM] + [VMEM] * (chips + seq + 1),
        flops=2 * slots * window * width,
        moved=10 * window * width,
        deps=current,
    )(place, own_sum, *chip_terms, own_tokens, *side_terms, choose)
    near_hidden, outgoing = near_hidden[:seq], near_hidden[seq:]

    came = [outgoing[0]] + [
        partner(block, "expert", 2 * w) for w, block in zip(range(1, chips), outgoing[1:])
    ]
    whole = [near_hidden[0]] + [partner(near_hidden[mask], "seq", mask) for mask in masks]
    crossed = partner(second_halves(came, whole[1:]), "expert", 1)
    rows = kernel_call(
        functools.partial(rows_body, chips, seq, groups, most_slots),
        shape((slots, width), BF16),
        [VMEM] * (chips + 1),
        moved=4 * slots * width,
    )(*came, crossed)
    if seq == 4:
        pieces = [rows, partner(rows, "seq", 1), partner(rows, "seq", 2)]
        half = slots // 2
        pieces = [[piece] for piece in pieces] + [
            [partner(pieces[1][:half], "seq", 2), partner(pieces[2][half:], "seq", 1)]
        ]
    else:
        pieces = [[rows]] + [[partner(rows, "seq", mask)] for mask in masks]

    before, waiting, downs = [], current, []
    for mask in range(seq):
        jobs = both(mask + early) if mask + early < seq else []
        gates = len(jobs)
        if mask == max(0, seq - 4):
            jobs = jobs + [(2, block, 1) for block in range(seq)]
        before, came_in = expert_chunk(
            mask, mask == 0, mask == seq - 1, place, pieces[mask], moe_gain[None], *waiting[:2], before, jobs, sources, downs
        )
        waiting = waiting[2:] + list(came_in[:gates])
        downs = downs + list(came_in[gates:])
    hidden = before[0]
    back = groups * most_slots
    sums = kernel_call(
        functools.partial(down_body, seq, cuts),
        [shape((back, model_width // (2 if seq == 4 and mask else 1)), BF16) for mask, _ in cuts],
        [SMEM] + [VMEM] * (seq + 1),
        [pltpu.VMEM((slots, model_width), BF16)],
        flops=2 * slots * model_width * gate_weight.shape[2],
        moved=2 * model_width * gate_weight.shape[2],
        limit=16,
    )(place, hidden, *downs)
    terms, places = scattered(sums[1:], masks)

    own_hidden, shares = kernel_call(
        functools.partial(shares_body, seq),
        [shape((own_rows, model_width), F32), shape((own_rows, lanes), F32)],
        [SMEM] + [VMEM] * (seq + 3),
        flops=2 * own_rows * model_width * lanes,
        moved=16 * own_rows * model_width,
        deps=[sums[0]],
    )(place, moe_gain[None], jnp.transpose(router_weight), named, *whole)
    answers = kernel_call(
        functools.partial(expert_sum_body, seq, groups, most_slots, places),
        [shape((per_chip, width), BF16)] * chips,
        [VMEM] * (1 + len(terms)),
        flops=seq * slots * width,
        moved=10 * slots * width,
        deps=[shares],
    )(sums[0], *terms)
    answers = [answers[0]] + [
        partner(block, "expert", 2 * w) for w, block in zip(range(1, chips), answers[1:])
    ]
    crossed_back = partner(second_halves(answers), "expert", 1)
    return kernel_call(
        functools.partial(combine_body, chips, seq, most_slots),
        shape((own_rows, model_width), BF16),
        [VMEM] * (chips + 5),
        flops=4 * slots * own_rows * model_width,
        moved=8 * slots * width,
    )(*answers, crossed_back, first, second, own_hidden, shares)


def solution(mesh):
    in_specs = (
        P("seq", None),
        P(),
        P("seq", None, "expert"),
        P(None, "expert"),
        P("expert"),
        P("expert", None),
        P(None, "expert"),
        P("expert"),
        P("expert", None),
        P("expert"),
        P("expert", "seq"),
        P(),
        P(),
        P(("seq", "expert"), None),
        P("expert", None, "seq"),
        P("expert", None, "seq"),
        P("expert", "seq", None),
    )
    out_specs = P(("seq", "expert"), None)
    return jax.shard_map(local, mesh=mesh, in_specs=in_specs, out_specs=out_specs, check_vma=False)
```

```python
import functools

import jax
import jax.numpy as jnp
from jax import lax
from jax.experimental import pallas as pl
from jax.experimental.pallas import tpu as pltpu
from jax.sharding import PartitionSpec as P

EPSILON = 1e-06
HALO = 16
ROUTE_ROWS = 2
LOG2_E = 1.4426950408889634
MIB = 1 << 20
BF16 = jnp.bfloat16
F32 = jnp.float32

VMEM = pl.BlockSpec(memory_space=pltpu.VMEM)
SMEM = pl.BlockSpec(memory_space=pltpu.SMEM)


def partner(block, axis, mask):
    size = lax.axis_size(axis)
    return lax.ppermute(block, axis, [(i, i ^ mask) for i in range(size)])


def later_partner(block, axis, mask):
    size = lax.axis_size(axis)
    return lax.ppermute(block, axis, [(i, i ^ mask) for i in range(size) if i < i ^ mask])


def after(values, *done):
    flat, tree = jax.tree.flatten(values)
    held = lax.optimization_barrier((*flat, *done))
    return jax.tree.unflatten(tree, held[: len(flat)])


def shape(dims, dtype):
    return jax.ShapeDtypeStruct(tuple(dims), dtype)


def kernel_call(body, outs, in_specs, scratch=(), flops=0, moved=0, limit=8, deps=()):
    deps = list(deps)
    count = len(in_specs)

    def with_deps(*refs):
        body(*refs[:count], *refs[count + len(deps) :])

    call = pl.pallas_call(
        with_deps,
        out_shape=outs,
        in_specs=list(in_specs) + [pl.BlockSpec(memory_space=pl.ANY)] * len(deps),
        out_specs=jax.tree.map(lambda _: VMEM, outs),
        scratch_shapes=list(scratch),
        compiler_params=pltpu.CompilerParams(vmem_limit_bytes=limit * MIB),
        cost_estimate=pl.CostEstimate(flops=flops, bytes_accessed=moved, transcendentals=0),
    )
    return lambda *operands: call(*operands, *deps)


def dot(left, right):
    return jnp.dot(left, right, preferred_element_type=F32)


def silu(v):
    return v / (1.0 + jnp.exp(-v))


def norm_body(seq, place, tokens, gain, own, *refs):
    sends, (held, factors, sems) = refs[: seq - 1], refs[seq - 1 :]
    length, own_width = own.shape
    half = own_width // 2
    me, core = place[0], place[1]
    parts = sems.shape[0] - 1
    size = length // parts
    copies = [pltpu.make_async_copy(gain, factors, sems.at[parts])]
    for i in range(parts):
        rows = pl.ds(i * size, size)
        copies.append(pltpu.make_async_copy(tokens.at[rows], held.at[rows], sems.at[i]))
    for copy in copies:
        copy.start()
    copies[0].wait()
    for i in range(parts):
        copies[1 + i].wait()
        rows = slice(i * size, (i + 1) * size)
        values = held[rows, :].astype(F32)
        inverse = lax.rsqrt(jnp.mean(values * values, axis=-1, keepdims=True) + EPSILON)

        def columns(start, width):
            part = pl.ds(pl.multiple_of(start, 128), width)
            return (held[rows, part].astype(F32) * inverse * factors[:, part]).astype(BF16)

        own[rows, :] = columns(me * own_width, own_width)
        for mask in range(1, seq):
            sends[mask - 1][rows, :] = columns((me ^ mask) * own_width + core * half, half)


def pass_body(*refs):
    for block, out in zip(refs[: len(refs) // 2], refs[len(refs) // 2 :]):
        out[...] = block[...]


def weight_body(source, out, sem):
    copy = pltpu.make_async_copy(source.at[:, pl.ds(0, out.shape[1])], out, sem)
    copy.start()
    copy.wait()


def project(core, own, mine, other, source, branch, weight, sems):
    depth, channels = weight.shape
    parts = sems.shape[0] if sems is not None else 0
    copies = []
    for i in range(parts):
        rows = pl.ds(i * (depth // parts), depth // parts)
        part = source.at[rows, pl.ds(branch * channels, channels)]
        copies.append((rows, pltpu.make_async_copy(part, weight.at[rows], sems.at[i])))
    for _, copy in copies:
        copy.start()
    first = 0.0
    for rows, copy in copies:
        copy.wait()
        first = first + dot(own[:, rows], weight[rows, :])
    yield first if copies else dot(own[...], weight[...])
    half = depth // 2
    near = weight[pl.ds(pl.multiple_of(core * half, half), half), :]
    far = weight[pl.ds(pl.multiple_of((1 - core) * half, half), half), :]
    for left, right in zip(mine, other):
        yield dot(left[...], near) + dot(right[...], far)


def mixer_project_body(seq, cuts, place, *refs):
    own, mine, other = refs[0], refs[1:seq], refs[seq : 2 * seq - 1]
    refs = refs[2 * seq - 1 :]
    (weight, routes), outs, tails = refs[:2], refs[2:-1], refs[-1]
    me = place[0]
    length = own.shape[0]

    def store(mask, rows, values):
        for (number, index), out in zip(cuts, outs):
            if number == mask:
                columns = out.shape[1]
                out[rows, :] = values[:, index * columns : (index + 1) * columns].astype(out.dtype)

    for mask, product in enumerate(project(place[1], own, mine, other, None, 0, weight, None)):
        store(mask, slice(HALO, HALO + length), product)
        tails[mask] = product[length - HALO :, :]
    for mask in range(seq):
        shard = me ^ mask
        source = me ^ jnp.maximum(shard - 1, 0)
        before = jnp.where(shard > 0, tails[source], 0.0)
        row = lax.broadcasted_iota(jnp.int32, before.shape, 0)
        store(mask, slice(0, HALO), jnp.where(row < ROUTE_ROWS, routes[mask], before))


def gate_project_body(seq, place, *refs):
    own, mine, other = refs[0], refs[1:seq], refs[seq : 2 * seq - 1]
    refs = refs[2 * seq - 1 :]
    (weight, own_tokens), outs, (held, sems) = refs[:2], refs[2 : seq + 2], refs[seq + 2 :]
    length, width = own.shape
    for index, product in enumerate(project(place[1], own, mine, other, weight, 1, held, sems)):
        outs[index][:length, :] = product.astype(outs[index].dtype)
        if index:
            start = pl.multiple_of((place[0] ^ index) * width, 128)
            rows = own_tokens[:, pl.ds(start, width)]
            spare = outs[index].shape[1] - width
            if spare:
                rows = jnp.concatenate([rows, jnp.zeros((rows.shape[0], spare), rows.dtype)], axis=1)
            outs[index][length:, :] = rows


def conv_body(places, *refs):
    own, terms = refs[0], refs[1 : 1 + len(places)]
    taps, bias, proj, activated, features = refs[1 + len(places) :]
    columns = [own[:, i * terms[0].shape[1] : (i + 1) * terms[0].shape[1]] for i in range(max(places) + 1)]
    for index, term in zip(places, terms):
        columns[index] = columns[index] + term[...].astype(F32)
    total = jnp.concatenate(columns, axis=1)
    padded = total.astype(BF16).astype(F32)
    length = activated.shape[0]
    count = taps.shape[0]
    convolved = bias[...]
    for tap in range(count):
        start = HALO - count + 1 + tap
        convolved = convolved + taps[tap : tap + 1, :] * padded[start : start + length]
    rounded = silu(convolved).astype(BF16)
    activated[...] = rounded
    rank = features.shape[1]
    states = (proj.shape[0] - rank) // 2

    def both_last(one, other):
        return lax.dot_general(one, other, (((1,), (1,)), ((), ())), preferred_element_type=F32)

    features[:length, :] = both_last(rounded, proj[:rank, :])
    maps = both_last(proj[rank:, :], rounded)
    below = jnp.zeros((features.shape[0] - length, rank), F32)
    features[length:, :] = below
    for i in range(2):
        features[length:, i * length : (i + 1) * length] = maps[i * states : (i + 1) * states]


def scan_body(maps, low_rank, activated, step_weight, step_bias, rate, y, cumulated, final, steps, drive):
    length, groups, lanes = y.shape
    states = rate.shape[0]
    raw = dot(low_rank[...], step_weight[...]) + step_bias[...]
    step_size = jnp.maximum(raw, 0.0) + jnp.log1p(jnp.exp(-jnp.abs(raw)))
    driven = step_size * activated[...].astype(F32)
    for group in range(groups):
        part = slice(group * lanes, (group + 1) * lanes)
        steps[:, group, :] = step_size[:, part]
        drive[:, group, :] = driven[:, part]
    rates = [rate[n] for n in range(states)]

    def advance(t, carry):
        state, running = carry
        step, push = steps[t], drive[t]
        running = running + step
        fresh = []
        out = jnp.zeros_like(step)
        for n in range(states):
            value = jnp.exp2(step * rates[n]) * state[n] + push * maps[n, t]
            out = out + value * maps[n, length + t]
            fresh.append(value)
        y[t] = out
        cumulated[t] = running
        return tuple(fresh), running

    zero = jnp.zeros((groups, lanes), F32)
    state, running = lax.fori_loop(0, length, advance, ((zero,) * states, zero), unroll=8)
    for n in range(states):
        final[n] = state[n].astype(BF16)
    upper = running.astype(BF16)
    final[states] = upper
    final[states + 1] = (running - upper.astype(F32)).astype(BF16)


def gated_body(seq, own_rows, place, maps, *refs):
    arrived = refs[: seq - 1]
    y, cumulated, rate, activated, skip_gain = refs[seq - 1 : seq + 4]
    gates = refs[seq + 4 : 2 * seq + 4]
    gated, scanned, result = refs[2 * seq + 4 :]
    length, groups, lanes = y.shape
    states = rate.shape[0]
    me, expert = place[0], place[2]
    zero = jnp.zeros((groups, lanes), F32)
    incoming = [zero] * states
    sums = [block[states].astype(F32) + block[states + 1].astype(F32) for block in arrived]
    for mask in range(1, seq):
        shard = me ^ mask
        between = zero
        for other in range(1, seq):
            middle = me ^ other
            inside = (shard < middle) & (middle < me)
            between = between + jnp.where(inside, sums[other - 1], 0.0)
        for n in range(states):
            term = jnp.exp2(rate[n] * between) * arrived[mask - 1][n].astype(F32)
            incoming[n] = incoming[n] + jnp.where(shard < me, term, 0.0)
    rates = [rate[n] for n in range(states)]

    def correct(t, carry):
        steps = cumulated[t]
        out = y[t]
        for n in range(states):
            out = out + (jnp.exp2(steps * rates[n]) * incoming[n]) * maps[n, length + t]
        scanned[t] = out
        return carry

    lax.fori_loop(0, length, correct, 0, unroll=8)
    for group in range(groups):
        part = slice(group * lanes, (group + 1) * lanes)
        gate = gates[0][:, part]
        for term in gates[1:]:
            gate = gate + term[:length, part].astype(F32)
        gate = gate.astype(BF16).astype(F32)
        drive = activated[:, part].astype(F32)
        result[:, part] = (scanned[:, group, :] + skip_gain[:, part] * drive) * silu(gate)
    blocks = length // own_rows
    moved = [
        result[pl.ds(pl.multiple_of((expert ^ k) * own_rows, own_rows), own_rows), :]
        for k in range(blocks)
    ]
    gated[...] = jnp.concatenate(moved, axis=0).astype(BF16)


def out_project_body(seq, own_rows, *refs):
    blocks = refs[:seq]
    weight, keep, send = refs[seq:]
    for shard in range(seq):
        product = dot(blocks[shard][...], weight[...])
        for owner in range(product.shape[0] // own_rows):
            rows = product[owner * own_rows : (owner + 1) * own_rows]
            place = (owner // 2, pl.ds(shard * own_rows, own_rows))
            if owner % 2 == 0:
                keep[place[0], place[1], :] = rows
            else:
                send[place[0], place[1], :] = rows.astype(BF16)


def core_sum_body(keep, arrived, own, *sends):
    own[...] = keep[0] + arrived[0].astype(F32)
    for w in range(1, keep.shape[0]):
        sends[w - 1][...] = (keep[w] + arrived[w].astype(F32)).astype(BF16)


def tables_body(seq, own_rows, most_slots, place, routes, *refs):
    terms, (choose, first, second, named) = refs[:-4], refs[-4:]
    slots, window = choose.shape
    near = routes[:8, :window]
    for term in terms:
        near = near + term[:16, :window].astype(F32)[:8]
    row = lax.broadcasted_iota(jnp.int32, (slots, window), 0)
    column = lax.broadcasted_iota(jnp.int32, (slots, window), 1)
    wanted = (place[2] ^ (row // (seq * most_slots))).astype(F32)
    shard = (row // most_slots) % seq
    hits = [jnp.where(near[i : i + 1, :] == wanted, 1.0, 0.0) for i in range(2)]
    source = lax.broadcasted_iota(jnp.int32, (window, window), 0)
    target = lax.broadcasted_iota(jnp.int32, (window, window), 1)
    earlier = (source // own_rows == target // own_rows) & (source < target)
    before = dot((hits[0] + hits[1]).astype(BF16), jnp.where(earlier, 1.0, 0.0).astype(BF16))
    numbered = jnp.where(before == (row % most_slots).astype(F32), 1.0, 0.0)
    here = jnp.where(shard == (place[0] ^ (column // own_rows)), numbered, 0.0)
    choose[...] = (here * (hits[0] + hits[1])).astype(BF16)
    first[...] = (numbered * hits[0])[:, :own_rows]
    second[...] = (numbered * hits[1])[:, :own_rows]
    same = jnp.where(source == target, 1.0, 0.0).astype(BF16)
    columns = lax.dot_general(
        same, near.astype(BF16), (((1,), (1,)), ((), ())), preferred_element_type=F32
    )
    named[...] = columns[:own_rows]


def reordered(table, outer, inner, count):
    rows = table.shape[0]
    row = lax.broadcasted_iota(jnp.int32, (rows, rows), 0)
    column = lax.broadcasted_iota(jnp.int32, (rows, rows), 1)
    big, small, number = row // (inner * count), (row // count) % inner, row % count
    choice = jnp.where(column == small * (outer * count) + big * count + number, 1.0, 0.0).astype(BF16)
    return dot(choice, table).astype(BF16)


def hidden_body(chips, seq, place, own, *refs):
    terms, refs = refs[: chips - 1], refs[chips - 1 :]
    own_tokens, refs = refs[0], refs[1:]
    payloads, refs = refs[: seq - 1], refs[seq - 1 :]
    choose, hidden = refs[0], refs[1 : 1 + seq]
    outs = refs[1 + seq :]
    total = own[...]
    for term in terms:
        total = total + term[...].astype(F32)
    width = own.shape[1]
    rows = own_tokens.shape[0]
    start = pl.multiple_of(place[0] * width, 128)
    residual = [own_tokens[:, pl.ds(start, width)].astype(F32)]
    for payload in payloads:
        residual.append(payload[payload.shape[0] - rows :, :width].astype(F32))
    rounded = (jnp.concatenate(residual, axis=0) + total).astype(BF16)
    for d, out in enumerate(hidden):
        out[...] = rounded[d * rows : (d + 1) * rows]
    slots = dot(choose[...], rounded).astype(BF16)
    rows = slots.shape[0] // chips
    for w in range(chips):
        outs[w][...] = slots[w * rows : (w + 1) * rows]


def start_copies(jobs, place, sources, outs, sems):
    copies = []
    for index, (source, mask, axis) in enumerate(jobs):
        size = outs[index].shape[axis]
        if axis:
            where = (0, slice(None), pl.ds(mask * size, size))
        else:
            where = (0, pl.ds(pl.multiple_of((place[0] ^ mask) * size, 16), size))
        copies.append(pltpu.make_async_copy(sources[source].at[where], outs[index], sems.at[index]))
    for copy in copies:
        copy.start()
    return copies


def in_hbm(sources):
    return [pltpu.with_memory_space_constraint(source, pltpu.HBM) for source in sources]


def fetched_shapes(jobs, sources, width):
    blocks = []
    for source, _, axis in jobs:
        rows, columns = sources[source].shape[1:]
        blocks.append(pltpu.VMEM((rows, width) if axis else (width, columns), BF16))
    return blocks


def fetch_body(jobs, count, place, *refs):
    sources, outs, sems = refs[:count], refs[count:-1], refs[-1]
    for copy in start_copies(jobs, place, sources, outs, sems):
        copy.wait()


def fetch(place, jobs, width, sources, deps):
    return kernel_call(
        functools.partial(fetch_body, jobs, len(sources)),
        fetched_shapes(jobs, sources, width),
        [SMEM] + [pl.BlockSpec(memory_space=pltpu.HBM)] * len(sources),
        [pltpu.SemaphoreType.DMA((len(jobs),))],
        moved=2 * len(jobs) * width * sources[0].shape[2],
        deps=deps,
    )(place, *in_hbm(sources))


def expert_body(mask, first, last, model_width, jobs, count, parts, place, *refs):
    pieces, (gain, gate, up), refs = refs[:parts], refs[parts : parts + 3], refs[parts + 3 :]
    before, refs = ([], refs) if first else (refs[:3], refs[3:])
    sources, refs = refs[:count], refs[count:]
    outs, refs = (refs[:1], refs[1:]) if last else (refs[:3], refs[3:])
    copies = start_copies(jobs, place, sources, refs[:-1], refs[-1]) if jobs else []
    width = pieces[0].shape[1]
    values = jnp.concatenate([piece[...].astype(F32) for piece in pieces], axis=0)
    square = jnp.sum(values * values, axis=-1, keepdims=True)
    if not first:
        square = square + before[2][:, 0:1]
    start = pl.multiple_of((place[0] ^ mask) * width, 128)
    rows = (values * gain[:, pl.ds(start, width)]).astype(BF16)
    inverse = lax.rsqrt(square / model_width + EPSILON)
    if not last:
        outs[2][...] = jnp.broadcast_to(square, outs[2].shape)
    hidden_units = gate.shape[1]
    tile = tile_of(hidden_units, 512)
    for step in range(hidden_units // tile):
        part = slice(step * tile, (step + 1) * tile)
        gate_act = dot(rows, gate[:, part])
        up_act = dot(rows, up[:, part])
        if not first:
            gate_act = gate_act + before[0][:, part]
            up_act = up_act + before[1][:, part]
        if last:
            outs[0][:, part] = (silu(gate_act * inverse) * (up_act * inverse)).astype(BF16)
        else:
            outs[0][:, part] = gate_act
            outs[1][:, part] = up_act
    for copy in copies:
        copy.wait()


def expert_chunk(mask, first, last, place, piece, gain, gate, up, before, jobs, sources, deps):
    slots, width = sum(part.shape[0] for part in piece), piece[0].shape[1]
    model_width, hidden_units = gain.shape[1], gate.shape[1]
    total = shape((slots, hidden_units), F32)
    outs = [total, total, shape((slots, 128), F32)]
    if last:
        outs = [shape((slots, hidden_units), BF16)]
    sources = sources if jobs else []
    far = pl.BlockSpec(memory_space=pltpu.HBM)
    results = kernel_call(
        functools.partial(expert_body, mask, first, last, model_width, jobs, len(sources), len(piece)),
        outs + fetched_shapes(jobs, sources, width),
        [SMEM] + [VMEM] * (3 + len(piece) + len(before)) + [far] * len(sources),
        [pltpu.SemaphoreType.DMA((len(jobs),))] if jobs else [],
        flops=4 * slots * width * hidden_units,
        moved=4 * width * hidden_units,
        limit=12,
        deps=deps,
    )(place, *piece, gain, gate, up, *before, *in_hbm(sources))
    return results[: len(outs)], results[len(outs) :]


def down_body(seq, cuts, place, hidden, *refs):
    downs, outs, product = refs[:seq], refs[seq:-1], refs[-1]
    width = downs[0].shape[1]
    tile = tile_of(width, 512)
    for block, down in enumerate(downs):
        for step in range(width // tile):
            part = slice(step * tile, (step + 1) * tile)
            to = slice(block * width + step * tile, block * width + (step + 1) * tile)
            product[:, to] = dot(hidden[...], down[:, part]).astype(BF16)
    for (mask, index), out in zip(cuts, outs):
        rows, columns = out.shape
        start = pl.multiple_of((place[0] ^ mask) * rows, 16)
        out[...] = product[pl.ds(start, rows), index * columns : (index + 1) * columns]


def pair_sum_body(*refs):
    count = len(refs) // 3
    for one, other, out in zip(refs[:count], refs[count : 2 * count], refs[2 * count :]):
        out[...] = (one[...].astype(F32) + other[...].astype(F32)).astype(BF16)


def expert_sum_body(seq, groups, most_slots, places, *refs):
    own, terms, outs = refs[0], refs[1 : 1 + len(places)], refs[1 + len(places) :]
    width = outs[0].shape[1]
    pieces = []
    for q in range(seq):
        total = own[:, q * width : (q + 1) * width].astype(F32)
        for index, term in zip(places, terms):
            start = q * width - index * term.shape[1]
            if 0 <= start < term.shape[1]:
                total = total + term[:, start : start + width].astype(F32)
        pieces.append(total.astype(BF16))
    pieces = reordered(jnp.concatenate(pieces, axis=0), groups, seq, most_slots)
    rows = pieces.shape[0] // len(outs)
    for w, out in enumerate(outs):
        out[...] = pieces[w * rows : (w + 1) * rows]


def shares_body(seq, place, gain, router, named, *refs):
    pieces, rows, shares = refs[:seq], refs[seq], refs[seq + 1]
    width = pieces[0].shape[1]
    for mask, piece in enumerate(pieces):
        start = pl.multiple_of((place[0] ^ mask) * width, 128)
        rows[:, pl.ds(start, width)] = piece[...].astype(F32)
    values = rows[...]
    inverse = lax.rsqrt(jnp.mean(values * values, axis=-1, keepdims=True) + EPSILON)
    moe_in = (values * inverse * gain[...]).astype(BF16)
    logits = lax.dot_general(
        moe_in, router[...], (((1,), (1,)), ((), ())), preferred_element_type=F32
    )
    lane = lax.broadcasted_iota(jnp.int32, logits.shape, 1).astype(F32)
    picked = [
        jnp.sum(jnp.where(lane == named[:, i : i + 1], logits, 0.0), axis=-1, keepdims=True)
        for i in range(2)
    ]
    first_share = 1.0 / (1.0 + jnp.exp(picked[1] - picked[0]))
    shares[...] = jnp.broadcast_to(first_share, shares.shape)


def halves_body(*refs):
    blocks, out = refs[:-1], refs[-1]
    for w, block in enumerate(blocks):
        out[w] = block[out.shape[1] :, :]


def second_halves(blocks, deps=()):
    rows, width = blocks[0].shape
    return kernel_call(
        halves_body,
        shape((len(blocks), rows // 2, width), BF16),
        [VMEM] * len(blocks),
        moved=2 * len(blocks) * rows * width,
        deps=deps,
    )(*blocks)


def rows_body(chips, seq, groups, most_slots, *refs):
    direct, crossed, out = refs[:chips], refs[chips], refs[chips + 1]
    half = crossed.shape[1]
    table = jnp.concatenate(
        [block for w in range(chips) for block in (direct[w][:half, :], crossed[w])], axis=0
    )
    out[...] = reordered(table, seq, groups, most_slots)


def combine_body(chips, seq, most_slots, *refs):
    direct = refs[:chips]
    crossed, first, second, rows, shares, out = refs[chips:]
    half = crossed.shape[1]
    table = jnp.concatenate(
        [block for w in range(chips) for block in (direct[w][:half, :], crossed[w])], axis=0
    )
    width = table.shape[1]
    row = lax.broadcasted_iota(jnp.int32, first.shape, 0)
    piece = (row // most_slots) % seq
    first_share = shares[:, 0:1]
    for q in range(seq):

        def rows_of(choice):
            chosen = jnp.where(piece == q, choice[...], 0.0).astype(BF16)
            return lax.dot_general(
                chosen, table, (((0,), (0,)), ((), ())), preferred_element_type=F32
            )

        part = slice(q * width, (q + 1) * width)
        sent = first_share * rows_of(first) + (1.0 - first_share) * rows_of(second)
        out[:, part] = (rows[:, part] + sent).astype(BF16)


halved = [(0, 0), (1, 0), (1, 1), (2, 0), (2, 1), (3, 0), (3, 1)]


def scattered(sends, masks, deps=()):
    if len(masks) != 3:
        terms = [partner(block, "seq", mask) for mask, block in zip(masks, sends)]
        return terms, [0] * len(terms)
    left, right, lower, upper, far_left, far_right = sends
    over = [partner(far_left, "seq", 1), partner(far_right, "seq", 2)]
    terms = [partner(left, "seq", 1), partner(upper, "seq", 2)]
    rows, columns = left.shape
    lower, right = kernel_call(
        pair_sum_body,
        [shape(left.shape, BF16)] * 2,
        [VMEM] * 4,
        flops=4 * rows * columns,
        moved=12 * rows * columns,
        deps=deps,
    )(lower, right, *over)
    return terms + [partner(right, "seq", 1), partner(lower, "seq", 2)], [0, 1, 1, 0]


def tile_of(total, most):
    for width in range(most, 0, -128):
        if total % width == 0:
            return width
    return total


def local(
    tokens,
    norm_gain,
    in_weight,
    conv_weight,
    conv_bias,
    proj_weight,
    step_weight,
    step_bias,
    decay_log,
    skip_gain,
    out_weight,
    moe_gain,
    router_weight,
    routes,
    gate_weight,
    up_weight,
    down_weight,
):
    seq, groups = lax.axis_size("seq"), lax.axis_size("expert")
    chips = groups // 2
    me, expert = lax.axis_index("seq"), lax.axis_index("expert")
    core = expert % 2
    place = jnp.stack([me, core, expert]).astype(jnp.int32)
    masks = range(1, seq)
    length, model_width = tokens.shape
    width = model_width // seq
    channels = in_weight.shape[2]
    rank_width = step_weight.shape[0]
    state_width = decay_log.shape[1]
    lanes = 128
    tiles = channels // lanes
    own_rows = routes.shape[0]
    experts = router_weight.shape[1]
    most_slots = max(2, 3 * own_rows // experts)
    window = seq * own_rows

    x_own, *x_send = kernel_call(
        functools.partial(norm_body, seq),
        [shape((length, width), BF16)] + [shape((length, width // 2), BF16)] * (seq - 1),
        [SMEM] + [pl.BlockSpec(memory_space=pltpu.HBM)] * 2,
        [
            pltpu.VMEM(tokens.shape, BF16),
            pltpu.VMEM((1, model_width), F32),
            pltpu.SemaphoreType.DMA((5,)),
        ],
        flops=8 * length * model_width,
        moved=4 * length * model_width,
        limit=24,
    )(place, *in_hbm([tokens, norm_gain[None]]))
    x_mine = [partner(block, "seq", mask) for mask, block in zip(masks, x_send)]
    weight = in_hbm([in_weight.reshape(width, 2 * channels)])[0]
    x_passed = kernel_call(
        pass_body,
        [shape((length, width // 2), BF16)] * (seq - 1),
        [VMEM] * (seq - 1),
        deps=[weight],
    )(*x_mine)
    x_other = [partner(block, "expert", 1) for block in x_passed]
    x = [x_own, *x_mine, *x_other]
    mixer_weight = kernel_call(
        weight_body,
        pltpu.VMEM((width, channels), BF16),
        [pl.BlockSpec(memory_space=pltpu.HBM)],
        [pltpu.SemaphoreType.DMA],
        moved=4 * width * channels,
        deps=x_passed[:1],
    )(weight)
    lane_routes = jnp.transpose(routes).astype(F32)
    spread_routes = jnp.stack(
        [
            jnp.pad(lane_routes, ((0, HALO - ROUTE_ROWS), (d * own_rows, channels - (d + 1) * own_rows)))
            for d in range(seq)
        ]
    )
    in_specs = [SMEM] + [VMEM] * (2 * seq - 1) + [pl.BlockSpec(memory_space=pltpu.HBM), VMEM]
    scratch = [pltpu.VMEM((width, channels), BF16), pltpu.SemaphoreType.DMA((4,))]
    cost = dict(flops=2 * seq * length * width * channels, moved=2 * width * channels, limit=24)
    cuts = halved if seq == 4 else [(mask, 0) for mask in range(seq)]
    mixer_own, *mixer_send = kernel_call(
        functools.partial(mixer_project_body, seq, cuts),
        [shape((HALO + length, channels), F32)]
        + [shape((HALO + length, channels // (2 if seq == 4 else 1)), BF16)] * (len(cuts) - 1),
        [SMEM] + [VMEM] * (2 * seq + 1),
        [pltpu.VMEM((seq, HALO, channels), F32)],
        **cost,
    )(place, *x, mixer_weight, spread_routes)
    assert width <= channels and window <= channels and 2 * length <= rank_width
    own_tokens = lax.dynamic_slice_in_dim(tokens, expert * own_rows, own_rows, 0)
    side_own, *side_send = kernel_call(
        functools.partial(gate_project_body, seq),
        [shape((length, channels), F32)] + [shape((length + own_rows, channels), BF16)] * (seq - 1),
        in_specs,
        scratch,
        **cost,
    )(place, *x, weight, own_tokens)

    mixer_terms, places = scattered(mixer_send, masks, [side_own])

    side_terms = [partner(block, "seq", mask) for mask, block in zip(masks, side_send)]
    activated, features = kernel_call(
        functools.partial(conv_body, places),
        [shape((length, channels), BF16), shape((length + state_width, rank_width), F32)],
        [VMEM] * (len(mixer_terms) + 4),
        limit=16,
    )(mixer_own, *mixer_terms, conv_weight, conv_bias[None], jnp.transpose(proj_weight))
    features = features + partner(features, "expert", 1)
    sent = features.astype(BF16)
    features_came = [partner(sent, "expert", 2 * w) for w in range(1, chips)]
    for term in features_came:
        features = features + term.astype(F32)
    low_rank, maps = features[:length].astype(BF16), features[length:]

    rate = -LOG2_E * jnp.exp(jnp.transpose(decay_log)).reshape(state_width, tiles, lanes)
    tiled = shape((length, tiles, lanes), F32)
    y, cumulated, final = kernel_call(
        scan_body,
        [tiled, tiled, shape((state_width + 2, tiles, lanes), BF16)],
        [SMEM] + [VMEM] * 5,
        [pltpu.VMEM(tiled.shape, F32)] * 2,
        limit=24,
    )(maps, low_rank, activated, step_weight, step_bias[None], rate)
    arrived = [partner(final, "seq", mask) for mask in masks]
    gated = kernel_call(
        functools.partial(gated_body, seq, own_rows),
        shape((length, channels), BF16),
        [SMEM, SMEM] + [VMEM] * (2 * seq + 4),
        [pltpu.VMEM(tiled.shape, F32), pltpu.VMEM((length, channels), F32)],
        limit=24,
    )(place, maps, *arrived, y, cumulated, rate, activated, skip_gain[None], side_own, *side_terms)

    blocks = [gated] + [partner(gated, "seq", mask) for mask in masks]

    slots = groups * seq * most_slots
    per_chip = slots // chips
    per_group = slots // groups
    route_terms = [term for term, index in zip(mixer_terms, places) if index == 0]
    choose, first, second, named = kernel_call(
        functools.partial(tables_body, seq, own_rows, most_slots),
        [shape((slots, window), BF16)] + [shape((slots, own_rows), F32)] * 2 + [shape((own_rows, 8), F32)],
        [SMEM, VMEM] + [VMEM] * len(route_terms),
        flops=2 * slots * window * window,
        moved=8 * slots * window,
    )(place, spread_routes[0], *route_terms)

    keep, send = kernel_call(
        functools.partial(out_project_body, seq, own_rows),
        [shape((chips, window, width), F32), shape((chips, window, width), BF16)],
        [VMEM] * (seq + 1),
        flops=2 * seq * length * channels * width,
        moved=2 * channels * width + 8 * seq * length * width,
        limit=16,
    )(*blocks, out_weight)
    crossing = partner(send, "expert", 1)
    own_sum, *chip_sends = kernel_call(
        core_sum_body,
        [shape((window, width), F32)] + [shape((window, width), BF16)] * (chips - 1),
        [VMEM] * 2,
        flops=chips * window * width,
        moved=10 * chips * window * width,
    )(keep, crossing)
    chip_terms = [partner(block, "expert", 2 * w) for w, block in zip(range(1, chips), chip_sends)]

    sources = [gate_weight, up_weight, down_weight]
    both = lambda mask: [(0, mask, 0), (1, mask, 0)]
    early = min(seq, 3)
    current = list(fetch(place, sum([both(mask) for mask in range(early)], []), width, sources[:2], [own_sum]))
    near_hidden = kernel_call(
        functools.partial(hidden_body, chips, seq),
        [shape((own_rows, width), BF16)] * seq + [shape((per_chip, width), BF16)] * chips,
        [SMEM] + [VMEM] * (chips + seq + 1),
        flops=2 * slots * window * width,
        moved=10 * window * width,
        deps=current,
    )(place, own_sum, *chip_terms, own_tokens, *side_terms, choose)
    near_hidden, outgoing = near_hidden[:seq], near_hidden[seq:]

    came = [outgoing[0]] + [
        partner(block, "expert", 2 * w) for w, block in zip(range(1, chips), outgoing[1:])
    ]
    whole = [near_hidden[0]] + [partner(near_hidden[mask], "seq", mask) for mask in masks]
    crossed = partner(second_halves(came, whole[1:]), "expert", 1)
    rows = kernel_call(
        functools.partial(rows_body, chips, seq, groups, most_slots),
        shape((slots, width), BF16),
        [VMEM] * (chips + 1),
        moved=4 * slots * width,
    )(*came, crossed)
    if seq == 4:
        pieces = [rows, partner(rows, "seq", 1), partner(rows, "seq", 2)]
        half = slots // 2
        pieces = [[piece] for piece in pieces] + [
            [partner(pieces[1][:half], "seq", 2), partner(pieces[2][half:], "seq", 1)]
        ]
    else:
        pieces = [[rows]] + [[partner(rows, "seq", mask)] for mask in masks]

    before, waiting, downs = [], current, []
    for mask in range(seq):
        jobs = both(mask + early) if mask + early < seq else []
        gates = len(jobs)
        if mask == max(0, seq - 4):
            jobs = jobs + [(2, block, 1) for block in range(seq)]
        before, came_in = expert_chunk(
            mask, mask == 0, mask == seq - 1, place, pieces[mask], moe_gain[None], *waiting[:2], before, jobs, sources, downs
        )
        waiting = waiting[2:] + list(came_in[:gates])
        downs = downs + list(came_in[gates:])
    hidden = before[0]
    back = groups * most_slots
    sums = kernel_call(
        functools.partial(down_body, seq, cuts),
        [shape((back, model_width // (2 if seq == 4 and mask else 1)), BF16) for mask, _ in cuts],
        [SMEM] + [VMEM] * (seq + 1),
        [pltpu.VMEM((slots, model_width), BF16)],
        flops=2 * slots * model_width * gate_weight.shape[2],
        moved=2 * model_width * gate_weight.shape[2],
        limit=16,
    )(place, hidden, *downs)
    terms, places = scattered(sums[1:], masks)

    own_hidden, shares = kernel_call(
        functools.partial(shares_body, seq),
        [shape((own_rows, model_width), F32), shape((own_rows, lanes), F32)],
        [SMEM] + [VMEM] * (seq + 3),
        flops=2 * own_rows * model_width * lanes,
        moved=16 * own_rows * model_width,
        deps=[sums[0]],
    )(place, moe_gain[None], jnp.transpose(router_weight), named, *whole)
    answers = kernel_call(
        functools.partial(expert_sum_body, seq, groups, most_slots, places),
        [shape((per_chip, width), BF16)] * chips,
        [VMEM] * (1 + len(terms)),
        flops=seq * slots * width,
        moved=10 * slots * width,
        deps=[shares],
    )(sums[0], *terms)
    answers = [answers[0]] + [
        partner(block, "expert", 2 * w) for w, block in zip(range(1, chips), answers[1:])
    ]
    crossed_back = partner(second_halves(answers), "expert", 1)
    return kernel_call(
        functools.partial(combine_body, chips, seq, most_slots),
        shape((own_rows, model_width), BF16),
        [VMEM] * (chips + 5),
        flops=4 * slots * own_rows * model_width,
        moved=8 * slots * width,
    )(*answers, crossed_back, first, second, own_hidden, shares)


def solution(mesh):
    in_specs = (
        P("seq", None),
        P(),
        P("seq", None, "expert"),
        P(None, "expert"),
        P("expert"),
        P("expert", None),
        P(None, "expert"),
        P("expert"),
        P("expert", None),
        P("expert"),
        P("expert", "seq"),
        P(),
        P(),
        P(("seq", "expert"), None),
        P("expert", None, "seq"),
        P("expert", None, "seq"),
        P("expert", "seq", None),
    )
    out_specs = P(("seq", "expert"), None)
    return jax.shard_map(local, mesh=mesh, in_specs=in_specs, out_specs=out_specs, check_vma=False)
```

```python
import functools

import jax
import jax.numpy as jnp
from jax import lax
from jax.experimental import pallas as pl
from jax.experimental.pallas import tpu as pltpu
from jax.sharding import PartitionSpec as P

EPSILON = 1e-06
HALO = 16
ROUTE_ROWS = 2
LOG2_E = 1.4426950408889634
MIB = 1 << 20
BF16 = jnp.bfloat16
F32 = jnp.float32

VMEM = pl.BlockSpec(memory_space=pltpu.VMEM)
SMEM = pl.BlockSpec(memory_space=pltpu.SMEM)


def partner(block, axis, mask):
    size = lax.axis_size(axis)
    return lax.ppermute(block, axis, [(i, i ^ mask) for i in range(size)])


def later_partner(block, axis, mask):
    size = lax.axis_size(axis)
    return lax.ppermute(block, axis, [(i, i ^ mask) for i in range(size) if i < i ^ mask])


def after(values, *done):
    flat, tree = jax.tree.flatten(values)
    held = lax.optimization_barrier((*flat, *done))
    return jax.tree.unflatten(tree, held[: len(flat)])


def shape(dims, dtype):
    return jax.ShapeDtypeStruct(tuple(dims), dtype)


def kernel_call(body, outs, in_specs, scratch=(), flops=0, moved=0, limit=8, deps=()):
    deps = list(deps)
    count = len(in_specs)

    def with_deps(*refs):
        body(*refs[:count], *refs[count + len(deps) :])

    call = pl.pallas_call(
        with_deps,
        out_shape=outs,
        in_specs=list(in_specs) + [pl.BlockSpec(memory_space=pl.ANY)] * len(deps),
        out_specs=jax.tree.map(lambda _: VMEM, outs),
        scratch_shapes=list(scratch),
        compiler_params=pltpu.CompilerParams(vmem_limit_bytes=limit * MIB),
        cost_estimate=pl.CostEstimate(flops=flops, bytes_accessed=moved, transcendentals=0),
    )
    return lambda *operands: call(*operands, *deps)


def dot(left, right):
    return jnp.dot(left, right, preferred_element_type=F32)


def silu(v):
    return v / (1.0 + jnp.exp(-v))


def norm_body(seq, place, tokens, gain, own, *refs):
    sends, (held, factors, sems) = refs[: seq - 1], refs[seq - 1 :]
    length, own_width = own.shape
    half = own_width // 2
    me, core = place[0], place[1]
    parts = sems.shape[0] - 1
    size = length // parts
    copies = [pltpu.make_async_copy(gain, factors, sems.at[parts])]
    for i in range(parts):
        rows = pl.ds(i * size, size)
        copies.append(pltpu.make_async_copy(tokens.at[rows], held.at[rows], sems.at[i]))
    for copy in copies:
        copy.start()
    copies[0].wait()
    for i in range(parts):
        copies[1 + i].wait()
        rows = slice(i * size, (i + 1) * size)
        values = held[rows, :].astype(F32)
        inverse = lax.rsqrt(jnp.mean(values * values, axis=-1, keepdims=True) + EPSILON)

        def columns(start, width):
            part = pl.ds(pl.multiple_of(start, 128), width)
            return (held[rows, part].astype(F32) * inverse * factors[:, part]).astype(BF16)

        own[rows, :] = columns(me * own_width, own_width)
        for mask in range(1, seq):
            sends[mask - 1][rows, :] = columns((me ^ mask) * own_width + core * half, half)


def pass_body(*refs):
    for block, out in zip(refs[: len(refs) // 2], refs[len(refs) // 2 :]):
        out[...] = block[...]


def weight_body(source, out, sem):
    copy = pltpu.make_async_copy(source.at[:, pl.ds(0, out.shape[1])], out, sem)
    copy.start()
    copy.wait()


def project(core, own, mine, other, source, branch, weight, sems):
    depth, channels = weight.shape
    parts = sems.shape[0] if sems is not None else 0
    copies = []
    for i in range(parts):
        rows = pl.ds(i * (depth // parts), depth // parts)
        part = source.at[rows, pl.ds(branch * channels, channels)]
        copies.append((rows, pltpu.make_async_copy(part, weight.at[rows], sems.at[i])))
    for _, copy in copies:
        copy.start()
    first = 0.0
    for rows, copy in copies:
        copy.wait()
        first = first + dot(own[:, rows], weight[rows, :])
    yield first if copies else dot(own[...], weight[...])
    half = depth // 2
    near = weight[pl.ds(pl.multiple_of(core * half, half), half), :]
    far = weight[pl.ds(pl.multiple_of((1 - core) * half, half), half), :]
    for left, right in zip(mine, other):
        yield dot(left[...], near) + dot(right[...], far)


def mixer_project_body(seq, cuts, place, *refs):
    own, mine, other = refs[0], refs[1:seq], refs[seq : 2 * seq - 1]
    refs = refs[2 * seq - 1 :]
    (weight, routes), outs, tails = refs[:2], refs[2:-1], refs[-1]
    me = place[0]
    length = own.shape[0]

    def store(mask, rows, values):
        for (number, index), out in zip(cuts, outs):
            if number == mask:
                columns = out.shape[1]
                out[rows, :] = values[:, index * columns : (index + 1) * columns].astype(out.dtype)

    for mask, product in enumerate(project(place[1], own, mine, other, None, 0, weight, None)):
        store(mask, slice(HALO, HALO + length), product)
        tails[mask] = product[length - HALO :, :]
    for mask in range(seq):
        shard = me ^ mask
        source = me ^ jnp.maximum(shard - 1, 0)
        before = jnp.where(shard > 0, tails[source], 0.0)
        row = lax.broadcasted_iota(jnp.int32, before.shape, 0)
        store(mask, slice(0, HALO), jnp.where(row < ROUTE_ROWS, routes[mask], before))


def gate_project_body(seq, place, *refs):
    own, mine, other = refs[0], refs[1:seq], refs[seq : 2 * seq - 1]
    refs = refs[2 * seq - 1 :]
    (weight, own_tokens), outs, (held, sems) = refs[:2], refs[2 : seq + 2], refs[seq + 2 :]
    length, width = own.shape
    for index, product in enumerate(project(place[1], own, mine, other, weight, 1, held, sems)):
        outs[index][:length, :] = product.astype(outs[index].dtype)
        if index:
            start = pl.multiple_of((place[0] ^ index) * width, 128)
            rows = own_tokens[:, pl.ds(start, width)]
            spare = outs[index].shape[1] - width
            if spare:
                rows = jnp.concatenate([rows, jnp.zeros((rows.shape[0], spare), rows.dtype)], axis=1)
            outs[index][length:, :] = rows


def conv_body(places, *refs):
    own, terms = refs[0], refs[1 : 1 + len(places)]
    taps, bias, proj, activated, features = refs[1 + len(places) :]
    columns = [own[:, i * terms[0].shape[1] : (i + 1) * terms[0].shape[1]] for i in range(max(places) + 1)]
    for index, term in zip(places, terms):
        columns[index] = columns[index] + term[...].astype(F32)
    total = jnp.concatenate(columns, axis=1)
    padded = total.astype(BF16).astype(F32)
    length = activated.shape[0]
    count = taps.shape[0]
    convolved = bias[...]
    for tap in range(count):
        start = HALO - count + 1 + tap
        convolved = convolved + taps[tap : tap + 1, :] * padded[start : start + length]
    rounded = silu(convolved).astype(BF16)
    activated[...] = rounded
    rank = features.shape[1]
    states = (proj.shape[0] - rank) // 2

    def both_last(one, other):
        return lax.dot_general(one, other, (((1,), (1,)), ((), ())), preferred_element_type=F32)

    features[:length, :] = both_last(rounded, proj[:rank, :])
    maps = both_last(proj[rank:, :], rounded)
    below = jnp.zeros((features.shape[0] - length, rank), F32)
    features[length:, :] = below
    for i in range(2):
        features[length:, i * length : (i + 1) * length] = maps[i * states : (i + 1) * states]


def scan_body(maps, low_rank, activated, step_weight, step_bias, rate, y, cumulated, final, steps, drive):
    length, groups, lanes = y.shape
    states = rate.shape[0]
    raw = dot(low_rank[...], step_weight[...]) + step_bias[...]
    step_size = jnp.maximum(raw, 0.0) + jnp.log1p(jnp.exp(-jnp.abs(raw)))
    driven = step_size * activated[...].astype(F32)
    for group in range(groups):
        part = slice(group * lanes, (group + 1) * lanes)
        steps[:, group, :] = step_size[:, part]
        drive[:, group, :] = driven[:, part]
    rates = [rate[n] for n in range(states)]

    def advance(t, carry):
        state, running = carry
        step, push = steps[t], drive[t]
        running = running + step
        fresh = []
        out = jnp.zeros_like(step)
        for n in range(states):
            value = jnp.exp2(step * rates[n]) * state[n] + push * maps[n, t]
            out = out + value * maps[n, length + t]
            fresh.append(value)
        y[t] = out
        cumulated[t] = running
        return tuple(fresh), running

    zero = jnp.zeros((groups, lanes), F32)
    state, running = lax.fori_loop(0, length, advance, ((zero,) * states, zero), unroll=8)
    for n in range(states):
        final[n] = state[n].astype(BF16)
    upper = running.astype(BF16)
    final[states] = upper
    final[states + 1] = (running - upper.astype(F32)).astype(BF16)


def gated_body(seq, own_rows, place, maps, *refs):
    arrived = refs[: seq - 1]
    y, cumulated, rate, activated, skip_gain = refs[seq - 1 : seq + 4]
    gates = refs[seq + 4 : 2 * seq + 4]
    gated, scanned, result = refs[2 * seq + 4 :]
    length, groups, lanes = y.shape
    states = rate.shape[0]
    me, expert = place[0], place[2]
    zero = jnp.zeros((groups, lanes), F32)
    incoming = [zero] * states
    sums = [block[states].astype(F32) + block[states + 1].astype(F32) for block in arrived]
    for mask in range(1, seq):
        shard = me ^ mask
        between = zero
        for other in range(1, seq):
            middle = me ^ other
            inside = (shard < middle) & (middle < me)
            between = between + jnp.where(inside, sums[other - 1], 0.0)
        for n in range(states):
            term = jnp.exp2(rate[n] * between) * arrived[mask - 1][n].astype(F32)
            incoming[n] = incoming[n] + jnp.where(shard < me, term, 0.0)
    rates = [rate[n] for n in range(states)]

    def correct(t, carry):
        steps = cumulated[t]
        out = y[t]
        for n in range(states):
            out = out + (jnp.exp2(steps * rates[n]) * incoming[n]) * maps[n, length + t]
        scanned[t] = out
        return carry

    lax.fori_loop(0, length, correct, 0, unroll=8)
    for group in range(groups):
        part = slice(group * lanes, (group + 1) * lanes)
        gate = gates[0][:, part]
        for term in gates[1:]:
            gate = gate + term[:length, part].astype(F32)
        gate = gate.astype(BF16).astype(F32)
        drive = activated[:, part].astype(F32)
        result[:, part] = (scanned[:, group, :] + skip_gain[:, part] * drive) * silu(gate)
    blocks = length // own_rows
    moved = [
        result[pl.ds(pl.multiple_of((expert ^ k) * own_rows, own_rows), own_rows), :]
        for k in range(blocks)
    ]
    gated[...] = jnp.concatenate(moved, axis=0).astype(BF16)


def out_project_body(seq, own_rows, *refs):
    blocks = refs[:seq]
    weight, keep, send = refs[seq:]
    for shard in range(seq):
        product = dot(blocks[shard][...], weight[...])
        for owner in range(product.shape[0] // own_rows):
            rows = product[owner * own_rows : (owner + 1) * own_rows]
            place = (owner // 2, pl.ds(shard * own_rows, own_rows))
            if owner % 2 == 0:
                keep[place[0], place[1], :] = rows
            else:
                send[place[0], place[1], :] = rows.astype(BF16)


def core_sum_body(keep, arrived, own, *sends):
    own[...] = keep[0] + arrived[0].astype(F32)
    for w in range(1, keep.shape[0]):
        sends[w - 1][...] = (keep[w] + arrived[w].astype(F32)).astype(BF16)


def tables_body(seq, own_rows, most_slots, place, routes, *refs):
    terms, (choose, first, second, named) = refs[:-4], refs[-4:]
    slots, window = choose.shape
    near = routes[:8, :window]
    for term in terms:
        near = near + term[:16, :window].astype(F32)[:8]
    row = lax.broadcasted_iota(jnp.int32, (slots, window), 0)
    column = lax.broadcasted_iota(jnp.int32, (slots, window), 1)
    wanted = (place[2] ^ (row // (seq * most_slots))).astype(F32)
    shard = (row // most_slots) % seq
    hits = [jnp.where(near[i : i + 1, :] == wanted, 1.0, 0.0) for i in range(2)]
    source = lax.broadcasted_iota(jnp.int32, (window, window), 0)
    target = lax.broadcasted_iota(jnp.int32, (window, window), 1)
    earlier = (source // own_rows == target // own_rows) & (source < target)
    before = dot((hits[0] + hits[1]).astype(BF16), jnp.where(earlier, 1.0, 0.0).astype(BF16))
    numbered = jnp.where(before == (row % most_slots).astype(F32), 1.0, 0.0)
    here = jnp.where(shard == (place[0] ^ (column // own_rows)), numbered, 0.0)
    choose[...] = (here * (hits[0] + hits[1])).astype(BF16)
    first[...] = (numbered * hits[0])[:, :own_rows]
    second[...] = (numbered * hits[1])[:, :own_rows]
    same = jnp.where(source == target, 1.0, 0.0).astype(BF16)
    columns = lax.dot_general(
        same, near.astype(BF16), (((1,), (1,)), ((), ())), preferred_element_type=F32
    )
    named[...] = columns[:own_rows]


def reordered(table, outer, inner, count):
    rows = table.shape[0]
    row = lax.broadcasted_iota(jnp.int32, (rows, rows), 0)
    column = lax.broadcasted_iota(jnp.int32, (rows, rows), 1)
    big, small, number = row // (inner * count), (row // count) % inner, row % count
    choice = jnp.where(column == small * (outer * count) + big * count + number, 1.0, 0.0).astype(BF16)
    return dot(choice, table).astype(BF16)


def hidden_body(chips, seq, place, own, *refs):
    terms, refs = refs[: chips - 1], refs[chips - 1 :]
    own_tokens, refs = refs[0], refs[1:]
    payloads, refs = refs[: seq - 1], refs[seq - 1 :]
    choose, hidden = refs[0], refs[1 : 1 + seq]
    outs = refs[1 + seq :]
    total = own[...]
    for term in terms:
        total = total + term[...].astype(F32)
    width = own.shape[1]
    rows = own_tokens.shape[0]
    start = pl.multiple_of(place[0] * width, 128)
    residual = [own_tokens[:, pl.ds(start, width)].astype(F32)]
    for payload in payloads:
        residual.append(payload[payload.shape[0] - rows :, :width].astype(F32))
    rounded = (jnp.concatenate(residual, axis=0) + total).astype(BF16)
    for d, out in enumerate(hidden):
        out[...] = rounded[d * rows : (d + 1) * rows]
    slots = dot(choose[...], rounded).astype(BF16)
    rows = slots.shape[0] // chips
    for w in range(chips):
        outs[w][...] = slots[w * rows : (w + 1) * rows]


def start_copies(jobs, place, sources, outs, sems):
    copies = []
    for index, (source, mask, axis) in enumerate(jobs):
        size = outs[index].shape[axis]
        if axis:
            where = (0, slice(None), pl.ds(mask * size, size))
        else:
            where = (0, pl.ds(pl.multiple_of((place[0] ^ mask) * size, 16), size))
        copies.append(pltpu.make_async_copy(sources[source].at[where], outs[index], sems.at[index]))
    for copy in copies:
        copy.start()
    return copies


def in_hbm(sources):
    return [pltpu.with_memory_space_constraint(source, pltpu.HBM) for source in sources]


def fetched_shapes(jobs, sources, width):
    blocks = []
    for source, _, axis in jobs:
        rows, columns = sources[source].shape[1:]
        blocks.append(pltpu.VMEM((rows, width) if axis else (width, columns), BF16))
    return blocks


def fetch_body(jobs, count, place, *refs):
    sources, outs, sems = refs[:count], refs[count:-1], refs[-1]
    for copy in start_copies(jobs, place, sources, outs, sems):
        copy.wait()


def fetch(place, jobs, width, sources, deps):
    return kernel_call(
        functools.partial(fetch_body, jobs, len(sources)),
        fetched_shapes(jobs, sources, width),
        [SMEM] + [pl.BlockSpec(memory_space=pltpu.HBM)] * len(sources),
        [pltpu.SemaphoreType.DMA((len(jobs),))],
        moved=2 * len(jobs) * width * sources[0].shape[2],
        deps=deps,
    )(place, *in_hbm(sources))


def expert_body(mask, first, last, model_width, jobs, count, parts, place, *refs):
    pieces, (gain, gate, up), refs = refs[:parts], refs[parts : parts + 3], refs[parts + 3 :]
    before, refs = ([], refs) if first else (refs[:3], refs[3:])
    sources, refs = refs[:count], refs[count:]
    outs, refs = (refs[:1], refs[1:]) if last else (refs[:3], refs[3:])
    copies = start_copies(jobs, place, sources, refs[:-1], refs[-1]) if jobs else []
    width = pieces[0].shape[1]
    values = jnp.concatenate([piece[...].astype(F32) for piece in pieces], axis=0)
    square = jnp.sum(values * values, axis=-1, keepdims=True)
    if not first:
        square = square + before[2][:, 0:1]
    start = pl.multiple_of((place[0] ^ mask) * width, 128)
    rows = (values * gain[:, pl.ds(start, width)]).astype(BF16)
    inverse = lax.rsqrt(square / model_width + EPSILON)
    if not last:
        outs[2][...] = jnp.broadcast_to(square, outs[2].shape)
    hidden_units = gate.shape[1]
    tile = tile_of(hidden_units, 512)
    for step in range(hidden_units // tile):
        part = slice(step * tile, (step + 1) * tile)
        gate_act = dot(rows, gate[:, part])
        up_act = dot(rows, up[:, part])
        if not first:
            gate_act = gate_act + before[0][:, part]
            up_act = up_act + before[1][:, part]
        if last:
            outs[0][:, part] = (silu(gate_act * inverse) * (up_act * inverse)).astype(BF16)
        else:
            outs[0][:, part] = gate_act
            outs[1][:, part] = up_act
    for copy in copies:
        copy.wait()


def expert_chunk(mask, first, last, place, piece, gain, gate, up, before, jobs, sources, deps):
    slots, width = sum(part.shape[0] for part in piece), piece[0].shape[1]
    model_width, hidden_units = gain.shape[1], gate.shape[1]
    total = shape((slots, hidden_units), F32)
    outs = [total, total, shape((slots, 128), F32)]
    if last:
        outs = [shape((slots, hidden_units), BF16)]
    sources = sources if jobs else []
    far = pl.BlockSpec(memory_space=pltpu.HBM)
    results = kernel_call(
        functools.partial(expert_body, mask, first, last, model_width, jobs, len(sources), len(piece)),
        outs + fetched_shapes(jobs, sources, width),
        [SMEM] + [VMEM] * (3 + len(piece) + len(before)) + [far] * len(sources),
        [pltpu.SemaphoreType.DMA((len(jobs),))] if jobs else [],
        flops=4 * slots * width * hidden_units,
        moved=4 * width * hidden_units,
        limit=12,
        deps=deps,
    )(place, *piece, gain, gate, up, *before, *in_hbm(sources))
    return results[: len(outs)], results[len(outs) :]


def down_body(seq, cuts, place, hidden, *refs):
    downs, outs, product = refs[:seq], refs[seq:-1], refs[-1]
    width = downs[0].shape[1]
    tile = tile_of(width, 512)
    for block, down in enumerate(downs):
        for step in range(width // tile):
            part = slice(step * tile, (step + 1) * tile)
            to = slice(block * width + step * tile, block * width + (step + 1) * tile)
            product[:, to] = dot(hidden[...], down[:, part]).astype(BF16)
    for (mask, index), out in zip(cuts, outs):
        rows, columns = out.shape
        start = pl.multiple_of((place[0] ^ mask) * rows, 16)
        out[...] = product[pl.ds(start, rows), index * columns : (index + 1) * columns]


def pair_sum_body(*refs):
    count = len(refs) // 3
    for one, other, out in zip(refs[:count], refs[count : 2 * count], refs[2 * count :]):
        out[...] = (one[...].astype(F32) + other[...].astype(F32)).astype(BF16)


def expert_sum_body(seq, groups, most_slots, places, *refs):
    own, terms, outs = refs[0], refs[1 : 1 + len(places)], refs[1 + len(places) :]
    width = outs[0].shape[1]
    pieces = []
    for q in range(seq):
        total = own[:, q * width : (q + 1) * width].astype(F32)
        for index, term in zip(places, terms):
            start = q * width - index * term.shape[1]
            if 0 <= start < term.shape[1]:
                total = total + term[:, start : start + width].astype(F32)
        pieces.append(total.astype(BF16))
    pieces = reordered(jnp.concatenate(pieces, axis=0), groups, seq, most_slots)
    rows = pieces.shape[0] // len(outs)
    for w, out in enumerate(outs):
        out[...] = pieces[w * rows : (w + 1) * rows]


def shares_body(seq, place, gain, router, named, *refs):
    pieces, rows, shares = refs[:seq], refs[seq], refs[seq + 1]
    width = pieces[0].shape[1]
    for mask, piece in enumerate(pieces):
        start = pl.multiple_of((place[0] ^ mask) * width, 128)
        rows[:, pl.ds(start, width)] = piece[...].astype(F32)
    values = rows[...]
    inverse = lax.rsqrt(jnp.mean(values * values, axis=-1, keepdims=True) + EPSILON)
    moe_in = (values * inverse * gain[...]).astype(BF16)
    logits = lax.dot_general(
        moe_in, router[...], (((1,), (1,)), ((), ())), preferred_element_type=F32
    )
    lane = lax.broadcasted_iota(jnp.int32, logits.shape, 1).astype(F32)
    picked = [
        jnp.sum(jnp.where(lane == named[:, i : i + 1], logits, 0.0), axis=-1, keepdims=True)
        for i in range(2)
    ]
    first_share = 1.0 / (1.0 + jnp.exp(picked[1] - picked[0]))
    shares[...] = jnp.broadcast_to(first_share, shares.shape)


def halves_body(*refs):
    blocks, out = refs[:-1], refs[-1]
    for w, block in enumerate(blocks):
        out[w] = block[out.shape[1] :, :]


def second_halves(blocks, deps=()):
    rows, width = blocks[0].shape
    return kernel_call(
        halves_body,
        shape((len(blocks), rows // 2, width), BF16),
        [VMEM] * len(blocks),
        moved=2 * len(blocks) * rows * width,
        deps=deps,
    )(*blocks)


def rows_body(chips, seq, groups, most_slots, *refs):
    direct, crossed, out = refs[:chips], refs[chips], refs[chips + 1]
    half = crossed.shape[1]
    table = jnp.concatenate(
        [block for w in range(chips) for block in (direct[w][:half, :], crossed[w])], axis=0
    )
    out[...] = reordered(table, seq, groups, most_slots)


def combine_body(chips, seq, most_slots, *refs):
    direct = refs[:chips]
    crossed, first, second, rows, shares, out = refs[chips:]
    half = crossed.shape[1]
    table = jnp.concatenate(
        [block for w in range(chips) for block in (direct[w][:half, :], crossed[w])], axis=0
    )
    width = table.shape[1]
    row = lax.broadcasted_iota(jnp.int32, first.shape, 0)
    piece = (row // most_slots) % seq
    first_share = shares[:, 0:1]
    for q in range(seq):

        def rows_of(choice):
            chosen = jnp.where(piece == q, choice[...], 0.0).astype(BF16)
            return lax.dot_general(
                chosen, table, (((0,), (0,)), ((), ())), preferred_element_type=F32
            )

        part = slice(q * width, (q + 1) * width)
        sent = first_share * rows_of(first) + (1.0 - first_share) * rows_of(second)
        out[:, part] = (rows[:, part] + sent).astype(BF16)


halved = [(0, 0), (1, 0), (1, 1), (2, 0), (2, 1), (3, 0), (3, 1)]


def scattered(sends, masks, deps=()):
    if len(masks) != 3:
        terms = [partner(block, "seq", mask) for mask, block in zip(masks, sends)]
        return terms, [0] * len(terms)
    left, right, lower, upper, far_left, far_right = sends
    over = [partner(far_left, "seq", 1), partner(far_right, "seq", 2)]
    terms = [partner(left, "seq", 1), partner(upper, "seq", 2)]
    rows, columns = left.shape
    lower, right = kernel_call(
        pair_sum_body,
        [shape(left.shape, BF16)] * 2,
        [VMEM] * 4,
        flops=4 * rows * columns,
        moved=12 * rows * columns,
        deps=deps,
    )(lower, right, *over)
    return terms + [partner(right, "seq", 1), partner(lower, "seq", 2)], [0, 1, 1, 0]


def tile_of(total, most):
    for width in range(most, 0, -128):
        if total % width == 0:
            return width
    return total


def local(
    tokens,
    norm_gain,
    in_weight,
    conv_weight,
    conv_bias,
    proj_weight,
    step_weight,
    step_bias,
    decay_log,
    skip_gain,
    out_weight,
    moe_gain,
    router_weight,
    routes,
    gate_weight,
    up_weight,
    down_weight,
):
    seq, groups = lax.axis_size("seq"), lax.axis_size("expert")
    chips = groups // 2
    me, expert = lax.axis_index("seq"), lax.axis_index("expert")
    core = expert % 2
    place = jnp.stack([me, core, expert]).astype(jnp.int32)
    masks = range(1, seq)
    length, model_width = tokens.shape
    width = model_width // seq
    channels = in_weight.shape[2]
    rank_width = step_weight.shape[0]
    state_width = decay_log.shape[1]
    lanes = 128
    tiles = channels // lanes
    own_rows = routes.shape[0]
    experts = router_weight.shape[1]
    most_slots = max(2, 3 * own_rows // experts)
    window = seq * own_rows

    x_own, *x_send = kernel_call(
        functools.partial(norm_body, seq),
        [shape((length, width), BF16)] + [shape((length, width // 2), BF16)] * (seq - 1),
        [SMEM] + [pl.BlockSpec(memory_space=pltpu.HBM)] * 2,
        [
            pltpu.VMEM(tokens.shape, BF16),
            pltpu.VMEM((1, model_width), F32),
            pltpu.SemaphoreType.DMA((5,)),
        ],
        flops=8 * length * model_width,
        moved=4 * length * model_width,
        limit=24,
    )(place, *in_hbm([tokens, norm_gain[None]]))
    x_mine = [partner(block, "seq", mask) for mask, block in zip(masks, x_send)]
    weight = in_hbm([in_weight.reshape(width, 2 * channels)])[0]
    x_passed = kernel_call(
        pass_body,
        [shape((length, width // 2), BF16)] * (seq - 1),
        [VMEM] * (seq - 1),
        deps=[weight],
    )(*x_mine)
    x_other = [partner(block, "expert", 1) for block in x_passed]
    x = [x_own, *x_mine, *x_other]
    mixer_weight = kernel_call(
        weight_body,
        pltpu.VMEM((width, channels), BF16),
        [pl.BlockSpec(memory_space=pltpu.HBM)],
        [pltpu.SemaphoreType.DMA],
        moved=4 * width * channels,
        deps=x_passed[:1],
    )(weight)
    lane_routes = jnp.transpose(routes).astype(F32)
    spread_routes = jnp.stack(
        [
            jnp.pad(lane_routes, ((0, HALO - ROUTE_ROWS), (d * own_rows, channels - (d + 1) * own_rows)))
            for d in range(seq)
        ]
    )
    in_specs = [SMEM] + [VMEM] * (2 * seq - 1) + [pl.BlockSpec(memory_space=pltpu.HBM), VMEM]
    scratch = [pltpu.VMEM((width, channels), BF16), pltpu.SemaphoreType.DMA((4,))]
    cost = dict(flops=2 * seq * length * width * channels, moved=2 * width * channels, limit=24)
    cuts = halved if seq == 4 else [(mask, 0) for mask in range(seq)]
    mixer_own, *mixer_send = kernel_call(
        functools.partial(mixer_project_body, seq, cuts),
        [shape((HALO + length, channels), F32)]
        + [shape((HALO + length, channels // (2 if seq == 4 else 1)), BF16)] * (len(cuts) - 1),
        [SMEM] + [VMEM] * (2 * seq + 1),
        [pltpu.VMEM((seq, HALO, channels), F32)],
        **cost,
    )(place, *x, mixer_weight, spread_routes)
    assert width <= channels and window <= channels and 2 * length <= rank_width
    own_tokens = lax.dynamic_slice_in_dim(tokens, expert * own_rows, own_rows, 0)
    side_own, *side_send = kernel_call(
        functools.partial(gate_project_body, seq),
        [shape((length, channels), F32)] + [shape((length + own_rows, channels), BF16)] * (seq - 1),
        in_specs,
        scratch,
        **cost,
    )(place, *x, weight, own_tokens)

    mixer_terms, places = scattered(mixer_send, masks, [side_own])

    activated, features = kernel_call(
        functools.partial(conv_body, places),
        [shape((length, channels), BF16), shape((length + state_width, rank_width), F32)],
        [VMEM] * (len(mixer_terms) + 4),
        limit=16,
    )(mixer_own, *mixer_terms, conv_weight, conv_bias[None], jnp.transpose(proj_weight))
    features = features + partner(features, "expert", 1)
    sent = features.astype(BF16)
    features_came = [partner(sent, "expert", 2 * w) for w in range(1, chips)]
    side_send = after(side_send, features_came[0])
    side_terms = [partner(block, "seq", mask) for mask, block in zip(masks, side_send)]
    for term in features_came:
        features = features + term.astype(F32)
    low_rank, maps = features[:length].astype(BF16), features[length:]

    rate = -LOG2_E * jnp.exp(jnp.transpose(decay_log)).reshape(state_width, tiles, lanes)
    tiled = shape((length, tiles, lanes), F32)
    y, cumulated, final = kernel_call(
        scan_body,
        [tiled, tiled, shape((state_width + 2, tiles, lanes), BF16)],
        [SMEM] + [VMEM] * 5,
        [pltpu.VMEM(tiled.shape, F32)] * 2,
        limit=24,
    )(maps, low_rank, activated, step_weight, step_bias[None], rate)
    arrived = [partner(final, "seq", mask) for mask in masks]
    gated = kernel_call(
        functools.partial(gated_body, seq, own_rows),
        shape((length, channels), BF16),
        [SMEM, SMEM] + [VMEM] * (2 * seq + 4),
        [pltpu.VMEM(tiled.shape, F32), pltpu.VMEM((length, channels), F32)],
        limit=24,
    )(place, maps, *arrived, y, cumulated, rate, activated, skip_gain[None], side_own, *side_terms)

    blocks = [gated] + [partner(gated, "seq", mask) for mask in masks]

    slots = groups * seq * most_slots
    per_chip = slots // chips
    per_group = slots // groups
    route_terms = [term for term, index in zip(mixer_terms, places) if index == 0]
    choose, first, second, named = kernel_call(
        functools.partial(tables_body, seq, own_rows, most_slots),
        [shape((slots, window), BF16)] + [shape((slots, own_rows), F32)] * 2 + [shape((own_rows, 8), F32)],
        [SMEM, VMEM] + [VMEM] * len(route_terms),
        flops=2 * slots * window * window,
        moved=8 * slots * window,
    )(place, spread_routes[0], *route_terms)

    keep, send = kernel_call(
        functools.partial(out_project_body, seq, own_rows),
        [shape((chips, window, width), F32), shape((chips, window, width), BF16)],
        [VMEM] * (seq + 1),
        flops=2 * seq * length * channels * width,
        moved=2 * channels * width + 8 * seq * length * width,
        limit=16,
    )(*blocks, out_weight)
    crossing = partner(send, "expert", 1)
    own_sum, *chip_sends = kernel_call(
        core_sum_body,
        [shape((window, width), F32)] + [shape((window, width), BF16)] * (chips - 1),
        [VMEM] * 2,
        flops=chips * window * width,
        moved=10 * chips * window * width,
    )(keep, crossing)
    chip_terms = [partner(block, "expert", 2 * w) for w, block in zip(range(1, chips), chip_sends)]

    sources = [gate_weight, up_weight, down_weight]
    both = lambda mask: [(0, mask, 0), (1, mask, 0)]
    early = min(seq, 3)
    current = list(fetch(place, sum([both(mask) for mask in range(early)], []), width, sources[:2], [own_sum]))
    near_hidden = kernel_call(
        functools.partial(hidden_body, chips, seq),
        [shape((own_rows, width), BF16)] * seq + [shape((per_chip, width), BF16)] * chips,
        [SMEM] + [VMEM] * (chips + seq + 1),
        flops=2 * slots * window * width,
        moved=10 * window * width,
        deps=current,
    )(place, own_sum, *chip_terms, own_tokens, *side_terms, choose)
    near_hidden, outgoing = near_hidden[:seq], near_hidden[seq:]

    came = [outgoing[0]] + [
        partner(block, "expert", 2 * w) for w, block in zip(range(1, chips), outgoing[1:])
    ]
    whole = [near_hidden[0]] + [partner(near_hidden[mask], "seq", mask) for mask in masks]
    crossed = partner(second_halves(came, whole[1:] + current), "expert", 1)
    rows = kernel_call(
        functools.partial(rows_body, chips, seq, groups, most_slots),
        shape((slots, width), BF16),
        [VMEM] * (chips + 1),
        moved=4 * slots * width,
        deps=current,
    )(*came, crossed)
    if seq == 4:
        pieces = [rows, partner(rows, "seq", 1), partner(rows, "seq", 2)]
        half = slots // 2
        pieces = [[piece] for piece in pieces] + [
            [partner(pieces[1][:half], "seq", 2), partner(pieces[2][half:], "seq", 1)]
        ]
    else:
        pieces = [[rows]] + [[partner(rows, "seq", mask)] for mask in masks]

    before, waiting, downs = [], current, []
    for mask in range(seq):
        jobs = both(mask + early) if mask + early < seq else []
        gates = len(jobs)
        if mask == max(0, seq - 4):
            jobs = jobs + [(2, block, 1) for block in range(seq)]
        before, came_in = expert_chunk(
            mask, mask == 0, mask == seq - 1, place, pieces[mask], moe_gain[None], *waiting[:2], before, jobs, sources, downs
        )
        waiting = waiting[2:] + list(came_in[:gates])
        downs = downs + list(came_in[gates:])
    hidden = before[0]
    back = groups * most_slots
    sums = kernel_call(
        functools.partial(down_body, seq, cuts),
        [shape((back, model_width // (2 if seq == 4 and mask else 1)), BF16) for mask, _ in cuts],
        [SMEM] + [VMEM] * (seq + 1),
        [pltpu.VMEM((slots, model_width), BF16)],
        flops=2 * slots * model_width * gate_weight.shape[2],
        moved=2 * model_width * gate_weight.shape[2],
        limit=16,
    )(place, hidden, *downs)
    terms, places = scattered(sums[1:], masks)

    own_hidden, shares = kernel_call(
        functools.partial(shares_body, seq),
        [shape((own_rows, model_width), F32), shape((own_rows, lanes), F32)],
        [SMEM] + [VMEM] * (seq + 3),
        flops=2 * own_rows * model_width * lanes,
        moved=16 * own_rows * model_width,
        deps=[sums[0]],
    )(place, moe_gain[None], jnp.transpose(router_weight), named, *whole)
    answers = kernel_call(
        functools.partial(expert_sum_body, seq, groups, most_slots, places),
        [shape((per_chip, width), BF16)] * chips,
        [VMEM] * (1 + len(terms)),
        flops=seq * slots * width,
        moved=10 * slots * width,
        deps=[shares],
    )(sums[0], *terms)
    answers = [answers[0]] + [
        partner(block, "expert", 2 * w) for w, block in zip(range(1, chips), answers[1:])
    ]
    crossed_back = partner(second_halves(answers), "expert", 1)
    return kernel_call(
        functools.partial(combine_body, chips, seq, most_slots),
        shape((own_rows, model_width), BF16),
        [VMEM] * (chips + 5),
        flops=4 * slots * own_rows * model_width,
        moved=8 * slots * width,
    )(*answers, crossed_back, first, second, own_hidden, shares)


def solution(mesh):
    in_specs = (
        P("seq", None),
        P(),
        P("seq", None, "expert"),
        P(None, "expert"),
        P("expert"),
        P("expert", None),
        P(None, "expert"),
        P("expert"),
        P("expert", None),
        P("expert"),
        P("expert", "seq"),
        P(),
        P(),
        P(("seq", "expert"), None),
        P("expert", None, "seq"),
        P("expert", None, "seq"),
        P("expert", "seq", None),
    )
    out_specs = P(("seq", "expert"), None)
    return jax.shard_map(local, mesh=mesh, in_specs=in_specs, out_specs=out_specs, check_vma=False)
```
